32 devices in a mesh: dp: 8 (over z, y), head: 4 (over x, core).
Axes of the slice: x: 2, y: 2, z: 4, core: 2. Of those that a mesh axis runs over, the one named last changes fastest.
Arguments:
- tokens: bfloat16 [32, 1024, 768], P('dp', 'head'), may hold values from -6 to 6
- qkv_weight: float32 [768, 2304], P('dp'), may hold values from -0.21875 to 0.21875
- proj_weight: float32 [768, 768], P('dp'), may hold values from -1.75 to 1.75
- up_weight: float32 [768, 3072], P('dp'), may hold values from -0.21875 to 0.21875
- down_weight: float32 [3072, 768], P('dp'), may hold values from -0.109375 to 0.109375
- attn_gain: float32 [768], P('dp'), may hold values from 0.1 to 1.9
- attn_bias: float32 [768], P('dp'), may hold values from -3 to 3
- ffn_gain: float32 [768], P('dp'), may hold values from 0.1 to 1.9
- ffn_bias: float32 [768], P('dp'), may hold values from -3 to 3
- cotangent: bfloat16 [32, 1024, 768], P('dp', 'head'), may hold values from -6 to 6
Outputs:
- output: bfloat16 [32, 1024, 768], P('dp', 'head')
- grad_tokens: float32 [32, 1024, 768], P('dp', 'head')
- grad_qkv: float32 [768, 2304], P('dp')
- grad_proj: float32 [768, 768], P('dp')
- grad_up: float32 [768, 3072], P('dp')
- grad_down: float32 [3072, 768], P('dp')
- grad_attn_gain: float32 [768], P('dp')
- grad_attn_bias: float32 [768], P('dp')
- grad_ffn_gain: float32 [768], P('dp')
- grad_ffn_bias: float32 [768], P('dp')
The draws below stay inside these ranges and needn't reach their ends.
All inputs are finite; a program needn't handle non-finite values.
Results may differ from the reference program's by a relative error of at most 0.013.
Values may be sent and summed in bfloat16 or wider, within the bound.
No kernel may reach another device: no remote copies, remote signals or barrier semaphores. Data moves between devices by JAX's collectives and lax.ppermute only.
A program may use at most 192 MiB of HBM per device.

```python
import jax
import jax.numpy as jnp
from jax import lax

D = 768
HEADS = 12
HEAD_DIM = 64
FF = 3072
SEQ = 1024
TOKENS = 32768
SEQS = 32


def block_levels(stream_key, dims, cuts, smallest, high):
    def one(axis_at, parts):
        steps = jax.random.uniform(jax.random.fold_in(jax.random.fold_in(stream_key, 6), axis_at), (parts,), jnp.float32, smallest / len(cuts), high / len(cuts))
        return jnp.repeat(jnp.exp(steps), dims[axis_at] // parts).reshape((-1,) + (1,) * (len(dims) - axis_at - 1))

    loudness = one(*cuts[0])
    for cut in cuts[1:]:
        loudness = loudness * one(*cut)
    return loudness


def bell_draw(stream_key, shape, spread, bound, shards=(), held_as=jnp.bfloat16):
    entries = spread * jax.random.normal(stream_key, shape, jnp.float32)
    if shards:
        entries = entries * block_levels(stream_key, shape, shards, -0.22, 0.18)
    return jnp.clip(entries, -bound, bound).astype(held_as)


def setup_inputs(seed: int = 0) -> dict:
    key_list = jax.random.split(jax.random.key(seed), 11)
    return {
        "tokens": bell_draw(key_list[0], (SEQS, SEQ, D), 1.0, 6.0, ((0, 8), (1, 4))),
        "qkv_weight": bell_draw(key_list[1], (D, 3 * D), D ** -0.5, 0.21875, ((0, 8),), jnp.float32),
        "proj_weight": bell_draw(key_list[2], (D, D), (D // 64) ** -0.5, 1.75, ((0, 8),), jnp.float32),
        "up_weight": bell_draw(key_list[3], (D, FF), D ** -0.5, 0.21875, ((0, 8),), jnp.float32),
        "down_weight": bell_draw(key_list[4], (FF, D), FF ** -0.5, 0.109375, ((0, 8),), jnp.float32),
        "attn_gain": jnp.clip(1.0 + 0.18 * jax.random.normal(key_list[5], (D,), jnp.float32), 0.1, 1.9),
        "attn_bias": bell_draw(key_list[6], (D,), 0.5, 3.0, ((0, 8),), jnp.float32),
        "ffn_gain": jnp.clip(1.0 + 0.18 * jax.random.normal(key_list[7], (D,), jnp.float32), 0.1, 1.9),
        "ffn_bias": bell_draw(key_list[8], (D,), 0.5, 3.0, ((0, 8),), jnp.float32),
        "cotangent": bell_draw(key_list[9], (SEQS, SEQ, D), 1.0, 6.0, ((0, 8), (1, 4))),
    }


@jax.custom_vjp
def low(v):
    return lax.optimization_barrier(v.astype(jnp.bfloat16)).astype(jnp.float32)

@jax.custom_vjp
def low_back(v):
    return v

def low_keep(v):
    return (low(v), None)

def low_pass(kept, grad):
    return (grad,)

def back_keep(v):
    return (v, None)

def back_low(kept, grad):
    return (low(grad),)
low.defvjp(low_keep, low_pass)
low_back.defvjp(back_keep, back_low)
EPSILON = 1e-05
HIGHEST = lax.Precision.HIGHEST

def layer_norm(vector, gain_vec, bias_vec):
    row_mean = lax.optimization_barrier(jnp.mean(vector, axis=-1, keepdims=True))
    centred = vector - row_mean
    variance = lax.optimization_barrier(jnp.mean(centred * centred, axis=-1, keepdims=True))
    return centred * lax.rsqrt(variance + EPSILON) * gain_vec + bias_vec

def attention(queries, key_rows, value_rows):
    block_rows = min(512, SEQ)
    scaling = HEAD_DIM ** (-0.5)
    key_pos = jnp.arange(SEQ, dtype=jnp.int32)

    def one_block(block_id):
        first_row = (block_id * block_rows).astype(jnp.int32)
        query_block = lax.dynamic_slice_in_dim(queries, first_row, block_rows, 1)
        raw_scores = jnp.einsum('bqhd,bkhd->bhqk', query_block, key_rows, precision=HIGHEST) * scaling
        scores = low_back(raw_scores)
        query_pos = first_row + jnp.arange(block_rows, dtype=jnp.int32)
        allowed = query_pos[:, None] >= key_pos[None, :]
        scores = jnp.where(allowed, scores, -1e+30)
        row_max = lax.optimization_barrier(jnp.max(scores, axis=-1, keepdims=True))
        weights = jnp.exp(scores - row_max)
        probs = weights / lax.optimization_barrier(jnp.sum(weights, axis=-1, keepdims=True))
        return jnp.einsum('bhqk,bkhd->bqhd', low(probs), value_rows, precision=HIGHEST)
    blocks = lax.map(jax.checkpoint(one_block), jnp.arange(SEQ // block_rows, dtype=jnp.int32))
    return jnp.moveaxis(blocks, 0, 1).reshape(queries.shape)

def block_forward(slab_in, qkv_weight, proj_weight, up_weight, down_weight, attn_gain, attn_bias, ffn_gain, ffn_bias):
    row_total = slab_in.shape[0]
    normed = low(layer_norm(slab_in, low(attn_gain), low(attn_bias)))
    mixed = jnp.dot(normed, low(qkv_weight), precision=HIGHEST)
    mixed = low(low_back(mixed)).reshape(row_total // SEQ, SEQ, 3, HEADS, HEAD_DIM)
    attended = attention(mixed[:, :, 0], mixed[:, :, 1], mixed[:, :, 2])
    attended = low(low_back(attended.reshape(row_total, D)))
    middle = slab_in + low_back(jnp.dot(attended, low(proj_weight), precision=HIGHEST))
    normed_two = low(layer_norm(middle, low(ffn_gain), low(ffn_bias)))
    hidden = low_back(jnp.dot(normed_two, low(up_weight), precision=HIGHEST))
    active = low(jax.nn.gelu(hidden, approximate=True))
    return middle + low_back(jnp.dot(active, low(down_weight), precision=HIGHEST))

def reference(tokens, qkv_weight, proj_weight, up_weight, down_weight, attn_gain, attn_bias, ffn_gain, ffn_bias, cotangent):
    params = (qkv_weight, proj_weight, up_weight, down_weight, attn_gain, attn_bias, ffn_gain, ffn_bias)
    seq_total = TOKENS // SEQ
    per_step = max((number for number in range(1, seq_total + 1) if seq_total % number == 0 and number * SEQ <= 4096))
    step_rows = per_step * SEQ
    inputs = tokens.astype(jnp.float32).reshape(seq_total // per_step, step_rows, D)
    upstream = cotangent.astype(jnp.float32).reshape(seq_total // per_step, step_rows, D)

    def advance(totals, slabs):
        slab_in, slab_grad = slabs
        result, pullback = jax.vjp(block_forward, slab_in, *params)
        gradients = pullback(slab_grad)
        totals = tuple((running + addend for running, addend in zip(totals, gradients[1:])))
        return (totals, (result.astype(jnp.bfloat16), gradients[0]))
    starting = tuple((jnp.zeros(member.shape, jnp.float32) for member in params))
    totals, (output, grad_tokens) = lax.scan(advance, starting, (inputs, upstream))
    return (output.reshape(seq_total, SEQ, D), grad_tokens.reshape(seq_total, SEQ, D).astype(jnp.float32), totals[0], totals[1], totals[2], totals[3], totals[4], totals[5], totals[6], totals[7])
```

```python
import jax
import jax.numpy as jnp
from jax import lax
from jax.sharding import PartitionSpec as P

HEADS = 12
HEAD_DIM = 64
SEQ = 1024
EPSILON = 1e-05
BOTH = ("dp", "head")


def layer_norm(vector, gain_vec, bias_vec):
    row_mean = jnp.mean(vector, axis=-1, keepdims=True)
    centred = vector - row_mean
    variance = jnp.mean(centred * centred, axis=-1, keepdims=True)
    return centred * lax.rsqrt(variance + EPSILON) * gain_vec + bias_vec


def gelu_tanh(vector):
    return jax.nn.gelu(vector, approximate=True)


def contract_rows(left, right):
    return lax.dot_general(
        left, right, (((0,), (0,)), ((), ())), preferred_element_type=jnp.float32
    )


def contract_cols(left, right):
    return lax.dot_general(
        left, right, (((1,), (1,)), ((), ())), preferred_element_type=jnp.float32
    )


def causal_mask(first_row, row_count, key_count):
    query_pos = first_row + jnp.arange(row_count)[:, None]
    key_pos = jnp.arange(key_count)[None, :]
    return query_pos >= key_pos


def attend_sequence(triple):
    query_rows, key_rows, value_rows = triple
    seq_len = query_rows.shape[0]
    block_rows = min(512, seq_len)
    scaling = query_rows.shape[-1] ** (-0.5)
    out_parts = []
    log_parts = []
    for block_id in range(seq_len // block_rows):
        first_row = block_id * block_rows
        last_row = first_row + block_rows
        raw_scores = (
            jnp.einsum(
                "qhd,khd->hqk",
                query_rows[first_row:last_row],
                key_rows[:last_row],
                preferred_element_type=jnp.float32,
            )
            * scaling
        )
        scores = jnp.where(causal_mask(first_row, block_rows, last_row), raw_scores, -1e30)
        row_max = jnp.max(scores, axis=-1, keepdims=True)
        weights = jnp.exp(scores - row_max)
        row_total = jnp.sum(weights, axis=-1, keepdims=True)
        probs_low = (weights / row_total).astype(jnp.bfloat16)
        out_parts.append(
            jnp.einsum(
                "hqk,khd->qhd", probs_low, value_rows[:last_row], preferred_element_type=jnp.float32
            )
        )
        log_parts.append(row_max + jnp.log(row_total))
    return (jnp.concatenate(out_parts, axis=0), jnp.concatenate(log_parts, axis=1))


def sequence_grads(bundle):
    query_rows, key_rows, value_rows, log_totals, grad_rows = bundle
    seq_len = query_rows.shape[0]
    block_rows = min(512, seq_len)
    scaling = query_rows.shape[-1] ** (-0.5)
    query_parts = []
    grad_keys = jnp.zeros(key_rows.shape, jnp.float32)
    grad_values = jnp.zeros(value_rows.shape, jnp.float32)
    for block_id in range(seq_len // block_rows):
        first_row = block_id * block_rows
        last_row = first_row + block_rows
        query_block = query_rows[first_row:last_row]
        key_part = key_rows[:last_row]
        grad_block = grad_rows[first_row:last_row]
        raw_scores = (
            jnp.einsum("qhd,khd->hqk", query_block, key_part, preferred_element_type=jnp.float32)
            * scaling
        )
        scores = jnp.where(causal_mask(first_row, block_rows, last_row), raw_scores, -1e30)
        probs = jnp.exp(scores - log_totals[:, first_row:last_row])
        probs_low = probs.astype(jnp.bfloat16)
        grad_probs = jnp.einsum(
            "qhd,khd->hqk", grad_block, value_rows[:last_row], preferred_element_type=jnp.float32
        )
        grad_values = grad_values.at[:last_row].add(
            jnp.einsum("hqk,qhd->khd", probs_low, grad_block, preferred_element_type=jnp.float32)
        )
        centre = jnp.sum(probs * grad_probs, axis=-1, keepdims=True)
        grad_scores = (probs * (grad_probs - centre)).astype(jnp.bfloat16)
        query_parts.append(
            jnp.einsum("hqk,khd->qhd", grad_scores, key_part, preferred_element_type=jnp.float32)
            * scaling
        )
        grad_keys = grad_keys.at[:last_row].add(
            jnp.einsum("hqk,qhd->khd", grad_scores, query_block, preferred_element_type=jnp.float32)
            * scaling
        )
    return (jnp.concatenate(query_parts, axis=0), grad_keys, grad_values)


def to_sequences(rows):
    return lax.all_to_all(rows, "head", split_axis=0, concat_axis=1, tiled=True)


def to_positions(rows):
    return lax.all_to_all(rows, "head", split_axis=1, concat_axis=0, tiled=True)


def gather(shard, splits):
    share = shard.shape[0] // splits
    mine = lax.dynamic_slice_in_dim(shard, lax.axis_index("head") * share, share, 0)
    return lax.all_gather(mine.astype(jnp.bfloat16), BOTH, axis=0, tiled=True)


def scatter(total):
    part = lax.psum_scatter(total.astype(jnp.bfloat16), BOTH, scatter_dimension=0, tiled=True)
    return lax.all_gather(part, "head", axis=0, tiled=True).astype(jnp.float32)


def local(
    tokens,
    qkv_weight,
    proj_weight,
    up_weight,
    down_weight,
    attn_gain,
    attn_bias,
    ffn_gain,
    ffn_bias,
    cotangent,
):
    splits = lax.axis_size("head")
    model_width = tokens.shape[-1]
    norm_table = jnp.stack([attn_gain, attn_bias, ffn_gain, ffn_bias], axis=1)
    first = gather(jnp.concatenate([qkv_weight, norm_table], axis=1), splits)
    full_qkv = first[:, : 3 * model_width]
    table = first[:, 3 * model_width :].astype(jnp.float32)
    own_tokens = to_sequences(tokens)
    own_cot = to_sequences(cotangent)
    full_proj = gather(proj_weight, splits)
    full_up = gather(up_weight, splits)
    full_down = gather(down_weight, splits)
    seq_count = own_tokens.shape[0]
    tok_rows = seq_count * SEQ
    inputs = own_tokens.astype(jnp.float32).reshape(tok_rows, model_width)
    normed, norm_pull = jax.vjp(layer_norm, inputs, table[:, 0], table[:, 1])
    normed_low = normed.astype(jnp.bfloat16)
    mixed = jnp.dot(normed_low, full_qkv, preferred_element_type=jnp.float32).astype(jnp.bfloat16)
    mixed = mixed.reshape(seq_count, SEQ, 3, HEADS, HEAD_DIM)
    queries, key_rows, value_rows = mixed[:, :, 0], mixed[:, :, 1], mixed[:, :, 2]
    attended, log_totals = lax.map(attend_sequence, (queries, key_rows, value_rows))
    token_heads = attended.astype(jnp.bfloat16).reshape(tok_rows, model_width)
    middle = inputs + jnp.dot(token_heads, full_proj, preferred_element_type=jnp.float32)
    normed_two, norm_pull_two = jax.vjp(layer_norm, middle, table[:, 2], table[:, 3])
    second_low = normed_two.astype(jnp.bfloat16)
    hidden = jnp.dot(second_low, full_up, preferred_element_type=jnp.float32)
    active, gelu_pull = jax.vjp(gelu_tanh, hidden)
    active_low = active.astype(jnp.bfloat16)
    output = (middle + jnp.dot(active_low, full_down, preferred_element_type=jnp.float32)).astype(
        jnp.bfloat16
    )
    out_home = to_positions(output.reshape(seq_count, SEQ, model_width))
    flat_cot = own_cot.reshape(tok_rows, model_width)
    grad_down = contract_rows(active_low, flat_cot)
    (grad_active,) = gelu_pull(contract_cols(flat_cot, full_down))
    grad_hidden = grad_active.astype(jnp.bfloat16)
    grad_up = contract_rows(second_low, grad_hidden)
    grad_second, grad_ffn_gain, grad_ffn_bias = norm_pull_two(contract_cols(grad_hidden, full_up))
    grad_middle = flat_cot.astype(jnp.float32) + grad_second
    grad_branch = grad_middle.astype(jnp.bfloat16)
    grad_proj = contract_rows(token_heads, grad_branch)
    grad_heads = contract_cols(grad_branch, full_proj).astype(jnp.bfloat16)
    grad_attended = grad_heads.reshape(seq_count, SEQ, HEADS, HEAD_DIM)
    grad_query, grad_keys, grad_values = lax.map(
        sequence_grads, (queries, key_rows, value_rows, log_totals, grad_attended)
    )
    back_mixed = (
        jnp.stack([grad_query, grad_keys, grad_values], axis=2)
        .astype(jnp.bfloat16)
        .reshape(tok_rows, 3 * model_width)
    )
    grad_qkv = contract_rows(normed_low, back_mixed)
    grad_normed, grad_attn_gain, grad_attn_bias = norm_pull(contract_cols(back_mixed, full_qkv))
    grad_tokens = (grad_middle + grad_normed).reshape(seq_count, SEQ, model_width)
    grad_home = to_positions(grad_tokens.astype(jnp.bfloat16)).astype(jnp.float32)
    grad_table = jnp.stack([grad_attn_gain, grad_attn_bias, grad_ffn_gain, grad_ffn_bias], axis=1)
    shard_down = scatter(grad_down)
    shard_up = scatter(grad_up)
    shard_proj = scatter(grad_proj)
    shard_first = scatter(jnp.concatenate([grad_qkv, grad_table], axis=1))
    shard_table = shard_first[:, 3 * model_width :]
    return (
        out_home,
        grad_home,
        shard_first[:, : 3 * model_width],
        shard_proj,
        shard_up,
        shard_down,
        shard_table[:, 0],
        shard_table[:, 1],
        shard_table[:, 2],
        shard_table[:, 3],
    )


def solution(mesh):
    rows = P("dp", "head", None)
    placed = (rows,) + (P("dp", None),) * 4 + (P("dp"),) * 4 + (rows,)
    return jax.shard_map(
        local,
        mesh=mesh,
        in_specs=placed,
        out_specs=(rows, rows) + (P("dp", None),) * 4 + (P("dp"),) * 4,
        check_vma=False,
    )
```

```python
import functools

import jax
import jax.numpy as jnp
from jax import lax
from jax.experimental import pallas as pl
from jax.experimental.pallas import tpu as pltpu
from jax.sharding import PartitionSpec as P

HEADS = 12
HEAD_DIM = 64
SEQ = 1024
EPSILON = 1e-05
BOTH = ("dp", "head")
BLOCK = 256
GELU_A = 0.7978845608028654
GELU_B = 0.044715
F32 = jnp.float32
BF16 = jnp.bfloat16
PARAMS = pltpu.CompilerParams(vmem_limit_bytes=56 * 2**20)


def dot_nn(left, right):
    return lax.dot_general(left, right, (((1,), (0,)), ((), ())), preferred_element_type=F32)


def dot_nt(left, right):
    return lax.dot_general(left, right, (((1,), (1,)), ((), ())), preferred_element_type=F32)


def dot_tn(left, right):
    return lax.dot_general(left, right, (((0,), (0,)), ((), ())), preferred_element_type=F32)


def cost(micros):
    return pl.CostEstimate(
        flops=int(micros * 1.1e9), bytes_accessed=int(micros * 3e6), transcendentals=0
    )


def whole(*shape):
    return pl.BlockSpec(shape, lambda *_: (0,) * len(shape))


def rows(count, width):
    return pl.BlockSpec((count, width), lambda i, *_: (i, 0))


def shaped(shape, dtype):
    return jax.ShapeDtypeStruct(shape, dtype)


def normalise(vector):
    centred = vector - jnp.mean(vector, axis=-1, keepdims=True)
    inverse = lax.rsqrt(jnp.mean(centred * centred, axis=-1, keepdims=True) + EPSILON)
    return centred * inverse, inverse


def norm_back(unit, inverse, gain, grad):
    scaled = grad * gain
    return inverse * (
        scaled
        - jnp.mean(scaled, axis=-1, keepdims=True)
        - unit * jnp.mean(scaled * unit, axis=-1, keepdims=True)
    )


def first_kernel(x_ref, wa_ref, wb_ref, low_ref, mixed_ref, table_ref):
    wide = wa_ref.shape[1]
    used = mixed_ref.shape[1] - wide

    @pl.when(pl.program_id(0) == 0)
    def _():
        table_ref[...] = wb_ref[:, used:].astype(F32).T[:8]

    unit, _ = normalise(x_ref[...].astype(F32))
    low = (unit * table_ref[0:1] + table_ref[1:2]).astype(BF16)
    low_ref[...] = low
    mixed_ref[:, :wide] = dot_nn(low, wa_ref[...]).astype(BF16)
    mixed_ref[:, wide:] = dot_nn(low, wb_ref[:, :used]).astype(BF16)


def first(x, wa, wb, wide):
    tok, dim = x.shape
    return pl.pallas_call(
        first_kernel,
        grid=(tok // BLOCK,),
        in_specs=[rows(BLOCK, dim), whole(*wa.shape), whole(*wb.shape)],
        out_specs=[rows(BLOCK, dim), rows(BLOCK, wide), whole(8, dim)],
        out_shape=[shaped((tok, dim), BF16), shaped((tok, wide), BF16), shaped((8, dim), F32)],
        compiler_params=PARAMS,
        cost_estimate=cost(1),
    )(x, wa, wb)


def second_kernel(low_ref, wa_ref, wb_ref, mixed_ref):
    wide = wa_ref.shape[1]
    used = mixed_ref.shape[1] - wide
    mixed_ref[:, :wide] = dot_nn(low_ref[...], wa_ref[...]).astype(BF16)
    mixed_ref[:, wide:] = dot_nn(low_ref[...], wb_ref[:, :used]).astype(BF16)


def second(low, wa, wb, wide):
    tok, dim = low.shape
    return pl.pallas_call(
        second_kernel,
        grid=(tok // BLOCK,),
        in_specs=[rows(BLOCK, dim), whole(*wa.shape), whole(*wb.shape)],
        out_specs=rows(BLOCK, wide),
        out_shape=shaped((tok, wide), BF16),
        compiler_params=PARAMS,
        cost_estimate=cost(1),
    )(low, wa, wb)


def lane_low(count):
    return lax.broadcasted_iota(jnp.int32, (count, 128), 1) < HEAD_DIM


def upper():
    return lax.broadcasted_iota(jnp.int32, (BLOCK, BLOCK), 0) <= lax.broadcasted_iota(
        jnp.int32, (BLOCK, BLOCK), 1
    )


def keep_head(low_lanes, head, value):
    zero = jnp.zeros((), value.dtype)
    return jnp.where(low_lanes, value, zero) if head == 0 else jnp.where(low_lanes, zero, value)


def attend_kernel(q_ref, k_ref, v_ref, o_ref, l_ref):
    seq = q_ref.shape[0]
    low_lanes = lane_low(BLOCK)
    allowed = upper()
    scaling = jnp.asarray(HEAD_DIM**-0.5, BF16)
    tiles = [(block, head) for block in range(seq // BLOCK) for head in range(2)]
    with_ones = jnp.concatenate([v_ref[...], jnp.ones((seq, 128), BF16)], axis=1)

    def score(block, head):
        end = (block + 1) * BLOCK
        queries = keep_head(low_lanes, head, q_ref[block * BLOCK : end, :] * scaling)
        raw = dot_nt(k_ref[:end, :], queries)
        last = jnp.where(allowed, raw[end - BLOCK :, :], -1e30)
        return jnp.concatenate([raw[: end - BLOCK, :], last], axis=0) if block else last

    ahead = 3
    waiting = [score(*tile) for tile in tiles[:ahead]]
    parts = []
    for step, (block, head) in enumerate(tiles):
        end = (block + 1) * BLOCK
        if step + ahead < len(tiles):
            waiting.append(score(*tiles[step + ahead]))
        scores = waiting.pop(0)
        row_max = jnp.max(scores, axis=0, keepdims=True)
        weights = jnp.exp(scores - row_max).astype(BF16)
        summed = dot_tn(weights, with_ones[:end])
        totals = summed[:, 128:]
        parts.append(summed[:, :128] / totals)
        l_ref[0, head : head + 1, block * BLOCK : end] = row_max + jnp.log(totals.T[0:1, :])
        if head == 1:
            o_ref[block * BLOCK : end, :] = jnp.where(low_lanes, parts[-2], parts[-1]).astype(BF16)


def attend(mixed):
    seq, wide = mixed.shape
    pairs = wide // 384

    def column(which):
        return pl.BlockSpec((seq, 128), lambda i: (0, which * pairs + i))

    return pl.pallas_call(
        attend_kernel,
        grid=(pairs,),
        in_specs=[column(0), column(1), column(2)],
        out_specs=[column(0), pl.BlockSpec((1, 2, seq), lambda i: (i, 0, 0))],
        out_shape=[shaped((seq, pairs * 128), BF16), shaped((pairs, 2, seq), F32)],
        compiler_params=PARAMS,
        cost_estimate=cost(1),
    )(mixed, mixed, mixed)


def attend_back_kernel(
    q_ref, k_ref, v_ref, do_ref, o_ref, l_ref, dq_ref, dk_ref, dv_ref, sum_k, sum_v
):
    seq = q_ref.shape[0]
    low_lanes = lane_low(BLOCK)
    low_all = lane_low(seq)
    allowed = upper()
    scaling = jnp.asarray(HEAD_DIM**-0.5, BF16)
    head_keys = [keep_head(low_all, head, k_ref[...]) for head in range(2)]
    for block in reversed(range(seq // BLOCK)):
        start, end = block * BLOCK, (block + 1) * BLOCK
        queries = q_ref[start:end, :] * scaling
        grads = do_ref[start:end, :]
        dots = (grads.astype(F32) * o_ref[start:end, :].astype(F32)).T
        add_q = add_k = add_v = None
        for head in range(2):
            q_head = keep_head(low_lanes, head, queries)
            g_head = keep_head(low_lanes, head, grads)
            centre = jnp.sum(dots[HEAD_DIM * head : HEAD_DIM * (head + 1)], axis=0, keepdims=True)
            scores = dot_nt(k_ref[:end, :], q_head)
            probs = jnp.exp(scores - l_ref[0, head : head + 1, start:end])
            last = jnp.where(allowed, probs[start:, :], 0.0)
            probs = jnp.concatenate([probs[:start, :], last], axis=0) if block else last
            grad_probs = dot_nt(v_ref[:end, :], g_head)
            grad_scores = (probs * (grad_probs - centre)).astype(BF16)
            terms = (
                dot_tn(grad_scores, head_keys[head][:end]),
                dot_nn(grad_scores, q_head),
                dot_nn(probs.astype(BF16), g_head),
            )
            if head == 0:
                add_q, add_k, add_v = terms
            else:
                add_q, add_k, add_v = add_q + terms[0], add_k + terms[1], add_v + terms[2]
        dq_ref[start:end, :] = (add_q * HEAD_DIM**-0.5).astype(BF16)
        if end == seq:
            sum_k[...] = add_k
            sum_v[...] = add_v
        else:
            sum_k[:end, :] += add_k
            sum_v[:end, :] += add_v
    dk_ref[...] = sum_k[...].astype(BF16)
    dv_ref[...] = sum_v[...].astype(BF16)


def attend_back(mixed, grad, attended, logs):
    seq, wide = mixed.shape
    pairs = wide // 384

    def column(which):
        return pl.BlockSpec((seq, 128), lambda i: (0, which * pairs + i))

    return pl.pallas_call(
        attend_back_kernel,
        grid=(pairs,),
        in_specs=[column(0), column(1), column(2), column(0), column(0)]
        + [pl.BlockSpec((1, 2, seq), lambda i: (i, 0, 0))],
        out_specs=[column(0)] * 3,
        out_shape=[shaped((seq, pairs * 128), BF16)] * 3,
        scratch_shapes=[pltpu.VMEM((seq, 128), F32)] * 2,
        compiler_params=PARAMS,
        cost_estimate=cost(1),
    )(mixed, mixed, mixed, grad, attended, logs)


def proj_kernel(core_ref, x_ref, am_ref, at_ref, pm_ref, pt_ref, table_ref, mid_ref, low_ref):
    half = am_ref.shape[1]
    mine = pl.multiple_of(core_ref[0] * half, half)
    theirs = pl.multiple_of((1 - core_ref[0]) * half, half)
    a_mine, a_theirs = am_ref[...], at_ref[...]
    for place, weight in ((mine, pm_ref), (theirs, pt_ref)):
        mid_ref[:, pl.ds(place, half)] = (
            x_ref[:, pl.ds(place, half)].astype(F32)
            + dot_nn(a_mine, weight[pl.ds(mine, half), :])
            + dot_nn(a_theirs, weight[pl.ds(theirs, half), :])
        )
    unit, _ = normalise(mid_ref[...])
    low_ref[...] = (unit * table_ref[2:3] + table_ref[3:4]).astype(BF16)


def proj_spec(dim):
    half = dim // 2
    return pl.BlockSpec((dim, half), lambda i, *_: (0, 4))


def project(core, x, a_mine, a_theirs, w_mine, w_theirs, table):
    tok, dim = x.shape
    half = dim // 2
    return pl.pallas_call(
        proj_kernel,
        grid_spec=pltpu.PrefetchScalarGridSpec(
            num_scalar_prefetch=1,
            grid=(tok // BLOCK,),
            in_specs=[rows(BLOCK, dim), rows(BLOCK, half), rows(BLOCK, half)]
            + [proj_spec(dim), proj_spec(dim), whole(8, dim)],
            out_specs=[rows(BLOCK, dim), rows(BLOCK, dim)],
        ),
        out_shape=[shaped((tok, dim), F32), shaped((tok, dim), BF16)],
        compiler_params=PARAMS,
        cost_estimate=cost(1),
    )(core, x, a_mine, a_theirs, w_mine, w_theirs, table)


def ffn_kernel(final, *refs):
    low_ref, cot_ref, up_ref, down_ref, out_in, back_in = refs[: 6 if final else 5] + (
        () if final else (None,)
    )
    out_ref, back_ref, gu_ref, gd_ref, out_sum, act, hid = refs[6 if final else 5 :]
    step = pl.program_id(0)
    up, down = up_ref[...], down_ref[...]

    @pl.when(step == 0)
    def _():
        out_sum[...] = out_in[...]
        back_ref[...] = back_in[...] if final else jnp.zeros_like(back_ref)

    for start in range(0, low_ref.shape[0], BLOCK):
        here = pl.ds(start, BLOCK)
        hidden = dot_nn(low_ref[here, :], up)
        grad_active = dot_nt(cot_ref[here, :], down)
        square = hidden * hidden
        bend = jnp.tanh(hidden * (GELU_A + (GELU_A * GELU_B) * square))
        gate = 0.5 + 0.5 * bend
        active = (hidden * gate).astype(BF16)
        slope = gate + hidden * (0.5 - 0.5 * bend * bend) * (
            GELU_A + (3 * GELU_A * GELU_B) * square
        )
        grad_hidden = (grad_active * slope).astype(BF16)
        act[here, :] = active
        hid[here, :] = grad_hidden
        out_sum[here, :] += dot_nn(active, down)
        back_ref[here, :] += dot_nt(grad_hidden, up)
    gu_ref[...] = dot_tn(low_ref[...], hid[...]).astype(BF16)
    gd_ref[...] = dot_tn(act[...], cot_ref[...]).astype(BF16)

    @pl.when(step == pl.num_programs(0) - 1)
    def _():
        out_ref[...] = out_sum[...].astype(out_ref.dtype)


def feed_forward(low, cot, up, down, out_in, back_in=None):
    tok, dim = low.shape
    final = back_in is not None
    chunk = dim
    wide = down.shape[0]
    return pl.pallas_call(
        functools.partial(ffn_kernel, final),
        grid=(wide // chunk,),
        in_specs=[whole(tok, dim), whole(tok, dim)]
        + [pl.BlockSpec((dim, chunk), lambda i: (0, i)), rows(chunk, dim)]
        + [whole(tok, dim)] * (2 if final else 1),
        out_specs=[whole(tok, dim), whole(tok, dim)]
        + [pl.BlockSpec((dim, chunk), lambda i: (0, i)), rows(chunk, dim)],
        out_shape=[shaped((tok, dim), BF16 if final else F32), shaped((tok, dim), F32)]
        + [shaped((dim, wide), BF16), shaped((wide, dim), BF16)],
        scratch_shapes=[pltpu.VMEM((tok, dim), F32)] + [pltpu.VMEM((tok, chunk), BF16)] * 2,
        compiler_params=PARAMS,
        cost_estimate=cost(1),
    )(low, cot, up, down, out_in, *((back_in,) if final else ()))


def middle_kernel(
    core_ref, mid_ref, back_ref, cot_ref, table_ref, pm_ref, pt_ref, am_ref, at_ref,
    grad_ref, gm_ref, gt_ref, wm_ref, wt_ref, norm_ref, sum_m, sum_t,
):
    half = am_ref.shape[1]
    step = pl.program_id(0)
    mine = pl.multiple_of(core_ref[0] * half, half)
    theirs = pl.multiple_of((1 - core_ref[0]) * half, half)

    @pl.when(step == 0)
    def _():
        sum_m[...] = jnp.zeros_like(sum_m)
        sum_t[...] = jnp.zeros_like(sum_t)
        norm_ref[...] = jnp.zeros_like(norm_ref)

    unit, inverse = normalise(mid_ref[...])
    grad = back_ref[...]
    norm_ref[0:1] += jnp.sum(grad * unit, axis=0, keepdims=True)
    norm_ref[1:2] += jnp.sum(grad, axis=0, keepdims=True)
    grad_ref[...] = cot_ref[...].astype(F32) + norm_back(unit, inverse, table_ref[2:3], grad)
    branch_m = grad_ref[:, pl.ds(mine, half)].astype(BF16)
    branch_t = grad_ref[:, pl.ds(theirs, half)].astype(BF16)
    for place, out in ((mine, gm_ref), (theirs, gt_ref)):
        out[...] = (
            dot_nt(branch_m, pm_ref[pl.ds(place, half), :])
            + dot_nt(branch_t, pt_ref[pl.ds(place, half), :])
        ).astype(BF16)
    for branch, total in ((branch_m, sum_m), (branch_t, sum_t)):
        total[pl.ds(mine, half), :] += dot_tn(am_ref[...], branch)
        total[pl.ds(theirs, half), :] += dot_tn(at_ref[...], branch)

    @pl.when(step == pl.num_programs(0) - 1)
    def _():
        wm_ref[...] = sum_m[...].astype(BF16)
        wt_ref[...] = sum_t[...].astype(BF16)


def middle_back(core, middle, back, cot, table, w_mine, w_theirs, a_mine, a_theirs):
    tok, dim = middle.shape
    half = dim // 2
    return pl.pallas_call(
        middle_kernel,
        grid_spec=pltpu.PrefetchScalarGridSpec(
            num_scalar_prefetch=1,
            grid=(tok // BLOCK,),
            in_specs=[rows(BLOCK, dim)] * 3
            + [whole(8, dim), proj_spec(dim), proj_spec(dim)]
            + [rows(BLOCK, half)] * 2,
            out_specs=[rows(BLOCK, dim), rows(BLOCK, half), rows(BLOCK, half)]
            + [whole(dim, half), whole(dim, half), whole(8, dim)],
            scratch_shapes=[pltpu.VMEM((dim, half), F32)] * 2,
        ),
        out_shape=[shaped((tok, dim), F32)]
        + [shaped((tok, half), BF16)] * 2
        + [shaped((dim, half), BF16)] * 2
        + [shaped((8, dim), F32)],
        compiler_params=PARAMS,
        cost_estimate=cost(1),
    )(core, middle, back, cot, table, w_mine, w_theirs, a_mine, a_theirs)


def qkv_grad_kernel(low_ref, q_ref, k_ref, v_ref, *refs):
    norm_refs, out_ref = refs[:-1], refs[-1]
    wide = q_ref.shape[1]
    for place, part in enumerate((q_ref, k_ref, v_ref)):
        out_ref[:, place * wide : (place + 1) * wide] = dot_tn(low_ref[...], part[...]).astype(BF16)
    tail = jnp.zeros((128, low_ref.shape[1]), F32)
    if norm_refs:
        tail = jnp.concatenate([norm_refs[0][:2], norm_refs[1][:2], tail[4:]], axis=0)
    out_ref[:, 3 * wide :] = tail.T.astype(BF16)


def qkv_grad(low, parts, *norms):
    tok, dim = low.shape
    wide = parts[0].shape[1]
    return pl.pallas_call(
        qkv_grad_kernel,
        in_specs=[whole(tok, dim)] + [whole(tok, wide)] * 3 + [whole(8, dim)] * len(norms),
        out_specs=whole(dim, 3 * wide + 128),
        out_shape=shaped((dim, 3 * wide + 128), BF16),
        compiler_params=PARAMS,
        cost_estimate=cost(1),
    )(low, *parts, *norms)


def last_kernel(x_ref, grad_ref, table_ref, *refs):
    parts, weights, (out_ref, norm_ref) = refs[:6], refs[6:10], refs[10:]

    @pl.when(pl.program_id(0) == 0)
    def _():
        norm_ref[...] = jnp.zeros_like(norm_ref)

    grad = None
    for side in range(2):
        left = jnp.concatenate([part[...] for part in parts[3 * side : 3 * side + 3]], axis=1)
        wa, wb = weights[2 * side], weights[2 * side + 1]
        cut = wa.shape[1]
        term = dot_nt(left[:, :cut], wa[...]) + dot_nt(
            left[:, cut:], wb[:, : left.shape[1] - cut]
        )
        grad = term if grad is None else grad + term
    unit, inverse = normalise(x_ref[...].astype(F32))
    norm_ref[0:1] += jnp.sum(grad * unit, axis=0, keepdims=True)
    norm_ref[1:2] += jnp.sum(grad, axis=0, keepdims=True)
    out_ref[...] = (grad_ref[...] + norm_back(unit, inverse, table_ref[0:1], grad)).astype(BF16)


def last(x, grad, table, parts, weights):
    tok, dim = x.shape
    return pl.pallas_call(
        last_kernel,
        grid=(tok // BLOCK,),
        in_specs=[rows(BLOCK, dim)] * 2
        + [whole(8, dim)]
        + [rows(BLOCK, part.shape[1]) for part in parts]
        + [whole(*weight.shape) for weight in weights],
        out_specs=[rows(BLOCK, dim), whole(8, dim)],
        out_shape=[shaped((tok, dim), BF16), shaped((8, dim), F32)],
        compiler_params=PARAMS,
        cost_estimate=cost(1),
    )(x, grad, table, *parts, *weights)


class Grid:
    def __init__(self):
        self.z_count = lax.axis_size("dp") // 2
        self.dp, self.head = lax.axis_index("dp"), lax.axis_index("head")
        self.z, self.y, self.x, self.c = self.dp // 2, self.dp % 2, self.head // 2, self.head % 2
        assert lax.axis_size("head") == 4 and lax.axis_size("dp") % 2 == 0

    def send(self, value, z=0, y=0, x=0, c=0):
        pairs = []
        for source in range(self.z_count * 8):
            zi, yi, xi, ci = source // 8, source // 4 % 2, source // 2 % 2, source % 2
            zt, yt, xt, ct = (zi + z) % self.z_count, yi ^ y, xi ^ x, ci ^ c
            pairs.append((source, ((zt * 2 + yt) * 2 + xt) * 2 + ct))
        return lax.ppermute(value, BOTH, pairs)

    def pick(self, value, axis, index):
        return lax.dynamic_index_in_dim(value, index, axis, keepdims=False)

    def join(self, mine, other, index, axis):
        first_one = index == 0
        return jnp.stack(
            [jnp.where(first_one, mine, other), jnp.where(first_one, other, mine)], axis=axis
        )

    def over_z(self, piece):
        out = jnp.zeros((self.z_count,) + piece.shape, piece.dtype)
        got = [piece] + [self.send(piece, z=step) for step in range(1, self.z_count)]
        for step, part in enumerate(got):
            place = (self.z - step) % self.z_count
            out = lax.dynamic_update_index_in_dim(out, part, place, 0)
        return out

    def over_y(self, value):
        return self.join(value, self.send(value, y=1), self.y, 1)

    def over_x(self, value, axis):
        return self.join(value, self.send(value, x=1), self.x, axis)

    def halves(self, name, values):
        axis, index = (1, self.y) if name == "y" else (values[0].ndim - 3, self.x)

        def part(place):
            return sum(self.pick(v, axis, place).astype(F32) for v in values).astype(BF16)

        return part(1 - index), part(index)

    def end(self, keep, got):
        total = keep.astype(F32) + got.astype(F32)
        low = total.astype(BF16)
        out = self.pick(total, 0, self.z)
        for step in range(1, self.z_count):
            out = out + self.send(self.pick(low, 0, (self.z + step) % self.z_count), z=step).astype(
                F32
            )
        return out.astype(BF16)

    def share(self, piece):
        both = self.join(piece, self.send(piece, x=1), self.x, 0)
        return self.join(both, self.send(both, c=1), self.c, 0)


def exchange(value):
    return lax.all_to_all(value, "head", split_axis=0, concat_axis=0, tiled=True)


def after(value, *done):
    return lax.optimization_barrier((value, done))[0]


def local(
    tokens,
    qkv_weight,
    proj_weight,
    up_weight,
    down_weight,
    attn_gain,
    attn_bias,
    ffn_gain,
    ffn_bias,
    cotangent,
):
    grid = Grid()
    dim = tokens.shape[-1]
    share = qkv_weight.shape[0]
    part = share // 2
    half = dim // 2
    hidden = up_weight.shape[1]
    dp_count = lax.axis_size("dp")
    fan = hidden // dp_count // 2
    core = grid.c.reshape(1).astype(jnp.int32)

    def row_half(value):
        return lax.dynamic_slice_in_dim(value, grid.x * part, part, 0)

    qkv = grid.pick(row_half(qkv_weight).reshape(part, 3, 2, half), 2, grid.c).reshape(part, -1)
    table = jnp.stack([attn_gain, attn_bias, ffn_gain, ffn_bias], axis=1)
    table = jnp.pad(row_half(table), ((0, 0), (0, 124)))
    piece = jnp.concatenate([qkv, table], axis=1).astype(BF16)
    cut = piece.shape[1] // 2
    up = grid.pick(row_half(up_weight).reshape(part, dp_count, 2, fan), 2, grid.c)
    proj = grid.pick(row_half(proj_weight).reshape(part, 2, half), 1, grid.c)
    up_piece = jnp.concatenate([up.reshape(part, -1), proj], axis=1).astype(BF16)
    down_piece = grid.pick(down_weight.reshape(2, fan, dim), 0, grid.c).astype(BF16)

    assert tokens.shape[0] == 4 and tokens.shape[1] * 4 == SEQ
    x = exchange(tokens).reshape(SEQ, dim)

    def flat(value):
        return value.reshape(-1, value.shape[-1])

    first_z = grid.over_z(piece)
    wa_y = grid.over_y(first_z[..., :cut])
    wb_x = grid.over_x(after(first_z[..., cut:], x), 1)
    up_z = grid.over_z(after(up_piece, first_z))
    wa_mine = flat(grid.over_x(after(wa_y, wb_x), 2))
    wb_mine = flat(grid.over_y(after(wb_x, wa_y)))
    wa_theirs, wb_theirs = grid.send(wa_mine, c=1), grid.send(wb_mine, c=1)
    up_y = grid.over_y(after(up_z, wb_mine))
    cot = exchange(after(cotangent, wa_mine)).reshape(SEQ, dim)
    down_z = grid.over_z(after(down_piece, up_z))

    low, mixed_mine, rows_table = first(x, wa_mine, wb_mine, 3 * half)
    att_mine, log_mine = attend(mixed_mine)
    up_mine = flat(grid.over_x(after(up_y, cot, att_mine), 2))
    mixed_theirs = second(after(low, att_mine, cot, up_y), wa_theirs, wb_theirs, 3 * half)
    down_mine = flat(grid.over_y(after(down_z, mixed_theirs)))
    att_theirs, log_theirs = attend(after(mixed_theirs, down_z))
    up_theirs, down_theirs = grid.send(up_mine, c=1), grid.send(down_mine, c=1)
    middle, low_two = project(core, x, att_mine, att_theirs, up_mine, up_theirs, rows_table)
    out, back, gu_mine, gd_mine = feed_forward(low_two, cot, up_mine, down_mine, middle)
    out, back, gu_theirs, gd_theirs = feed_forward(
        low_two, cot, up_theirs, down_theirs, out, back
    )
    out_home = exchange(out.reshape(4, SEQ // 4, dim))

    def blocks(value):
        return value.reshape(grid.z_count, 2, 2, -1, value.shape[-1])

    gd_core, gu_core = grid.send(gd_theirs, c=1), grid.send(gu_theirs, c=1)
    grad_middle, ga_mine, ga_theirs, gp_mine, gp_theirs, norm_two = middle_back(
        core, middle, back, cot, rows_table, up_mine, up_theirs, att_mine, att_theirs
    )
    gp_core = grid.send(gp_theirs, c=1)
    gd_out, gd_keep = grid.halves("y", [blocks(gd_mine), blocks(after(gd_core, grad_middle))])
    gu_out, gu_keep = grid.halves("x", [blocks(gu_mine), blocks(after(gu_core, grad_middle))])
    gd_got, gu_got = grid.send(gd_out, y=1), grid.send(gu_out, x=1)
    d_theirs = attend_back(
        mixed_theirs, after(ga_theirs, gd_out, gu_out, out_home), att_theirs, log_theirs
    )
    gp_out, gp_keep = grid.halves("x", [blocks(gp_mine), blocks(after(gp_core, d_theirs))])
    gp_got = grid.send(gp_out, x=1)
    gq_theirs = qkv_grad(low, after(d_theirs, gp_out))
    gq_core = grid.send(gq_theirs, c=1)
    gd_out, gd_keep = grid.halves("x", [gd_keep, after(gd_got, gq_theirs)])
    gu_out, gu_keep = grid.halves(
        "y",
        [
            jnp.concatenate([gu_keep, gp_keep], axis=-1),
            jnp.concatenate([after(gu_got, gq_theirs), gp_got], axis=-1),
        ],
    )
    gd_got, gu_got = grid.send(gd_out, x=1), grid.send(gu_out, y=1)
    d_mine = attend_back(mixed_mine, after(ga_mine, gd_out, gu_out), att_mine, log_mine)
    gd_got, gu_got = after((gd_got, gu_got), d_mine)
    sum_down = grid.end(gd_keep, gd_got)
    grad_x, norm_one = last(
        x,
        after(grad_middle, gd_got, gu_got),
        rows_table,
        d_mine + d_theirs,
        (wa_mine, wb_mine, wa_theirs, wb_theirs),
    )
    grad_home = exchange(grad_x.reshape(4, SEQ // 4, dim)).astype(F32)
    sum_up = grid.end(gu_keep, gu_got)
    gq_mine = qkv_grad(low, after(d_mine, sum_down), norm_one, norm_two)
    gq_out, gq_keep = grid.halves("y", [blocks(gq_mine), blocks(gq_core)])
    gq_got = grid.send(gq_out, y=1)
    gq_out, gq_keep = grid.halves("x", [gq_keep, gq_got])
    gq_got = grid.send(after(gq_out, sum_up), x=1)
    sum_qkv = grid.end(gq_keep, gq_got)

    all_up = grid.share(sum_up).reshape(2, share, -1)
    shard_up = (
        all_up[:, :, : 2 * dim]
        .reshape(2, share, dp_count, fan)
        .transpose(1, 2, 0, 3)
        .reshape(share, hidden)
        .astype(F32)
    )
    shard_proj = all_up[:, :, 2 * dim :].transpose(1, 0, 2).reshape(share, dim).astype(F32)
    shard_down = grid.share(sum_down).reshape(-1, dim).astype(F32)
    all_qkv = grid.share(sum_qkv).reshape(2, share, -1)
    shard_qkv = all_qkv[:, :, : 3 * half].reshape(2, share, 3, half)
    shard_qkv = shard_qkv.transpose(1, 2, 0, 3).reshape(share, 3 * dim).astype(F32)
    norms = all_qkv[:, :, 3 * half : 3 * half + 4].astype(F32)
    norms = (norms[0] + norms[1]).T
    return (
        out_home,
        grad_home,
        shard_qkv,
        shard_proj,
        shard_up,
        shard_down,
        norms[0],
        norms[1],
        norms[2],
        norms[3],
    )


def solution(mesh):
    spread = P("dp", "head", None)
    placed = (spread,) + (P("dp", None),) * 4 + (P("dp"),) * 4 + (spread,)
    return jax.shard_map(
        local,
        mesh=mesh,
        in_specs=placed,
        out_specs=(spread, spread) + (P("dp", None),) * 4 + (P("dp"),) * 4,
        check_vma=False,
    )
```

```python
import functools

import jax
import jax.numpy as jnp
from jax import lax
from jax.experimental import pallas as pl
from jax.experimental.pallas import tpu as pltpu
from jax.sharding import PartitionSpec as P

HEADS = 12
HEAD_DIM = 64
SEQ = 1024
EPSILON = 1e-05
BOTH = ("dp", "head")
BLOCK = 256
GELU_A = 0.7978845608028654
GELU_B = 0.044715
F32 = jnp.float32
BF16 = jnp.bfloat16


def params(mebi):
    return pltpu.CompilerParams(vmem_limit_bytes=mebi * 2**20)


def dot_nn(left, right):
    return lax.dot_general(left, right, (((1,), (0,)), ((), ())), preferred_element_type=F32)


def dot_nt(left, right):
    return lax.dot_general(left, right, (((1,), (1,)), ((), ())), preferred_element_type=F32)


def dot_tn(left, right):
    return lax.dot_general(left, right, (((0,), (0,)), ((), ())), preferred_element_type=F32)


def cost(micros):
    return pl.CostEstimate(
        flops=int(micros * 1.1e9), bytes_accessed=int(micros * 3e6), transcendentals=0
    )


def whole(*shape):
    return pl.BlockSpec(shape, lambda *_: (0,) * len(shape))


def part_of(pair, which):
    parts, _, count, dim = pair.shape
    return pl.BlockSpec((parts, 1, count, dim), lambda *_: (0, which, 0, 0))


def part_rows(pair, which):
    _, _, count, dim = pair.shape
    return pl.BlockSpec((1, 1, count, dim), lambda i, *_: (i, which, 0, 0))


def rows(count, width):
    return pl.BlockSpec((count, width), lambda i, *_: (i, 0))


def shaped(shape, dtype):
    return jax.ShapeDtypeStruct(shape, dtype)


def normalise(vector):
    centred = vector - jnp.mean(vector, axis=-1, keepdims=True)
    inverse = lax.rsqrt(jnp.mean(centred * centred, axis=-1, keepdims=True) + EPSILON)
    return centred * inverse, inverse


def norm_back(unit, inverse, gain, grad):
    scaled = grad * gain
    return inverse * (
        scaled
        - jnp.mean(scaled, axis=-1, keepdims=True)
        - unit * jnp.mean(scaled * unit, axis=-1, keepdims=True)
    )


def proj_kernel(core_ref, x_ref, am_ref, at_ref, pm_ref, pt_ref, table_ref, mid_ref, low_ref, total):
    half = am_ref.shape[1]
    mine = pl.multiple_of(core_ref[0] * half, half)
    theirs = pl.multiple_of((1 - core_ref[0]) * half, half)
    a_mine, a_theirs = am_ref[...], at_ref[...]
    for place, weight in ((mine, pm_ref), (theirs, pt_ref)):
        total[:, pl.ds(place, half)] = (
            x_ref[0, 0, :, pl.ds(place, half)].astype(F32)
            + dot_nn(a_mine, weight[pl.ds(mine, half), :])
            + dot_nn(a_theirs, weight[pl.ds(theirs, half), :])
        )
    mid_ref[...] = total[...].astype(BF16)
    unit, _ = normalise(total[...])
    low_ref[...] = (unit * table_ref[2:3] + table_ref[3:4]).astype(BF16)


def proj_spec(dim):
    half = dim // 2
    return pl.BlockSpec((dim, half), lambda i, *_: (0, 4))


def project(core, x, a_mine, a_theirs, w_mine, w_theirs, table):
    tok, dim = SEQ, x.shape[-1]
    half = dim // 2
    return pl.pallas_call(
        proj_kernel,
        grid_spec=pltpu.PrefetchScalarGridSpec(
            num_scalar_prefetch=1,
            grid=(tok // BLOCK,),
            in_specs=[part_rows(x, 0), rows(BLOCK, half), rows(BLOCK, half)]
            + [proj_spec(dim), proj_spec(dim), whole(8, dim)],
            out_specs=[rows(BLOCK, dim), rows(BLOCK, dim)],
            scratch_shapes=[pltpu.VMEM((BLOCK, dim), F32)],
        ),
        out_shape=[shaped((tok, dim), BF16), shaped((tok, dim), BF16)],
        compiler_params=params(58),
        cost_estimate=cost(0.01),
    )(core, x, a_mine, a_theirs, w_mine, w_theirs, table)


def middle_kernel(
    core_ref, mid_ref, back_ref, cot_ref, table_ref, pm_ref, pt_ref, am_ref, at_ref,
    grad_ref, gm_ref, gt_ref, wm_ref, wt_ref, norm_ref, heads, branch,
):
    half = am_ref.shape[1]
    step = pl.program_id(0)
    mine = pl.multiple_of(core_ref[0] * half, half)
    theirs = pl.multiple_of((1 - core_ref[0]) * half, half)
    here = pl.ds(pl.multiple_of(step * BLOCK, BLOCK), BLOCK)

    @pl.when(step == 0)
    def _():
        norm_ref[...] = jnp.zeros_like(norm_ref)

    unit, inverse = normalise(mid_ref[...].astype(F32))
    grad = back_ref[...].astype(F32)
    norm_ref[0:1] += jnp.sum(grad * unit, axis=0, keepdims=True)
    norm_ref[1:2] += jnp.sum(grad, axis=0, keepdims=True)
    back = norm_back(unit, inverse, table_ref[2:3], grad)
    grad_ref[...] = (cot_ref[0, 0].astype(F32) + back).astype(BF16)
    branch[here, :half] = grad_ref[:, pl.ds(mine, half)]
    branch[here, half:] = grad_ref[:, pl.ds(theirs, half)]
    heads[here, :half] = am_ref[...]
    heads[here, half:] = at_ref[...]
    for place, out in ((mine, gm_ref), (theirs, gt_ref)):
        out[...] = (
            dot_nt(branch[here, :half], pm_ref[pl.ds(place, half), :])
            + dot_nt(branch[here, half:], pt_ref[pl.ds(place, half), :])
        ).astype(BF16)

    @pl.when(step == pl.num_programs(0) - 1)
    def _():
        for place, start in ((mine, 0), (theirs, half)):
            total = dot_tn(heads[:, start : start + half], branch[...]).astype(BF16)
            wm_ref[pl.ds(place, half), :] = total[:, :half]
            wt_ref[pl.ds(place, half), :] = total[:, half:]


def middle_back(core, middle, back, cot, table, w_mine, w_theirs, a_mine, a_theirs):
    tok, dim = middle.shape
    half = dim // 2
    return pl.pallas_call(
        middle_kernel,
        grid_spec=pltpu.PrefetchScalarGridSpec(
            num_scalar_prefetch=1,
            grid=(tok // BLOCK,),
            in_specs=[rows(BLOCK, dim), rows(BLOCK, dim), part_rows(cot, 1)]
            + [whole(8, dim), proj_spec(dim), proj_spec(dim)]
            + [rows(BLOCK, half)] * 2,
            out_specs=[rows(BLOCK, dim), rows(BLOCK, half), rows(BLOCK, half)]
            + [whole(dim, half), whole(dim, half), whole(8, dim)],
            scratch_shapes=[pltpu.VMEM((tok, dim), BF16)] * 2,
        ),
        out_shape=[shaped((tok, dim), BF16)]
        + [shaped((tok, half), BF16)] * 2
        + [shaped((dim, half), BF16)] * 2
        + [shaped((8, dim), F32)],
        compiler_params=params(58),
        cost_estimate=cost(0.01),
    )(core, middle, back, cot, table, w_mine, w_theirs, a_mine, a_theirs)


def lane_low(count):
    return lax.broadcasted_iota(jnp.int32, (count, 128), 1) < HEAD_DIM


def upper():
    return lax.broadcasted_iota(jnp.int32, (BLOCK, BLOCK), 0) <= lax.broadcasted_iota(
        jnp.int32, (BLOCK, BLOCK), 1
    )


def keep_head(low_lanes, head, value):
    zero = jnp.zeros((), value.dtype)
    return jnp.where(low_lanes, value, zero) if head == 0 else jnp.where(low_lanes, zero, value)


def attend_kernel(first, *refs):
    if first:
        x_ref, w_ref, tail_ref, low_ref, mixed_ref, o_ref, l_ref, table_ref = refs
    else:
        low_ref, w_ref, mixed_ref, o_ref, l_ref = refs
    seq = mixed_ref.shape[0]

    if first:

        @pl.when(pl.program_id(0) == 0)
        def _():
            table_ref[...] = tail_ref[...].astype(F32).T[:8]
            for start in range(0, seq, BLOCK):
                here = pl.ds(start, BLOCK)
                unit, _ = normalise(x_ref[start // BLOCK, 0].astype(F32))
                low_ref[here, :] = (unit * table_ref[0:1] + table_ref[1:2]).astype(BF16)

    mixed_ref[...] = dot_nn(low_ref[...], w_ref[...]).astype(BF16)
    q_ref, k_ref, v_ref = (mixed_ref.at[:, 128 * i : 128 * (i + 1)] for i in range(3))
    low_lanes = lane_low(BLOCK)
    allowed = upper()
    scaling = jnp.asarray(HEAD_DIM**-0.5, BF16)
    tiles = [(block, head) for block in range(seq // BLOCK) for head in range(2)]
    with_ones = jnp.concatenate([v_ref[...], jnp.ones((seq, 128), BF16)], axis=1)

    def score(block, head):
        end = (block + 1) * BLOCK
        queries = keep_head(low_lanes, head, q_ref[block * BLOCK : end, :] * scaling)
        raw = dot_nt(k_ref[:end, :], queries)
        last = jnp.where(allowed, raw[end - BLOCK :, :], -1e30)
        return jnp.concatenate([raw[: end - BLOCK, :], last], axis=0) if block else last

    ahead = 3
    waiting = [score(*tile) for tile in tiles[:ahead]]
    parts = []
    for step, (block, head) in enumerate(tiles):
        end = (block + 1) * BLOCK
        if step + ahead < len(tiles):
            waiting.append(score(*tiles[step + ahead]))
        scores = waiting.pop(0)
        row_max = jnp.max(scores, axis=0, keepdims=True)
        weights = jnp.exp(scores - row_max).astype(BF16)
        summed = dot_tn(weights, with_ones[:end])
        totals = summed[:, 128:]
        parts.append(summed[:, :128] / totals)
        l_ref[0, head : head + 1, block * BLOCK : end] = row_max + jnp.log(totals.T[0:1, :])
        if head == 1:
            o_ref[block * BLOCK : end, :] = jnp.where(low_lanes, parts[-2], parts[-1]).astype(BF16)


def columns(count, width):
    return pl.BlockSpec((count, width), lambda i, *_: (0, i))


def attend(value, weight, pairs, first):
    seq, dim = SEQ, value.shape[-1]
    group = 3 * 128
    tail = pl.BlockSpec((dim, 128), lambda i: (0, 3 * pairs))
    return pl.pallas_call(
        functools.partial(attend_kernel, first),
        grid=(pairs,),
        in_specs=[part_of(value, 0) if first else whole(seq, dim), columns(dim, group)]
        + ([tail] if first else []),
        out_specs=([whole(seq, dim)] if first else [])
        + [columns(seq, group), columns(seq, 128), pl.BlockSpec((1, 2, seq), lambda i: (i, 0, 0))]
        + ([whole(8, dim)] if first else []),
        out_shape=([shaped((seq, dim), BF16)] if first else [])
        + [shaped((seq, pairs * group), BF16), shaped((seq, pairs * 128), BF16)]
        + [shaped((pairs, 2, seq), F32)]
        + ([shaped((8, dim), F32)] if first else []),
        compiler_params=params(58),
        cost_estimate=cost(0.01),
    )(value, weight, *((weight,) if first else ()))


def attend_back_kernel(carry, final, *refs):
    mixed_ref, do_ref, o_ref, l_ref, low_ref, w_ref, *refs = refs
    if carry:
        grad_in, *refs = refs
    if final:
        x_ref, mid_ref, table_ref, norm_two, *refs = refs
    gq_ref, more_ref, *refs = refs
    if final:
        out_ref, norm_ref, *refs = refs
    else:
        grad_ref, *refs = refs
    sum_k, sum_v, both, every = refs
    q_ref, k_ref, v_ref = (mixed_ref.at[:, 128 * i : 128 * (i + 1)] for i in range(3))
    dq_ref, dk_ref, dv_ref = (both.at[:, 128 * i : 128 * (i + 1)] for i in range(3))
    seq = mixed_ref.shape[0]
    step = pl.program_id(0)
    low_lanes = lane_low(BLOCK)
    low_all = lane_low(seq)
    allowed = upper()
    scaling = jnp.asarray(HEAD_DIM**-0.5, BF16)
    head_keys = [keep_head(low_all, head, k_ref[...]) for head in range(2)]
    for block in reversed(range(seq // BLOCK)):
        start, end = block * BLOCK, (block + 1) * BLOCK
        queries = q_ref[start:end, :] * scaling
        grads = do_ref[start:end, :]
        dots = (grads.astype(F32) * o_ref[start:end, :].astype(F32)).T
        add_q = add_k = add_v = None
        for head in range(2):
            q_head = keep_head(low_lanes, head, queries)
            g_head = keep_head(low_lanes, head, grads)
            centre = jnp.sum(dots[HEAD_DIM * head : HEAD_DIM * (head + 1)], axis=0, keepdims=True)
            scores = dot_nt(k_ref[:end, :], q_head)
            probs = jnp.exp(scores - l_ref[0, head : head + 1, start:end])
            last = jnp.where(allowed, probs[start:, :], 0.0)
            probs = jnp.concatenate([probs[:start, :], last], axis=0) if block else last
            grad_probs = dot_nt(v_ref[:end, :], g_head)
            grad_scores = (probs * (grad_probs - centre)).astype(BF16)
            terms = (
                dot_tn(grad_scores, head_keys[head][:end]),
                dot_nn(grad_scores, q_head),
                dot_nn(probs.astype(BF16), g_head),
            )
            if head == 0:
                add_q, add_k, add_v = terms
            else:
                add_q, add_k, add_v = add_q + terms[0], add_k + terms[1], add_v + terms[2]
        dq_ref[start:end, :] = (add_q * HEAD_DIM**-0.5).astype(BF16)
        if end == seq:
            sum_k[...] = add_k
            sum_v[...] = add_v
        else:
            sum_k[:end, :] += add_k
            sum_v[:end, :] += add_v
    dk_ref[...] = sum_k[...].astype(BF16)
    dv_ref[...] = sum_v[...].astype(BF16)

    here = pl.ds(pl.multiple_of(step * 384, 384), 384)
    grad_qkv = dot_tn(low_ref[...], both[...]).astype(BF16)
    every[:, here] = both[...]

    @pl.when(step < pl.num_programs(0) - 1)
    def _():
        gq_ref[:, here] = grad_qkv

    @pl.when(step == pl.num_programs(0) - 1)
    def _():
        more_ref[:, :384] = grad_qkv


    @pl.when(step == pl.num_programs(0) - 1)
    def _():
        if final:
            norm_ref[...] = jnp.zeros_like(norm_ref)
        for start in range(0, seq, BLOCK):
            here = pl.ds(start, BLOCK)
            grad = dot_nt(every[here, :], w_ref[...])
            if carry:
                grad = grad + grad_in[here, :].astype(F32)
            if not final:
                grad_ref[here, :] = grad.astype(BF16)
                continue
            unit, inverse = normalise(x_ref[start // BLOCK, 0].astype(F32))
            norm_ref[0:1] += jnp.sum(grad * unit, axis=0, keepdims=True)
            norm_ref[1:2] += jnp.sum(grad, axis=0, keepdims=True)
            back = norm_back(unit, inverse, table_ref[0:1], grad)
            out_ref[here, :] = (mid_ref[here, :].astype(F32) + back).astype(BF16)
        tail = jnp.zeros((128, low_ref.shape[1]), F32)
        if final:
            tail = jnp.concatenate([norm_ref[:2], norm_two[:2], tail[4:]], axis=0)
        more_ref[:, 384:] = tail.T.astype(BF16)


def attend_back(mixed, grad, attended, logs, low, weight, start, pairs, carry=None, final=()):
    seq, dim = low.shape
    group = 3 * 128

    def column(width):
        return pl.BlockSpec((seq, width), lambda i: (0, start + i))

    more = [whole(seq, dim)] if carry is not None else []
    more += [part_of(final[0], 0), whole(seq, dim), whole(8, dim), whole(8, dim)] if final else []
    wide = pairs * group
    widths = [wide - group, group + 128]
    return pl.pallas_call(
        functools.partial(attend_back_kernel, carry is not None, bool(final)),
        grid=(pairs,),
        in_specs=[column(group), column(128), column(128)]
        + [pl.BlockSpec((1, 2, seq), lambda i: (start + i, 0, 0)), whole(seq, dim)]
        + [pl.BlockSpec((dim, wide), lambda i: (0, start // pairs))]
        + more,
        out_specs=[whole(dim, width) for width in widths]
        + [whole(seq, dim)]
        + ([whole(8, dim)] if final else []),
        out_shape=[shaped((dim, width), BF16) for width in widths]
        + [shaped((seq, dim), BF16)]
        + ([shaped((8, dim), F32)] if final else []),
        scratch_shapes=[pltpu.VMEM((seq, 128), F32)] * 2
        + [pltpu.VMEM((seq, group), BF16), pltpu.VMEM((seq, wide), BF16)],
        compiler_params=params(58),
        cost_estimate=cost(0.01),
    )(mixed, grad, attended, logs, low, weight, *(() if carry is None else (carry,)), *final)


def ffn_kernel(final, paired, *refs):
    low_ref, cot_ref, up_ref, down_ref, out_in = refs[:5]
    back_in = refs[5] if final else None
    out_ref, back_ref, gu_ref, gd_ref, out_sum, back_sum, act, hid = refs[5 + final :]

    def chunk(first):
        up, down = up_ref[...], down_ref[...]
        for start in range(0, low_ref.shape[0], BLOCK):
            here = pl.ds(start, BLOCK)
            hidden = dot_nn(low_ref[here, :], up)
            grad_active = dot_nt(cot_ref[start // BLOCK, 0], down)
            square = hidden * hidden
            bend = jnp.tanh(hidden * (GELU_A + (GELU_A * GELU_B) * square))
            gate = 0.5 + 0.5 * bend
            active = (hidden * gate).astype(BF16)
            slope = gate + hidden * (0.5 - 0.5 * bend * bend) * (
                GELU_A + (3 * GELU_A * GELU_B) * square
            )
            grad_hidden = (grad_active * slope).astype(BF16)
            act[here, :] = active
            hid[here, :] = grad_hidden
            add_out, add_back = dot_nn(active, down), dot_nt(grad_hidden, up)
            if first:
                out_sum[here, :] = add_out
                back_sum[here, :] = add_back
            else:
                total = out_sum[here, :] + add_out + out_in[here, :].astype(F32)
                out_ref[here, :] = total.astype(out_ref.dtype)
                total = back_sum[here, :] + add_back
                if final:
                    total = total + back_in[here, :].astype(F32)
                back_ref[here, :] = total.astype(BF16)
        gu_ref[...] = dot_tn(low_ref[...], hid[...]).astype(BF16)
        cot = cot_ref[...].reshape(act.shape[0], -1)
        grad_down = dot_tn(act[...], cot).astype(BF16)
        if paired:
            dim = grad_down.shape[1]
            grad_down = grad_down.reshape(-1, 2 * paired, dim)
            for side in range(2):
                gd_ref[:, side * dim : (side + 1) * dim] = grad_down[
                    :, side * paired : (side + 1) * paired
                ].reshape(-1, dim)
        else:
            gd_ref[...] = grad_down

    for place in range(2):

        @pl.when(pl.program_id(0) == place)
        def _(place=place):
            chunk(place == 0)


def feed_forward(low, pair, up, down, out_in, part, back_in=None):
    tok, dim = low.shape
    final = back_in is not None
    wide = down.shape[0]
    chunk = wide // 2
    paired = part if part % 16 == 0 else 0
    tall, long = (chunk // 2, 2 * dim) if paired else (chunk, dim)
    outs = pl.pallas_call(
        functools.partial(ffn_kernel, int(final), paired),
        grid=(2,),
        in_specs=[whole(tok, dim), part_of(pair, 1), columns(dim, chunk), rows(chunk, dim)]
        + [whole(tok, dim)] * (2 if final else 1),
        out_specs=[whole(tok, dim), whole(tok, dim), columns(dim, chunk), rows(tall, long)],
        out_shape=[shaped((tok, dim), BF16 if final else F32), shaped((tok, dim), BF16)]
        + [shaped((dim, wide), BF16), shaped((2 * tall, long), BF16)],
        scratch_shapes=[pltpu.VMEM((tok, dim), F32)] * 2 + [pltpu.VMEM((tok, chunk), BF16)] * 2,
        compiler_params=params(58),
        cost_estimate=cost(0.01),
    )(low, pair, up, down, out_in, *((back_in,) if final else ()))
    if paired:
        return outs
    grad_down = outs[3].reshape(-1, 2, part, dim).transpose(0, 2, 1, 3).reshape(-1, 2 * dim)
    return list(outs[:3]) + [grad_down]


def by_place(where_ref, refs):
    x, c = where_ref[0], where_ref[1]
    own, other_x, other_c, other_both = (ref[...].astype(F32) for ref in refs)
    low_x = [jnp.where(x == 0, own, other_x), jnp.where(x == 0, other_c, other_both)]
    high_x = [jnp.where(x == 0, other_x, own), jnp.where(x == 0, other_both, other_c)]
    return [
        [jnp.where(c == 0, side[0], side[1]) for side in (low_x, high_x)],
        [jnp.where(c == 0, side[1], side[0]) for side in (low_x, high_x)],
    ]


def finish_ffn(fan, where_ref, all_ref, up_ref, down_ref):
    part, dim = all_ref.shape[2], down_ref.shape[1]
    count = up_ref.shape[1] // fan // 2
    for core in range(2):
        for side in range(2):
            here = slice(side * part, (side + 1) * part)
            for block in range(count):
                place = (2 * block + core) * fan
                up_ref[here, place : place + fan] = all_ref[
                    core, side, :, block * fan : (block + 1) * fan
                ].astype(F32)
            start = count * fan
            for half in range(2):
                place = core * fan + side * fan // 2 + half * part
                down_ref[place : place + part, :] = all_ref[
                    core, side, :, start + half * dim : start + (half + 1) * dim
                ].astype(F32)


def finish_qkv(pairs, where_ref, *refs):
    pieces, (qkv_ref, proj_ref, *norm_refs) = by_place(where_ref, refs[:4]), refs[4:]
    part, dim = refs[0].shape[0], qkv_ref.shape[1] // 3
    sums = []
    for side in range(2):
        here = slice(side * part, (side + 1) * part)
        for core in range(2):
            piece = pieces[core][side]
            for pair in range(pairs):
                for which in range(3):
                    place = which * dim + core * dim // 2 + pair * 128
                    start = (pair * 3 + which) * 128
                    qkv_ref[here, place : place + 128] = piece[:, start : start + 128]
            start = pairs * 384 + 128
            proj_ref[here, core * dim // 2 : (core + 1) * dim // 2] = piece[:, start:]
        norms = slice(pairs * 384, pairs * 384 + 128)
        sums.append(pieces[0][side][:, norms] + pieces[1][side][:, norms])
    sums = jnp.concatenate(sums, axis=0).T
    for place, norm_ref in enumerate(norm_refs):
        norm_ref[...] = sums[place : place + 1].reshape(norm_ref.shape)


def finish(kernel, where, pieces, *shapes):
    return pl.pallas_call(
        kernel,
        grid_spec=pltpu.PrefetchScalarGridSpec(
            num_scalar_prefetch=1,
            grid=(1,),
            in_specs=[whole(*piece.shape) for piece in pieces],
            out_specs=[whole(*shape) for shape in shapes],
        ),
        out_shape=[shaped(shape, F32) for shape in shapes],
        compiler_params=params(58),
        cost_estimate=cost(0.01),
    )(where, *pieces)


class Grid:
    def __init__(self):
        self.z_count = lax.axis_size("dp") // 2
        self.dp, self.head = lax.axis_index("dp"), lax.axis_index("head")
        self.z, self.y, self.x, self.c = self.dp // 2, self.dp % 2, self.head // 2, self.head % 2
        assert lax.axis_size("head") == 4 and lax.axis_size("dp") % 2 == 0

    def send(self, value, z=0, y=0, x=0, c=0):
        pairs = []
        for source in range(self.z_count * 8):
            zi, yi, xi, ci = source // 8, source // 4 % 2, source // 2 % 2, source % 2
            zt, yt, xt, ct = (zi + z) % self.z_count, yi ^ y, xi ^ x, ci ^ c
            pairs.append((source, ((zt * 2 + yt) * 2 + xt) * 2 + ct))
        return lax.ppermute(value, BOTH, pairs)

    def pick(self, value, axis, index):
        return lax.dynamic_index_in_dim(value, index, axis, keepdims=False)

    def join(self, mine, other, index, axis):
        shape = mine.shape[:axis] + (2,) + mine.shape[axis:]
        here = lax.broadcasted_iota(jnp.int32, shape, axis) == index
        mine, other = (jnp.broadcast_to(jnp.expand_dims(v, axis), shape) for v in (mine, other))
        return jnp.where(here, mine, other)

    def to_z(self, piece):
        return [piece] + [self.send(piece, z=step) for step in range(1, self.z_count)]

    def by_z(self, got):
        shape = (self.z_count,) + got[0].shape
        steps = (self.z - lax.broadcasted_iota(jnp.int32, shape, 0)) % self.z_count
        out = jnp.broadcast_to(got[0], shape)
        for step in range(1, self.z_count):
            out = jnp.where(steps == step, jnp.broadcast_to(got[step], shape), out)
        return out

    def over_y(self, value, got):
        return self.join(value, got, self.y, 1)

    def over_x(self, value, got, axis):
        return self.join(value, got, self.x, axis)

    def halves(self, name, values):
        axis, index = (1, self.y) if name == "y" else (values[0].ndim - 3, self.x)
        low, high = (
            sum(lax.index_in_dim(v, place, axis, False).astype(F32) for v in values).astype(BF16)
            for place in range(2)
        )
        return jnp.where(index == 0, high, low), jnp.where(index == 0, low, high)

    def by_block(self, *values):
        totals = [keep.astype(F32) + got.astype(F32) for keep, got in values]
        return [
            jnp.concatenate(
                [self.pick(total, 0, (self.z + step) % self.z_count) for total in totals], axis=-1
            ).astype(BF16)
            for step in range(self.z_count)
        ]

    def end(self, parts):
        return self.total(
            [parts[0]] + [self.send(part, z=step) for step, part in enumerate(parts) if step]
        )

    def total(self, parts):
        return sum(value.astype(F32) for value in parts).astype(BF16)

    def share(self, piece):
        return [piece, self.send(piece, x=1), self.send(piece, c=1), self.send(piece, x=1, c=1)]

    def share_all(self, piece):
        both = self.join(piece, self.send(piece, x=1), self.x, 0)
        return self.join(both, self.send(both, c=1), self.c, 0)


def exchange(value):
    return lax.all_to_all(value, "head", split_axis=0, concat_axis=0, tiled=True)


def after(value, *done):
    return lax.optimization_barrier((value, done))[0]


def flat(value):
    return value.reshape(-1, value.shape[-1])


def local(
    tokens,
    qkv_weight,
    proj_weight,
    up_weight,
    down_weight,
    attn_gain,
    attn_bias,
    ffn_gain,
    ffn_bias,
    cotangent,
):
    grid = Grid()
    dim = tokens.shape[-1]
    share = qkv_weight.shape[0]
    part = share // 2
    half = dim // 2
    pairs = half // 128
    hidden = up_weight.shape[1]
    dp_count = lax.axis_size("dp")
    fan = hidden // dp_count // 2
    core = grid.c.reshape(1).astype(jnp.int32)
    assert tokens.shape[0] == 4 and tokens.shape[1] * 4 == SEQ
    assert fan == 4 * part

    def row_half(value):
        return lax.dynamic_slice_in_dim(value, grid.x * part, part, 0)

    qkv = grid.pick(qkv_weight.reshape(share, 3, 2, pairs, 128), 2, grid.c)
    qkv = qkv.transpose(0, 2, 1, 3).reshape(share, -1)
    table = jnp.stack([attn_gain, attn_bias, ffn_gain, ffn_bias], axis=1)
    table = jnp.pad(table, ((0, 0), (0, 124)))
    piece = jnp.concatenate([qkv, table], axis=1).astype(BF16)
    up = grid.pick(row_half(up_weight).reshape(part, dp_count, 2, fan), 2, grid.c)
    proj = grid.pick(row_half(proj_weight).reshape(part, 2, half), 1, grid.c)
    up_piece = jnp.concatenate([up.reshape(part, -1), proj], axis=1).astype(BF16)
    down_piece = grid.pick(down_weight.reshape(2, fan, dim), 0, grid.c).astype(BF16)
    where_head = jnp.stack([grid.x, grid.c]).astype(jnp.int32)

    both = exchange(after(jnp.stack([tokens, cotangent], axis=1), piece))
    first_z = grid.by_z(after(grid.to_z(piece), up_piece, down_piece))
    up_got = grid.to_z(after(up_piece, first_z))
    w_mine = flat(grid.over_y(first_z, after(grid.send(first_z, y=1), up_got)))
    w_theirs = grid.send(w_mine, c=1)
    up_z = grid.by_z(after(up_got, w_mine))
    up_y = grid.send(up_z, y=1)
    down_got = grid.to_z(after(down_piece, w_mine, both))

    up_x = grid.send(up_z, x=1)
    up_xy = grid.send(after(up_y, down_got), x=1)
    down_z = grid.by_z(after(down_got, up_z))
    down_y = grid.send(down_z, y=1)
    low, mixed_mine, att_mine, log_mine, table = attend(
        after(both, up_x, down_z), w_mine, pairs, True
    )
    mixed_theirs, att_theirs, log_theirs = attend(low, w_theirs, pairs, False)
    up_y = grid.over_y(up_z, up_y)
    up_x = grid.over_y(up_x, after(up_xy, att_theirs))
    up_mine = flat(grid.over_x(up_y, up_x, 2))
    up_theirs = grid.send(up_mine, c=1)
    down_mine = flat(grid.over_y(down_z, after(down_y, att_theirs)))
    down_theirs = grid.send(down_mine, c=1)
    middle, low_two = project(core, both, att_mine, att_theirs, up_mine, up_theirs, table)
    out, back, gu_mine, gd_mine = feed_forward(
        low_two, both, up_mine, after(down_mine, low_two), middle, part
    )
    out, back, gu_theirs, gd_theirs = feed_forward(
        low_two, both, up_theirs, after(down_theirs, back), out, part, back
    )

    def blocks(value):
        return value.reshape(grid.z_count, 2, 2, -1, value.shape[-1])

    gd_core, gu_core = grid.send(gd_theirs, c=1), grid.send(gu_theirs, c=1)
    gd_out, gd_keep = grid.halves("y", [blocks(gd_mine), blocks(gd_core)])
    gd_got = grid.send(gd_out, y=1)
    gu_out, gu_keep = grid.halves("x", [blocks(gu_mine), blocks(after(gu_core, gd_out))])
    gu_got = grid.send(gu_out, x=1)
    grad_middle, ga_mine, ga_theirs, gp_mine, gp_theirs, norm_two = middle_back(
        core, middle, after(back, gd_out, gu_out), both, table, up_mine, up_theirs, att_mine,
        att_theirs,
    )
    gp_core = grid.send(gp_theirs, c=1)
    gq_theirs, gq_rest, grad_low = attend_back(
        mixed_theirs, ga_theirs, att_theirs, log_theirs, low, w_theirs, 0, pairs
    )
    gq_core = [grid.send(value, c=1) for value in (gq_theirs, gq_rest)]
    gd_got, gu_got, gp_core = after((gd_got, gu_got, gp_core), grad_low)
    gd_out, gd_keep = grid.halves("x", [gd_keep, gd_got])
    gd_got = grid.send(gd_out, x=1)
    gu_out, gu_keep = grid.halves("y", [gu_keep, gu_got])
    gu_got = grid.send(gu_out, y=1)
    out_home = exchange(after(out.reshape(4, SEQ // 4, dim), gd_out, gu_out))
    gq_mine, gq_more, grad_x, _ = attend_back(
        mixed_mine, after(ga_mine, gd_out, gu_out, gq_core, gp_core), att_mine, log_mine, low,
        w_mine, 0, pairs, carry=grad_low, final=(both, grad_middle, table, norm_two),
    )
    gq_core, gd_got, gu_got = after((gq_core, gd_got, gu_got), gq_mine)
    left_out, left_keep = grid.halves(
        "x", [blocks(gq_mine), blocks(gq_core[0])]
    )
    left_got = grid.send(left_out, x=1)
    right_out, right_keep = grid.halves(
        "y",
        [
            jnp.concatenate([blocks(gq_more), blocks(gp_mine)], axis=-1),
            jnp.concatenate([blocks(gq_core[1]), blocks(gp_core)], axis=-1),
        ],
    )
    right_got = grid.send(right_out, y=1)
    gd_got, gu_got, out_home = after((gd_got, gu_got, out_home), left_out, right_out)
    ffn_parts = grid.by_block((gu_keep, gu_got), (gd_keep, gd_got))
    left_got, right_got = after((left_got, right_got), ffn_parts)
    ffn_got = [grid.send(part, z=step) for step, part in enumerate(ffn_parts) if step]
    left_out, left_keep = grid.halves("y", [left_keep, left_got])
    left_got = grid.send(left_out, y=1)
    right_out, right_keep = grid.halves("x", [right_keep, right_got])
    right_got = grid.send(right_out, x=1)
    grad_home = exchange(after(grad_x.reshape(4, SEQ // 4, dim), left_got))
    left_got, right_got = after((left_got, right_got), ffn_got)
    qkv_parts = grid.by_block((left_keep, left_got), (right_keep, right_got))
    sum_ffn = after(grid.total([ffn_parts[0], *ffn_got]), qkv_parts)
    ffn_x = grid.send(sum_ffn, x=1)
    qkv_got = [grid.send(part, z=step) for step, part in enumerate(qkv_parts) if step]
    qkv_got, grad_home = after((qkv_got, grad_home), grad_home)
    sum_qkv = grid.total([qkv_parts[0], *qkv_got])
    ffn_x = grid.join(sum_ffn, ffn_x, grid.x, 0)
    all_ffn = grid.join(ffn_x, grid.send(ffn_x, c=1), grid.c, 0)
    shares = grid.share(sum_qkv)
    grad_home = after(grad_home, sum_qkv).astype(F32)
    shard_up, shard_down = finish(
        functools.partial(finish_ffn, fan), where_head, [after(all_ffn, sum_qkv)],
        (share, hidden), (2 * fan, dim),
    )
    shard_qkv, shard_proj, *norms = finish(
        functools.partial(finish_qkv, pairs), where_head, after(shares, shard_up),
        (share, 3 * dim), (share, dim), *[(share,)] * 4,
    )
    return (
        out_home,
        grad_home,
        shard_qkv,
        shard_proj,
        shard_up,
        shard_down,
        norms[0],
        norms[1],
        norms[2],
        norms[3],
    )


def solution(mesh):
    spread = P("dp", "head", None)
    placed = (spread,) + (P("dp", None),) * 4 + (P("dp"),) * 4 + (spread,)
    return jax.shard_map(
        local,
        mesh=mesh,
        in_specs=placed,
        out_specs=(spread, spread) + (P("dp", None),) * 4 + (P("dp"),) * 4,
        check_vma=False,
    )
```

```python
import functools

import jax
import jax.numpy as jnp
from jax import lax
from jax.experimental import pallas as pl
from jax.experimental.pallas import tpu as pltpu
from jax.sharding import PartitionSpec as P

HEADS = 12
HEAD_DIM = 64
SEQ = 1024
EPSILON = 1e-05
BOTH = ("dp", "head")
BLOCK = 256
GELU_A = 0.7978845608028654
GELU_B = 0.044715
F32 = jnp.float32
BF16 = jnp.bfloat16


def params(mebi):
    return pltpu.CompilerParams(vmem_limit_bytes=mebi * 2**20)


def dot_nn(left, right):
    return lax.dot_general(left, right, (((1,), (0,)), ((), ())), preferred_element_type=F32)


def dot_nt(left, right):
    return lax.dot_general(left, right, (((1,), (1,)), ((), ())), preferred_element_type=F32)


def dot_tn(left, right):
    return lax.dot_general(left, right, (((0,), (0,)), ((), ())), preferred_element_type=F32)


def cost(micros):
    return pl.CostEstimate(
        flops=int(micros * 1.1e9), bytes_accessed=int(micros * 3e6), transcendentals=0
    )


def whole(*shape):
    return pl.BlockSpec(shape, lambda *_: (0,) * len(shape))


def part_of(pair, which):
    parts, _, count, dim = pair.shape
    return pl.BlockSpec((parts, 1, count, dim), lambda *_: (0, which, 0, 0))


def part_rows(pair, which):
    _, _, count, dim = pair.shape
    return pl.BlockSpec((1, 1, count, dim), lambda i, *_: (i, which, 0, 0))


def rows(count, width):
    return pl.BlockSpec((count, width), lambda i, *_: (i, 0))


def shaped(shape, dtype):
    return jax.ShapeDtypeStruct(shape, dtype)


def normalise(vector):
    centred = vector - jnp.mean(vector, axis=-1, keepdims=True)
    inverse = lax.rsqrt(jnp.mean(centred * centred, axis=-1, keepdims=True) + EPSILON)
    return centred * inverse, inverse


def norm_back(unit, inverse, gain, grad):
    scaled = grad * gain
    return inverse * (
        scaled
        - jnp.mean(scaled, axis=-1, keepdims=True)
        - unit * jnp.mean(scaled * unit, axis=-1, keepdims=True)
    )


def proj_kernel(core_ref, x_ref, am_ref, at_ref, pm_ref, pt_ref, table_ref, mid_ref, low_ref, total):
    half = am_ref.shape[1]
    mine = pl.multiple_of(core_ref[0] * half, half)
    theirs = pl.multiple_of((1 - core_ref[0]) * half, half)
    a_mine, a_theirs = am_ref[...], at_ref[...]
    for place, weight in ((mine, pm_ref), (theirs, pt_ref)):
        total[:, pl.ds(place, half)] = (
            x_ref[0, 0, :, pl.ds(place, half)].astype(F32)
            + dot_nn(a_mine, weight[pl.ds(mine, half), :])
            + dot_nn(a_theirs, weight[pl.ds(theirs, half), :])
        )
    mid_ref[...] = total[...].astype(BF16)
    unit, _ = normalise(total[...])
    low_ref[...] = (unit * table_ref[2:3] + table_ref[3:4]).astype(BF16)


def proj_spec(dim):
    half = dim // 2
    return pl.BlockSpec((dim, half), lambda i, *_: (0, 4))


def project(core, x, a_mine, a_theirs, w_mine, w_theirs, table):
    tok, dim = SEQ, x.shape[-1]
    half = dim // 2
    return pl.pallas_call(
        proj_kernel,
        grid_spec=pltpu.PrefetchScalarGridSpec(
            num_scalar_prefetch=1,
            grid=(tok // BLOCK,),
            in_specs=[part_rows(x, 0), rows(BLOCK, half), rows(BLOCK, half)]
            + [proj_spec(dim), proj_spec(dim), whole(8, dim)],
            out_specs=[rows(BLOCK, dim), rows(BLOCK, dim)],
            scratch_shapes=[pltpu.VMEM((BLOCK, dim), F32)],
        ),
        out_shape=[shaped((tok, dim), BF16), shaped((tok, dim), BF16)],
        compiler_params=params(58),
        cost_estimate=cost(0.01),
    )(core, x, a_mine, a_theirs, w_mine, w_theirs, table)


def middle_kernel(
    core_ref, mid_ref, back_ref, cot_ref, table_ref, pm_ref, pt_ref, am_ref, at_ref,
    grad_ref, gm_ref, gt_ref, wm_ref, wt_ref, norm_ref, heads, branch,
):
    half = am_ref.shape[1]
    step = pl.program_id(0)
    mine = pl.multiple_of(core_ref[0] * half, half)
    theirs = pl.multiple_of((1 - core_ref[0]) * half, half)
    here = pl.ds(pl.multiple_of(step * BLOCK, BLOCK), BLOCK)

    @pl.when(step == 0)
    def _():
        norm_ref[...] = jnp.zeros_like(norm_ref)

    unit, inverse = normalise(mid_ref[...].astype(F32))
    grad = back_ref[...].astype(F32)
    norm_ref[0:1] += jnp.sum(grad * unit, axis=0, keepdims=True)
    norm_ref[1:2] += jnp.sum(grad, axis=0, keepdims=True)
    back = norm_back(unit, inverse, table_ref[2:3], grad)
    grad_ref[...] = (cot_ref[0, 0].astype(F32) + back).astype(BF16)
    branch[here, :half] = grad_ref[:, pl.ds(mine, half)]
    branch[here, half:] = grad_ref[:, pl.ds(theirs, half)]
    heads[here, :half] = am_ref[...]
    heads[here, half:] = at_ref[...]
    for place, out in ((mine, gm_ref), (theirs, gt_ref)):
        out[...] = (
            dot_nt(branch[here, :half], pm_ref[pl.ds(place, half), :])
            + dot_nt(branch[here, half:], pt_ref[pl.ds(place, half), :])
        ).astype(BF16)

    @pl.when(step == pl.num_programs(0) - 1)
    def _():
        for place, start in ((mine, 0), (theirs, half)):
            total = dot_tn(heads[:, start : start + half], branch[...]).astype(BF16)
            wm_ref[pl.ds(place, half), :] = total[:, :half]
            wt_ref[pl.ds(place, half), :] = total[:, half:]


def middle_back(core, middle, back, cot, table, w_mine, w_theirs, a_mine, a_theirs):
    tok, dim = middle.shape
    half = dim // 2
    return pl.pallas_call(
        middle_kernel,
        grid_spec=pltpu.PrefetchScalarGridSpec(
            num_scalar_prefetch=1,
            grid=(tok // BLOCK,),
            in_specs=[rows(BLOCK, dim), rows(BLOCK, dim), part_rows(cot, 1)]
            + [whole(8, dim), proj_spec(dim), proj_spec(dim)]
            + [rows(BLOCK, half)] * 2,
            out_specs=[rows(BLOCK, dim), rows(BLOCK, half), rows(BLOCK, half)]
            + [whole(dim, half), whole(dim, half), whole(8, dim)],
            scratch_shapes=[pltpu.VMEM((tok, dim), BF16)] * 2,
        ),
        out_shape=[shaped((tok, dim), BF16)]
        + [shaped((tok, half), BF16)] * 2
        + [shaped((dim, half), BF16)] * 2
        + [shaped((8, dim), F32)],
        compiler_params=params(58),
        cost_estimate=cost(0.01),
    )(core, middle, back, cot, table, w_mine, w_theirs, a_mine, a_theirs)


def lane_low(count):
    return lax.broadcasted_iota(jnp.int32, (count, 128), 1) < HEAD_DIM


def upper():
    return lax.broadcasted_iota(jnp.int32, (BLOCK, BLOCK), 0) <= lax.broadcasted_iota(
        jnp.int32, (BLOCK, BLOCK), 1
    )


def keep_head(low_lanes, head, value):
    zero = jnp.zeros((), value.dtype)
    return jnp.where(low_lanes, value, zero) if head == 0 else jnp.where(low_lanes, zero, value)


def attend_kernel(first, *refs):
    if first:
        x_ref, w_ref, tail_ref, low_ref, mixed_ref, o_ref, l_ref, table_ref = refs
    else:
        low_ref, w_ref, mixed_ref, o_ref, l_ref = refs
    seq = mixed_ref.shape[0]

    if first:

        @pl.when(pl.program_id(0) == 0)
        def _():
            table_ref[...] = tail_ref[...].astype(F32).T[:8]
            for start in range(0, seq, BLOCK):
                here = pl.ds(start, BLOCK)
                unit, _ = normalise(x_ref[start // BLOCK, 0].astype(F32))
                low_ref[here, :] = (unit * table_ref[0:1] + table_ref[1:2]).astype(BF16)

    mixed_ref[...] = dot_nn(low_ref[...], w_ref[...]).astype(BF16)
    q_ref, k_ref, v_ref = (mixed_ref.at[:, 128 * i : 128 * (i + 1)] for i in range(3))
    low_lanes = lane_low(BLOCK)
    allowed = upper()
    scaling = jnp.asarray(HEAD_DIM**-0.5, BF16)
    tiles = [(block, head) for block in range(seq // BLOCK) for head in range(2)]
    with_ones = jnp.concatenate([v_ref[...], jnp.ones((seq, 128), BF16)], axis=1)

    def score(block, head):
        end = (block + 1) * BLOCK
        queries = keep_head(low_lanes, head, q_ref[block * BLOCK : end, :] * scaling)
        raw = dot_nt(k_ref[:end, :], queries)
        last = jnp.where(allowed, raw[end - BLOCK :, :], -1e30)
        return jnp.concatenate([raw[: end - BLOCK, :], last], axis=0) if block else last

    ahead = 3
    waiting = [score(*tile) for tile in tiles[:ahead]]
    parts = []
    for step, (block, head) in enumerate(tiles):
        end = (block + 1) * BLOCK
        if step + ahead < len(tiles):
            waiting.append(score(*tiles[step + ahead]))
        scores = waiting.pop(0)
        row_max = jnp.max(scores, axis=0, keepdims=True)
        weights = jnp.exp(scores - row_max).astype(BF16)
        summed = dot_tn(weights, with_ones[:end])
        totals = summed[:, 128:]
        parts.append(summed[:, :128] / totals)
        l_ref[0, head : head + 1, block * BLOCK : end] = row_max + jnp.log(totals.T[0:1, :])
        if head == 1:
            o_ref[block * BLOCK : end, :] = jnp.where(low_lanes, parts[-2], parts[-1]).astype(BF16)


def columns(count, width):
    return pl.BlockSpec((count, width), lambda i, *_: (0, i))


def attend(value, weight, pairs, first):
    seq, dim = SEQ, value.shape[-1]
    group = 3 * 128
    tail = pl.BlockSpec((dim, 128), lambda i: (0, 3 * pairs))
    return pl.pallas_call(
        functools.partial(attend_kernel, first),
        grid=(pairs,),
        in_specs=[part_of(value, 0) if first else whole(seq, dim), columns(dim, group)]
        + ([tail] if first else []),
        out_specs=([whole(seq, dim)] if first else [])
        + [columns(seq, group), columns(seq, 128), pl.BlockSpec((1, 2, seq), lambda i: (i, 0, 0))]
        + ([whole(8, dim)] if first else []),
        out_shape=([shaped((seq, dim), BF16)] if first else [])
        + [shaped((seq, pairs * group), BF16), shaped((seq, pairs * 128), BF16)]
        + [shaped((pairs, 2, seq), F32)]
        + ([shaped((8, dim), F32)] if first else []),
        compiler_params=params(58),
        cost_estimate=cost(0.01),
    )(value, weight, *((weight,) if first else ()))


def attend_back_kernel(carry, final, part, *refs):
    if part:
        where_ref, *refs = refs
    mixed_ref, do_ref, o_ref, l_ref, low_ref, w_ref, *refs = refs
    if carry:
        grad_in, *refs = refs
    if final:
        x_ref, mid_ref, table_ref, norm_two, *refs = refs
    if part:
        core_ref, core_more, gp_ref, gp_core, *refs = refs
        left_out, left_keep, right_out, right_keep, *refs = refs
    else:
        gq_ref, more_ref, *refs = refs
    if final:
        out_ref, norm_ref, *refs = refs
    else:
        grad_ref, *refs = refs
    sum_k, sum_v, both, every, *sums = refs
    q_ref, k_ref, v_ref = (mixed_ref.at[:, 128 * i : 128 * (i + 1)] for i in range(3))
    dq_ref, dk_ref, dv_ref = (both.at[:, 128 * i : 128 * (i + 1)] for i in range(3))
    seq = mixed_ref.shape[0]
    step = pl.program_id(0)
    low_lanes = lane_low(BLOCK)
    low_all = lane_low(seq)
    allowed = upper()
    scaling = jnp.asarray(HEAD_DIM**-0.5, BF16)
    head_keys = [keep_head(low_all, head, k_ref[...]) for head in range(2)]
    for block in reversed(range(seq // BLOCK)):
        start, end = block * BLOCK, (block + 1) * BLOCK
        queries = q_ref[start:end, :] * scaling
        grads = do_ref[start:end, :]
        dots = (grads.astype(F32) * o_ref[start:end, :].astype(F32)).T
        add_q = add_k = add_v = None
        for head in range(2):
            q_head = keep_head(low_lanes, head, queries)
            g_head = keep_head(low_lanes, head, grads)
            centre = jnp.sum(dots[HEAD_DIM * head : HEAD_DIM * (head + 1)], axis=0, keepdims=True)
            scores = dot_nt(k_ref[:end, :], q_head)
            probs = jnp.exp(scores - l_ref[0, head : head + 1, start:end])
            last = jnp.where(allowed, probs[start:, :], 0.0)
            probs = jnp.concatenate([probs[:start, :], last], axis=0) if block else last
            grad_probs = dot_nt(v_ref[:end, :], g_head)
            grad_scores = (probs * (grad_probs - centre)).astype(BF16)
            terms = (
                dot_tn(grad_scores, head_keys[head][:end]),
                dot_nn(grad_scores, q_head),
                dot_nn(probs.astype(BF16), g_head),
            )
            if head == 0:
                add_q, add_k, add_v = terms
            else:
                add_q, add_k, add_v = add_q + terms[0], add_k + terms[1], add_v + terms[2]
        dq_ref[start:end, :] = (add_q * HEAD_DIM**-0.5).astype(BF16)
        if end == seq:
            sum_k[...] = add_k
            sum_v[...] = add_v
        else:
            sum_k[:end, :] += add_k
            sum_v[:end, :] += add_v
    dk_ref[...] = sum_k[...].astype(BF16)
    dv_ref[...] = sum_v[...].astype(BF16)

    here = pl.ds(pl.multiple_of(step * 384, 384), 384)
    grad_qkv = dot_tn(low_ref[...], both[...]).astype(BF16)
    every[:, here] = both[...]

    def cut(out, keep, columns, source, size, index):
        for block in range(source.shape[0] // (2 * size)):
            to = pl.ds(block * size, size)
            for ref, side in ((out, 1 - index), (keep, index)):
                start = pl.multiple_of(block * 2 * size + side * size, 16)
                ref[to, columns] = source[pl.ds(start, size), :]

    @pl.when(step < pl.num_programs(0) - 1)
    def _():
        if part:
            sums[0][...] = (grad_qkv.astype(F32) + core_ref[:, here].astype(F32)).astype(BF16)
            cut(left_out, left_keep, here, sums[0], part, where_ref[0])
        else:
            gq_ref[:, here] = grad_qkv

    @pl.when(step == pl.num_programs(0) - 1)
    def _():
        if part:
            sums[1][:, :384] = (
                grad_qkv.astype(F32) + core_more[:, :384].astype(F32)
            ).astype(BF16)
        else:
            more_ref[:, :384] = grad_qkv


    @pl.when(step == pl.num_programs(0) - 1)
    def _():
        if final:
            norm_ref[...] = jnp.zeros_like(norm_ref)
        for start in range(0, seq, BLOCK):
            here = pl.ds(start, BLOCK)
            grad = dot_nt(every[here, :], w_ref[...])
            if carry:
                grad = grad + grad_in[here, :].astype(F32)
            if not final:
                grad_ref[here, :] = grad.astype(BF16)
                continue
            unit, inverse = normalise(x_ref[start // BLOCK, 0].astype(F32))
            norm_ref[0:1] += jnp.sum(grad * unit, axis=0, keepdims=True)
            norm_ref[1:2] += jnp.sum(grad, axis=0, keepdims=True)
            back = norm_back(unit, inverse, table_ref[0:1], grad)
            out_ref[here, :] = (mid_ref[here, :].astype(F32) + back).astype(BF16)
        tail = jnp.zeros((128, low_ref.shape[1]), F32)
        if final:
            tail = jnp.concatenate([norm_ref[:2], norm_two[:2], tail[4:]], axis=0)
        if part:
            sums[1][:, 384:512] = (tail.T + core_more[:, 384:].astype(F32)).astype(BF16)
            sums[1][:, 512:] = (gp_ref[...].astype(F32) + gp_core[...].astype(F32)).astype(BF16)
            cut(right_out, right_keep, slice(None), sums[1], 2 * part, where_ref[1])
        else:
            more_ref[:, 384:] = tail.T.astype(BF16)


def attend_back(
    mixed, grad, attended, logs, low, weight, pairs, carry=None, final=(), where=None, others=(), part=0
):
    seq, dim = low.shape
    group = 3 * 128
    wide = pairs * group

    def column(width):
        return pl.BlockSpec((seq, width), lambda i, *_: (0, i))

    more = [whole(seq, dim)] if carry is not None else []
    more += [part_of(final[0], 0), whole(seq, dim), whole(8, dim), whole(8, dim)] if final else []
    more += [whole(*other.shape) for other in others]
    widths = [wide - group, group + 128]
    outs = [(dim, width) for width in widths]
    scratch = [pltpu.VMEM((seq, 128), F32)] * 2
    scratch += [pltpu.VMEM((seq, group), BF16), pltpu.VMEM((seq, wide), BF16)]
    if part:
        widths[1] += others[2].shape[1]
        outs = [(dim // 2, width) for width in widths for _ in range(2)]
        scratch += [pltpu.VMEM((dim, group), BF16), pltpu.VMEM((dim, widths[1]), BF16)]
    return pl.pallas_call(
        functools.partial(attend_back_kernel, carry is not None, bool(final), part),
        grid_spec=pltpu.PrefetchScalarGridSpec(
            num_scalar_prefetch=1 if part else 0,
            grid=(pairs,),
            in_specs=[column(group), column(128), column(128)]
            + [pl.BlockSpec((1, 2, seq), lambda i, *_: (i, 0, 0)), whole(seq, dim)]
            + [whole(dim, wide)]
            + more,
            out_specs=[whole(*shape) for shape in outs]
            + [whole(seq, dim)]
            + ([whole(8, dim)] if final else []),
            scratch_shapes=scratch,
        ),
        out_shape=[shaped(shape, BF16) for shape in outs]
        + [shaped((seq, dim), BF16)]
        + ([shaped((8, dim), F32)] if final else []),
        compiler_params=params(58),
        cost_estimate=cost(0.01),
    )(
        *((where,) if part else ()),
        mixed,
        grad,
        attended,
        logs,
        low,
        weight,
        *(() if carry is None else (carry,)),
        *final,
        *others,
    )


def ffn_kernel(final, paired, *refs):
    low_ref, cot_ref, up_ref, down_ref, out_in = refs[:5]
    back_in = refs[5] if final else None
    out_ref, back_ref, gu_ref, gd_ref, out_sum, back_sum, act, hid = refs[5 + final :]

    def chunk(first):
        up, down = up_ref[...], down_ref[...]
        for start in range(0, low_ref.shape[0], BLOCK):
            here = pl.ds(start, BLOCK)
            hidden = dot_nn(low_ref[here, :], up)
            grad_active = dot_nt(cot_ref[start // BLOCK, 0], down)
            square = hidden * hidden
            bend = jnp.tanh(hidden * (GELU_A + (GELU_A * GELU_B) * square))
            gate = 0.5 + 0.5 * bend
            active = (hidden * gate).astype(BF16)
            slope = gate + hidden * (0.5 - 0.5 * bend * bend) * (
                GELU_A + (3 * GELU_A * GELU_B) * square
            )
            grad_hidden = (grad_active * slope).astype(BF16)
            act[here, :] = active
            hid[here, :] = grad_hidden
            add_out, add_back = dot_nn(active, down), dot_nt(grad_hidden, up)
            if first:
                out_sum[here, :] = add_out
                back_sum[here, :] = add_back
            else:
                total = out_sum[here, :] + add_out + out_in[here, :].astype(F32)
                out_ref[here, :] = total.astype(out_ref.dtype)
                total = back_sum[here, :] + add_back
                if final:
                    total = total + back_in[here, :].astype(F32)
                back_ref[here, :] = total.astype(BF16)
        gu_ref[...] = dot_tn(low_ref[...], hid[...]).astype(BF16)
        cot = cot_ref[...].reshape(act.shape[0], -1)
        grad_down = dot_tn(act[...], cot).astype(BF16)
        if paired:
            dim = grad_down.shape[1]
            grad_down = grad_down.reshape(-1, 2 * paired, dim)
            for side in range(2):
                gd_ref[:, side * dim : (side + 1) * dim] = grad_down[
                    :, side * paired : (side + 1) * paired
                ].reshape(-1, dim)
        else:
            gd_ref[...] = grad_down

    for place in range(2):

        @pl.when(pl.program_id(0) == place)
        def _(place=place):
            chunk(place == 0)


def feed_forward(low, pair, up, down, out_in, part, back_in=None):
    tok, dim = low.shape
    final = back_in is not None
    wide = down.shape[0]
    chunk = wide // 2
    paired = part if part % 16 == 0 else 0
    tall, long = (chunk // 2, 2 * dim) if paired else (chunk, dim)
    outs = pl.pallas_call(
        functools.partial(ffn_kernel, int(final), paired),
        grid=(2,),
        in_specs=[whole(tok, dim), part_of(pair, 1), columns(dim, chunk), rows(chunk, dim)]
        + [whole(tok, dim)] * (2 if final else 1),
        out_specs=[whole(tok, dim), whole(tok, dim), columns(dim, chunk), rows(tall, long)],
        out_shape=[shaped((tok, dim), BF16 if final else F32), shaped((tok, dim), BF16)]
        + [shaped((dim, wide), BF16), shaped((2 * tall, long), BF16)],
        scratch_shapes=[pltpu.VMEM((tok, dim), F32)] * 2 + [pltpu.VMEM((tok, chunk), BF16)] * 2,
        compiler_params=params(58),
        cost_estimate=cost(0.01),
    )(low, pair, up, down, out_in, *((back_in,) if final else ()))
    if paired:
        return outs
    grad_down = outs[3].reshape(-1, 2, part, dim).transpose(0, 2, 1, 3).reshape(-1, 2 * dim)
    return list(outs[:3]) + [grad_down]


def by_place(where_ref, refs):
    x, c = where_ref[0], where_ref[1]
    own, other_x, other_c, other_both = (ref[...].astype(F32) for ref in refs)
    low_x = [jnp.where(x == 0, own, other_x), jnp.where(x == 0, other_c, other_both)]
    high_x = [jnp.where(x == 0, other_x, own), jnp.where(x == 0, other_both, other_c)]
    return [
        [jnp.where(c == 0, side[0], side[1]) for side in (low_x, high_x)],
        [jnp.where(c == 0, side[1], side[0]) for side in (low_x, high_x)],
    ]


def finish_ffn(fan, where_ref, all_ref, up_ref, down_ref):
    part, dim = all_ref.shape[2], down_ref.shape[1]
    count = up_ref.shape[1] // fan // 2
    for core in range(2):
        for side in range(2):
            here = slice(side * part, (side + 1) * part)
            for block in range(count):
                place = (2 * block + core) * fan
                up_ref[here, place : place + fan] = all_ref[
                    core, side, :, block * fan : (block + 1) * fan
                ].astype(F32)
            start = count * fan
            for half in range(2):
                place = core * fan + side * fan // 2 + half * part
                down_ref[place : place + part, :] = all_ref[
                    core, side, :, start + half * dim : start + (half + 1) * dim
                ].astype(F32)


def finish_qkv(pairs, where_ref, *refs):
    pieces, (qkv_ref, proj_ref, *norm_refs) = by_place(where_ref, refs[:4]), refs[4:]
    part, dim = refs[0].shape[0], qkv_ref.shape[1] // 3
    sums = []
    for side in range(2):
        here = slice(side * part, (side + 1) * part)
        for core in range(2):
            piece = pieces[core][side]
            for pair in range(pairs):
                for which in range(3):
                    place = which * dim + core * dim // 2 + pair * 128
                    start = (pair * 3 + which) * 128
                    qkv_ref[here, place : place + 128] = piece[:, start : start + 128]
            start = pairs * 384 + 128
            proj_ref[here, core * dim // 2 : (core + 1) * dim // 2] = piece[:, start:]
        norms = slice(pairs * 384, pairs * 384 + 128)
        sums.append(pieces[0][side][:, norms] + pieces[1][side][:, norms])
    sums = jnp.concatenate(sums, axis=0).T
    for place, norm_ref in enumerate(norm_refs):
        norm_ref[...] = sums[place : place + 1].reshape(norm_ref.shape)


def settle_kernel(in_ref, out_ref):
    out_ref[...] = in_ref[...]


def settle(value):
    spec = pl.BlockSpec((1,) + value.shape[1:], lambda i: (i, 0, 0))
    return pl.pallas_call(
        settle_kernel,
        grid=value.shape[:1],
        in_specs=[spec],
        out_specs=spec,
        out_shape=shaped(value.shape, value.dtype),
        cost_estimate=cost(0.01),
    )(value)


def finish(kernel, where, pieces, *shapes):
    return pl.pallas_call(
        kernel,
        grid_spec=pltpu.PrefetchScalarGridSpec(
            num_scalar_prefetch=1,
            grid=(1,),
            in_specs=[whole(*piece.shape) for piece in pieces],
            out_specs=[whole(*shape) for shape in shapes],
        ),
        out_shape=[shaped(shape, F32) for shape in shapes],
        compiler_params=params(58),
        cost_estimate=cost(0.01),
    )(where, *pieces)


class Grid:
    def __init__(self):
        self.z_count = lax.axis_size("dp") // 2
        self.dp, self.head = lax.axis_index("dp"), lax.axis_index("head")
        self.z, self.y, self.x, self.c = self.dp // 2, self.dp % 2, self.head // 2, self.head % 2
        assert lax.axis_size("head") == 4 and lax.axis_size("dp") % 2 == 0

    def send(self, value, z=0, y=0, x=0, c=0):
        pairs = []
        for source in range(self.z_count * 8):
            zi, yi, xi, ci = source // 8, source // 4 % 2, source // 2 % 2, source % 2
            zt, yt, xt, ct = (zi + z) % self.z_count, yi ^ y, xi ^ x, ci ^ c
            pairs.append((source, ((zt * 2 + yt) * 2 + xt) * 2 + ct))
        return lax.ppermute(value, BOTH, pairs)

    def pick(self, value, axis, index):
        return lax.dynamic_index_in_dim(value, index, axis, keepdims=False)

    def join(self, mine, other, index, axis):
        shape = mine.shape[:axis] + (2,) + mine.shape[axis:]
        here = lax.broadcasted_iota(jnp.int32, shape, axis) == index
        mine, other = (jnp.broadcast_to(jnp.expand_dims(v, axis), shape) for v in (mine, other))
        return jnp.where(here, mine, other)

    def to_z(self, piece):
        return [piece] + [self.send(piece, z=step) for step in range(1, self.z_count)]

    def by_z(self, got):
        shape = (self.z_count,) + got[0].shape
        steps = (self.z - lax.broadcasted_iota(jnp.int32, shape, 0)) % self.z_count
        out = jnp.broadcast_to(got[0], shape)
        for step in range(1, self.z_count):
            out = jnp.where(steps == step, jnp.broadcast_to(got[step], shape), out)
        return out

    def over_z(self, piece):
        copies = jnp.broadcast_to(piece, (self.z_count,) + piece.shape)
        groups = [list(range(y, self.z_count * 2, 2)) for y in range(2)]
        return lax.all_to_all(
            copies, "dp", split_axis=0, concat_axis=0, tiled=True, axis_index_groups=groups
        )

    def over_y(self, value, got):
        return self.join(value, got, self.y, 1)

    def over_x(self, value, got, axis):
        return self.join(value, got, self.x, axis)

    def halves(self, name, values):
        axis, index = (1, self.y) if name == "y" else (values[0].ndim - 3, self.x)
        low, high = (
            sum(lax.index_in_dim(v, place, axis, False).astype(F32) for v in values).astype(BF16)
            for place in range(2)
        )
        return jnp.where(index == 0, high, low), jnp.where(index == 0, low, high)

    def by_block(self, *values):
        totals = [keep.astype(F32) + got.astype(F32) for keep, got in values]
        return [
            jnp.concatenate(
                [self.pick(total, 0, (self.z + step) % self.z_count) for total in totals], axis=-1
            ).astype(BF16)
            for step in range(self.z_count)
        ]

    def end(self, parts):
        return self.total(
            [parts[0]] + [self.send(part, z=step) for step, part in enumerate(parts) if step]
        )

    def total(self, parts):
        return sum(value.astype(F32) for value in parts).astype(BF16)

    def share(self, piece):
        return [piece, self.send(piece, x=1), self.send(piece, c=1), self.send(piece, x=1, c=1)]

    def share_all(self, piece):
        both = self.join(piece, self.send(piece, x=1), self.x, 0)
        return self.join(both, self.send(both, c=1), self.c, 0)


def exchange(value):
    return lax.all_to_all(value, "head", split_axis=0, concat_axis=0, tiled=True)


def after(value, *done):
    return lax.optimization_barrier((value, done))[0]


def flat(value):
    return value.reshape(-1, value.shape[-1])


def local(
    tokens,
    qkv_weight,
    proj_weight,
    up_weight,
    down_weight,
    attn_gain,
    attn_bias,
    ffn_gain,
    ffn_bias,
    cotangent,
):
    grid = Grid()
    dim = tokens.shape[-1]
    share = qkv_weight.shape[0]
    part = share // 2
    half = dim // 2
    pairs = half // 128
    hidden = up_weight.shape[1]
    dp_count = lax.axis_size("dp")
    fan = hidden // dp_count // 2
    core = grid.c.reshape(1).astype(jnp.int32)
    assert tokens.shape[0] == 4 and tokens.shape[1] * 4 == SEQ
    assert fan == 4 * part

    def row_half(value):
        return lax.dynamic_slice_in_dim(value, grid.x * part, part, 0)

    qkv = grid.pick(qkv_weight.reshape(share, 3, 2, pairs, 128), 2, grid.c)
    qkv = qkv.transpose(0, 2, 1, 3).reshape(share, -1)
    table = jnp.stack([attn_gain, attn_bias, ffn_gain, ffn_bias], axis=1)
    table = jnp.pad(table, ((0, 0), (0, 124)))
    piece = jnp.concatenate([qkv, table], axis=1).astype(BF16)
    up = grid.pick(row_half(up_weight).reshape(part, dp_count, 2, fan), 2, grid.c)
    proj = grid.pick(row_half(proj_weight).reshape(part, 2, half), 1, grid.c)
    up_piece = jnp.concatenate([up.reshape(part, -1), proj], axis=1).astype(BF16)
    down_piece = grid.pick(down_weight.reshape(2, fan, dim), 0, grid.c).astype(BF16)
    where = jnp.stack([grid.x, grid.y]).astype(jnp.int32)
    where_head = jnp.stack([grid.x, grid.c]).astype(jnp.int32)

    both = exchange(after(jnp.stack([tokens, cotangent], axis=1), piece))
    first_z = grid.by_z(after(grid.to_z(piece), up_piece, down_piece))
    up_got = grid.to_z(after(up_piece, first_z))
    w_mine = flat(grid.over_y(first_z, after(grid.send(first_z, y=1), up_got)))
    w_theirs = grid.send(w_mine, c=1)
    up_z = grid.by_z(after(up_got, w_mine))
    up_y = grid.send(up_z, y=1)
    up_x = grid.send(up_z, x=1)
    down_both = grid.join(
        down_piece, grid.send(after(down_piece, up_got), y=1), grid.y, 0
    )
    down_mine = grid.over_z(after(down_both, both))
    low, mixed_mine, att_mine, log_mine, table = attend(
        after(both, up_z), w_mine, pairs, True
    )
    mixed_theirs, att_theirs, log_theirs = attend(low, w_theirs, pairs, False)
    up_y, up_x = after((up_y, up_x), att_mine, att_theirs)
    up_xy = grid.send(up_y, x=1)
    up_y = grid.over_y(up_z, up_y)
    up_x = grid.over_y(up_x, up_xy)
    up_mine = flat(grid.over_x(up_y, up_x, 2))
    up_theirs = grid.send(up_mine, c=1)
    down_mine = flat(after(down_mine, up_xy))
    down_theirs = grid.send(down_mine, c=1)
    middle, low_two = project(core, both, att_mine, att_theirs, up_mine, up_theirs, table)
    out, back, gu_theirs, gd_theirs = feed_forward(
        low_two, both, up_theirs, after(down_theirs, low_two), middle, part
    )
    gd_core, gu_core = grid.send(gd_theirs, c=1), grid.send(gu_theirs, c=1)
    out, back, gu_mine, gd_mine = feed_forward(low_two, both, up_mine, down_mine, out, part, back)
    gd_core, gu_core = after((gd_core, gu_core), back)

    def blocks(value):
        return value.reshape(grid.z_count, 2, 2, -1, value.shape[-1])

    gd_out, gd_keep = grid.halves("y", [blocks(gd_mine), blocks(gd_core)])
    gd_got = grid.send(gd_out, y=1)
    gu_out, gu_keep = grid.halves("x", [blocks(gu_mine), blocks(after(gu_core, gd_out))])
    gu_got = grid.send(gu_out, x=1)
    grad_middle, ga_mine, ga_theirs, gp_mine, gp_theirs, norm_two = middle_back(
        core, middle, after(back, gd_out, gu_out), both, table, up_mine, up_theirs, att_mine,
        att_theirs,
    )
    gp_core = grid.send(gp_theirs, c=1)
    gq_theirs, gq_rest, grad_low = attend_back(
        mixed_theirs, ga_theirs, att_theirs, log_theirs, low, w_theirs, pairs
    )
    gq_core = [grid.send(value, c=1) for value in (gq_theirs, gq_rest)]
    gd_got, gu_got, gp_core = after((gd_got, gu_got, gp_core), grad_low)
    gd_out, gd_keep = grid.halves("x", [gd_keep, gd_got])
    gd_got = grid.send(gd_out, x=1)
    gu_out, gu_keep = grid.halves("y", [gu_keep, gu_got])
    gu_got = grid.send(gu_out, y=1)
    out_home = exchange(after(out.reshape(4, SEQ // 4, dim), gd_out, gu_out))
    mine = (mixed_mine, after(ga_mine, gd_out, gu_out), att_mine, log_mine, low, w_mine, pairs)
    final = (both, grad_middle, table, norm_two)
    if part % 16 == 0:
        *cuts, grad_x, _ = attend_back(
            *mine, grad_low, final, where, (*gq_core, gp_mine, gp_core), part
        )
        left_out, left_keep, right_out, right_keep = cuts
    else:
        gq_mine, gq_more, grad_x, _ = attend_back(*mine, grad_low, final)
        left_out, left_keep = grid.halves("x", [blocks(gq_mine), blocks(gq_core[0])])
        right_out, right_keep = grid.halves(
            "y",
            [
                jnp.concatenate([blocks(gq_more), blocks(gp_mine)], axis=-1),
                jnp.concatenate([blocks(gq_core[1]), blocks(gp_core)], axis=-1),
            ],
        )
    left_got, right_got = grid.send(left_out, x=1), grid.send(right_out, y=1)
    left_keep, left_got, right_keep, right_got = (
        value.reshape(grid.z_count, 2, part, -1)
        for value in (left_keep, left_got, right_keep, right_got)
    )
    gd_got, gu_got, out_home = after((gd_got, gu_got, out_home), left_out, right_out)
    out_home = settle(out_home)
    ffn_parts = grid.by_block((gu_keep, gu_got), (gd_keep, gd_got))
    left_got, right_got = after((left_got, right_got), ffn_parts, out_home)
    ffn_got = [grid.send(part, z=step) for step, part in enumerate(ffn_parts) if step]
    left_out, left_keep = grid.halves("y", [left_keep, left_got])
    left_got = grid.send(left_out, y=1)
    right_out, right_keep = grid.halves("x", [right_keep, right_got])
    right_got = grid.send(right_out, x=1)
    grad_home = exchange(after(grad_x.reshape(4, SEQ // 4, dim), left_got))
    left_got, right_got = after((left_got, right_got), ffn_got)
    qkv_parts = grid.by_block((left_keep, left_got), (right_keep, right_got))
    sum_ffn = after(grid.total([ffn_parts[0], *ffn_got]), qkv_parts)
    ffn_x = grid.send(sum_ffn, x=1)
    qkv_got = [grid.send(part, z=step) for step, part in enumerate(qkv_parts) if step]
    qkv_got, grad_home = after((qkv_got, grad_home), grad_home)
    sum_qkv = grid.total([qkv_parts[0], *qkv_got])
    ffn_x = grid.join(sum_ffn, ffn_x, grid.x, 0)
    all_ffn = grid.join(ffn_x, grid.send(ffn_x, c=1), grid.c, 0)
    shares = grid.share(sum_qkv)
    grad_home = after(grad_home, sum_qkv).astype(F32)
    shard_up, shard_down = finish(
        functools.partial(finish_ffn, fan), where_head, [after(all_ffn, sum_qkv)],
        (share, hidden), (2 * fan, dim),
    )
    shard_qkv, shard_proj, *norms = finish(
        functools.partial(finish_qkv, pairs), where_head, after(shares, shard_up),
        (share, 3 * dim), (share, dim), *[(share,)] * 4,
    )
    return (
        out_home,
        grad_home,
        shard_qkv,
        shard_proj,
        shard_up,
        shard_down,
        norms[0],
        norms[1],
        norms[2],
        norms[3],
    )


def solution(mesh):
    spread = P("dp", "head", None)
    placed = (spread,) + (P("dp", None),) * 4 + (P("dp"),) * 4 + (spread,)
    return jax.shard_map(
        local,
        mesh=mesh,
        in_specs=placed,
        out_specs=(spread, spread) + (P("dp", None),) * 4 + (P("dp"),) * 4,
        check_vma=False,
    )
```

```python
import functools

import jax
import jax.numpy as jnp
from jax import lax
from jax.experimental import pallas as pl
from jax.experimental.pallas import tpu as pltpu
from jax.sharding import PartitionSpec as P

HEADS = 12
HEAD_DIM = 64
SEQ = 1024
EPSILON = 1e-05
BOTH = ("dp", "head")
BLOCK = 256
GELU_A = 0.7978845608028654
GELU_B = 0.044715
F32 = jnp.float32
BF16 = jnp.bfloat16


def params(mebi):
    return pltpu.CompilerParams(vmem_limit_bytes=mebi * 2**20)


def dot_nn(left, right):
    return lax.dot_general(left, right, (((1,), (0,)), ((), ())), preferred_element_type=F32)


def dot_nt(left, right):
    return lax.dot_general(left, right, (((1,), (1,)), ((), ())), preferred_element_type=F32)


def dot_tn(left, right):
    return lax.dot_general(left, right, (((0,), (0,)), ((), ())), preferred_element_type=F32)


def cost(micros):
    return pl.CostEstimate(
        flops=int(micros * 1.1e9), bytes_accessed=int(micros * 3e6), transcendentals=0
    )


def whole(*shape):
    return pl.BlockSpec(shape, lambda *_: (0,) * len(shape))


def part_of(pair, which):
    parts, _, count, dim = pair.shape
    return pl.BlockSpec((parts, 1, count, dim), lambda *_: (0, which, 0, 0))


def part_rows(pair, which):
    _, _, count, dim = pair.shape
    return pl.BlockSpec((1, 1, count, dim), lambda i, *_: (i, which, 0, 0))


def rows(count, width):
    return pl.BlockSpec((count, width), lambda i, *_: (i, 0))


def shaped(shape, dtype):
    return jax.ShapeDtypeStruct(shape, dtype)


def normalise(vector):
    centred = vector - jnp.mean(vector, axis=-1, keepdims=True)
    inverse = lax.rsqrt(jnp.mean(centred * centred, axis=-1, keepdims=True) + EPSILON)
    return centred * inverse, inverse


def norm_back(unit, inverse, gain, grad):
    scaled = grad * gain
    return inverse * (
        scaled
        - jnp.mean(scaled, axis=-1, keepdims=True)
        - unit * jnp.mean(scaled * unit, axis=-1, keepdims=True)
    )


def proj_kernel(core_ref, x_ref, am_ref, at_ref, pm_ref, pt_ref, table_ref, mid_ref, low_ref, total):
    half = am_ref.shape[1]
    mine = pl.multiple_of(core_ref[0] * half, half)
    theirs = pl.multiple_of((1 - core_ref[0]) * half, half)
    a_mine, a_theirs = am_ref[...], at_ref[...]
    for place, weight in ((mine, pm_ref), (theirs, pt_ref)):
        total[:, pl.ds(place, half)] = (
            x_ref[0, 0, :, pl.ds(place, half)].astype(F32)
            + dot_nn(a_mine, weight[pl.ds(mine, half), :])
            + dot_nn(a_theirs, weight[pl.ds(theirs, half), :])
        )
    mid_ref[...] = total[...].astype(BF16)
    unit, _ = normalise(total[...])
    low_ref[...] = (unit * table_ref[2:3] + table_ref[3:4]).astype(BF16)


def proj_spec(dim):
    half = dim // 2
    return pl.BlockSpec((dim, half), lambda i, *_: (0, 4))


def project(core, x, a_mine, a_theirs, w_mine, w_theirs, table):
    tok, dim = SEQ, x.shape[-1]
    half = dim // 2
    return pl.pallas_call(
        proj_kernel,
        grid_spec=pltpu.PrefetchScalarGridSpec(
            num_scalar_prefetch=1,
            grid=(tok // BLOCK,),
            in_specs=[part_rows(x, 0), rows(BLOCK, half), rows(BLOCK, half)]
            + [proj_spec(dim), proj_spec(dim), whole(8, dim)],
            out_specs=[rows(BLOCK, dim), rows(BLOCK, dim)],
            scratch_shapes=[pltpu.VMEM((BLOCK, dim), F32)],
        ),
        out_shape=[shaped((tok, dim), BF16), shaped((tok, dim), BF16)],
        compiler_params=params(58),
        cost_estimate=cost(0.01),
    )(core, x, a_mine, a_theirs, w_mine, w_theirs, table)


def middle_kernel(
    core_ref, mid_ref, back_ref, cot_ref, table_ref, pm_ref, pt_ref, am_ref, at_ref,
    grad_ref, gm_ref, gt_ref, wm_ref, wt_ref, norm_ref, heads, branch,
):
    half = am_ref.shape[1]
    step = pl.program_id(0)
    mine = pl.multiple_of(core_ref[0] * half, half)
    theirs = pl.multiple_of((1 - core_ref[0]) * half, half)
    here = pl.ds(pl.multiple_of(step * BLOCK, BLOCK), BLOCK)

    @pl.when(step == 0)
    def _():
        norm_ref[...] = jnp.zeros_like(norm_ref)

    unit, inverse = normalise(mid_ref[...].astype(F32))
    grad = back_ref[...].astype(F32)
    norm_ref[0:1] += jnp.sum(grad * unit, axis=0, keepdims=True)
    norm_ref[1:2] += jnp.sum(grad, axis=0, keepdims=True)
    back = norm_back(unit, inverse, table_ref[2:3], grad)
    grad_ref[...] = (cot_ref[0, 0].astype(F32) + back).astype(BF16)
    branch[here, :half] = grad_ref[:, pl.ds(mine, half)]
    branch[here, half:] = grad_ref[:, pl.ds(theirs, half)]
    heads[here, :half] = am_ref[...]
    heads[here, half:] = at_ref[...]
    for place, out in ((mine, gm_ref), (theirs, gt_ref)):
        out[...] = (
            dot_nt(branch[here, :half], pm_ref[pl.ds(place, half), :])
            + dot_nt(branch[here, half:], pt_ref[pl.ds(place, half), :])
        ).astype(BF16)

    @pl.when(step == pl.num_programs(0) - 1)
    def _():
        for place, start in ((mine, 0), (theirs, half)):
            total = dot_tn(heads[:, start : start + half], branch[...]).astype(BF16)
            wm_ref[pl.ds(place, half), :] = total[:, :half]
            wt_ref[pl.ds(place, half), :] = total[:, half:]


def middle_back(core, middle, back, cot, table, w_mine, w_theirs, a_mine, a_theirs):
    tok, dim = middle.shape
    half = dim // 2
    return pl.pallas_call(
        middle_kernel,
        grid_spec=pltpu.PrefetchScalarGridSpec(
            num_scalar_prefetch=1,
            grid=(tok // BLOCK,),
            in_specs=[rows(BLOCK, dim), rows(BLOCK, dim), part_rows(cot, 1)]
            + [whole(8, dim), proj_spec(dim), proj_spec(dim)]
            + [rows(BLOCK, half)] * 2,
            out_specs=[rows(BLOCK, dim), rows(BLOCK, half), rows(BLOCK, half)]
            + [whole(dim, half), whole(dim, half), whole(8, dim)],
            scratch_shapes=[pltpu.VMEM((tok, dim), BF16)] * 2,
        ),
        out_shape=[shaped((tok, dim), BF16)]
        + [shaped((tok, half), BF16)] * 2
        + [shaped((dim, half), BF16)] * 2
        + [shaped((8, dim), F32)],
        compiler_params=params(58),
        cost_estimate=cost(0.01),
    )(core, middle, back, cot, table, w_mine, w_theirs, a_mine, a_theirs)


def lane_low(count):
    return lax.broadcasted_iota(jnp.int32, (count, 128), 1) < HEAD_DIM


def upper():
    return lax.broadcasted_iota(jnp.int32, (BLOCK, BLOCK), 0) <= lax.broadcasted_iota(
        jnp.int32, (BLOCK, BLOCK), 1
    )


def keep_head(low_lanes, head, value):
    zero = jnp.zeros((), value.dtype)
    return jnp.where(low_lanes, value, zero) if head == 0 else jnp.where(low_lanes, zero, value)


def attend_kernel(first, *refs):
    if first:
        x_ref, w_ref, tail_ref, low_ref, mixed_ref, o_ref, l_ref, table_ref = refs
    else:
        low_ref, w_ref, mixed_ref, o_ref, l_ref = refs
    seq = mixed_ref.shape[0]

    if first:

        @pl.when(pl.program_id(0) == 0)
        def _():
            table_ref[...] = tail_ref[...].astype(F32).T[:8]
            for start in range(0, seq, BLOCK):
                here = pl.ds(start, BLOCK)
                unit, _ = normalise(x_ref[start // BLOCK, 0].astype(F32))
                low_ref[here, :] = (unit * table_ref[0:1] + table_ref[1:2]).astype(BF16)

    mixed_ref[...] = dot_nn(low_ref[...], w_ref[...]).astype(BF16)
    q_ref, k_ref, v_ref = (mixed_ref.at[:, 128 * i : 128 * (i + 1)] for i in range(3))
    low_lanes = lane_low(BLOCK)
    allowed = upper()
    scaling = jnp.asarray(HEAD_DIM**-0.5, BF16)
    tiles = [(block, head) for block in range(seq // BLOCK) for head in range(2)]
    with_ones = jnp.concatenate([v_ref[...], jnp.ones((seq, 128), BF16)], axis=1)

    def score(block, head):
        end = (block + 1) * BLOCK
        queries = keep_head(low_lanes, head, q_ref[block * BLOCK : end, :] * scaling)
        raw = dot_nt(k_ref[:end, :], queries)
        last = jnp.where(allowed, raw[end - BLOCK :, :], -1e30)
        return jnp.concatenate([raw[: end - BLOCK, :], last], axis=0) if block else last

    ahead = 3
    waiting = [score(*tile) for tile in tiles[:ahead]]
    parts = []
    for step, (block, head) in enumerate(tiles):
        end = (block + 1) * BLOCK
        if step + ahead < len(tiles):
            waiting.append(score(*tiles[step + ahead]))
        scores = waiting.pop(0)
        row_max = jnp.max(scores, axis=0, keepdims=True)
        weights = jnp.exp(scores - row_max).astype(BF16)
        summed = dot_tn(weights, with_ones[:end])
        totals = summed[:, 128:]
        parts.append(summed[:, :128] / totals)
        l_ref[0, head : head + 1, block * BLOCK : end] = row_max + jnp.log(totals.T[0:1, :])
        if head == 1:
            o_ref[block * BLOCK : end, :] = jnp.where(low_lanes, parts[-2], parts[-1]).astype(BF16)


def columns(count, width):
    return pl.BlockSpec((count, width), lambda i, *_: (0, i))


def attend(value, weight, pairs, first):
    seq, dim = SEQ, value.shape[-1]
    group = 3 * 128
    tail = pl.BlockSpec((dim, 128), lambda i: (0, 3 * pairs))
    return pl.pallas_call(
        functools.partial(attend_kernel, first),
        grid=(pairs,),
        in_specs=[part_of(value, 0) if first else whole(seq, dim), columns(dim, group)]
        + ([tail] if first else []),
        out_specs=([whole(seq, dim)] if first else [])
        + [columns(seq, group), columns(seq, 128), pl.BlockSpec((1, 2, seq), lambda i: (i, 0, 0))]
        + ([whole(8, dim)] if first else []),
        out_shape=([shaped((seq, dim), BF16)] if first else [])
        + [shaped((seq, pairs * group), BF16), shaped((seq, pairs * 128), BF16)]
        + [shaped((pairs, 2, seq), F32)]
        + ([shaped((8, dim), F32)] if first else []),
        compiler_params=params(58),
        cost_estimate=cost(0.01),
    )(value, weight, *((weight,) if first else ()))


def attend_back_kernel(carry, final, part, *refs):
    if part:
        where_ref, *refs = refs
    mixed_ref, do_ref, o_ref, l_ref, low_ref, w_ref, *refs = refs
    if carry:
        grad_in, *refs = refs
    if final:
        x_ref, mid_ref, table_ref, norm_two, *refs = refs
    if part:
        core_ref, core_more, gp_ref, gp_core, *refs = refs
        left_out, left_keep, right_out, right_keep, *refs = refs
    else:
        gq_ref, more_ref, *refs = refs
    if final:
        out_ref, norm_ref, *refs = refs
    else:
        grad_ref, *refs = refs
    sum_k, sum_v, both, every, *sums = refs
    q_ref, k_ref, v_ref = (mixed_ref.at[:, 128 * i : 128 * (i + 1)] for i in range(3))
    dq_ref, dk_ref, dv_ref = (both.at[:, 128 * i : 128 * (i + 1)] for i in range(3))
    seq = mixed_ref.shape[0]
    step = pl.program_id(0)
    low_lanes = lane_low(BLOCK)
    low_all = lane_low(seq)
    allowed = upper()
    scaling = jnp.asarray(HEAD_DIM**-0.5, BF16)
    head_keys = [keep_head(low_all, head, k_ref[...]) for head in range(2)]
    tiles = [(block, head) for block in reversed(range(seq // BLOCK)) for head in range(2)]

    def scored(block, head):
        start, end = block * BLOCK, (block + 1) * BLOCK
        q_head = keep_head(low_lanes, head, q_ref[start:end, :] * scaling)
        g_head = keep_head(low_lanes, head, do_ref[start:end, :])
        return q_head, g_head, dot_nt(k_ref[:end, :], q_head), dot_nt(v_ref[:end, :], g_head)

    ahead = 2
    waiting = [scored(*tile) for tile in tiles[:ahead]]
    for number, (block, head) in enumerate(tiles):
        start, end = block * BLOCK, (block + 1) * BLOCK
        if number + ahead < len(tiles):
            waiting.append(scored(*tiles[number + ahead]))
        q_head, g_head, scores, grad_probs = waiting.pop(0)
        if head == 0:
            dots = (do_ref[start:end, :].astype(F32) * o_ref[start:end, :].astype(F32)).T
        centre = jnp.sum(dots[HEAD_DIM * head : HEAD_DIM * (head + 1)], axis=0, keepdims=True)
        probs = jnp.exp(scores - l_ref[0, head : head + 1, start:end])
        last = jnp.where(allowed, probs[start:, :], 0.0)
        probs = jnp.concatenate([probs[:start, :], last], axis=0) if block else last
        grad_scores = (probs * (grad_probs - centre)).astype(BF16)
        terms = (
            dot_tn(grad_scores, head_keys[head][:end]),
            dot_nn(grad_scores, q_head),
            dot_nn(probs.astype(BF16), g_head),
        )
        if head == 0:
            add_q, add_k, add_v = terms
            continue
        add_q, add_k, add_v = add_q + terms[0], add_k + terms[1], add_v + terms[2]
        dq_ref[start:end, :] = (add_q * HEAD_DIM**-0.5).astype(BF16)
        if end == seq:
            sum_k[...] = add_k
            sum_v[...] = add_v
        else:
            sum_k[:end, :] += add_k
            sum_v[:end, :] += add_v
    dk_ref[...] = sum_k[...].astype(BF16)
    dv_ref[...] = sum_v[...].astype(BF16)

    here = pl.ds(pl.multiple_of(step * 384, 384), 384)
    grad_qkv = dot_tn(low_ref[...], both[...]).astype(BF16)
    every[:, here] = both[...]

    def cut(out, keep, columns, source, size, index):
        for block in range(source.shape[0] // (2 * size)):
            to = pl.ds(block * size, size)
            for ref, side in ((out, 1 - index), (keep, index)):
                start = pl.multiple_of(block * 2 * size + side * size, 16)
                ref[to, columns] = source[pl.ds(start, size), :]

    @pl.when(step < pl.num_programs(0) - 1)
    def _():
        if part:
            sums[0][...] = (grad_qkv.astype(F32) + core_ref[:, here].astype(F32)).astype(BF16)
            cut(left_out, left_keep, here, sums[0], part, where_ref[0])
        else:
            gq_ref[:, here] = grad_qkv

    @pl.when(step == pl.num_programs(0) - 1)
    def _():
        if part:
            sums[1][:, :384] = (
                grad_qkv.astype(F32) + core_more[:, :384].astype(F32)
            ).astype(BF16)
        else:
            more_ref[:, :384] = grad_qkv


    @pl.when(step == pl.num_programs(0) - 1)
    def _():
        if final:
            norm_ref[...] = jnp.zeros_like(norm_ref)
        for start in range(0, seq, BLOCK):
            here = pl.ds(start, BLOCK)
            grad = dot_nt(every[here, :], w_ref[...])
            if carry:
                grad = grad + grad_in[here, :].astype(F32)
            if not final:
                grad_ref[here, :] = grad.astype(BF16)
                continue
            unit, inverse = normalise(x_ref[start // BLOCK, 0].astype(F32))
            norm_ref[0:1] += jnp.sum(grad * unit, axis=0, keepdims=True)
            norm_ref[1:2] += jnp.sum(grad, axis=0, keepdims=True)
            back = norm_back(unit, inverse, table_ref[0:1], grad)
            out_ref[here, :] = (mid_ref[here, :].astype(F32) + back).astype(BF16)
        tail = jnp.zeros((128, low_ref.shape[1]), F32)
        if final:
            tail = jnp.concatenate([norm_ref[:2], norm_two[:2], tail[4:]], axis=0)
        if part:
            sums[1][:, 384:512] = (tail.T + core_more[:, 384:].astype(F32)).astype(BF16)
            sums[1][:, 512:] = (gp_ref[...].astype(F32) + gp_core[...].astype(F32)).astype(BF16)
            cut(right_out, right_keep, slice(None), sums[1], 2 * part, where_ref[1])
        else:
            more_ref[:, 384:] = tail.T.astype(BF16)


def attend_back(
    mixed, grad, attended, logs, low, weight, pairs, carry=None, final=(), where=None, others=(), part=0
):
    seq, dim = low.shape
    group = 3 * 128
    wide = pairs * group

    def column(width):
        return pl.BlockSpec((seq, width), lambda i, *_: (0, i))

    more = [whole(seq, dim)] if carry is not None else []
    more += [part_of(final[0], 0), whole(seq, dim), whole(8, dim), whole(8, dim)] if final else []
    more += [whole(*other.shape) for other in others]
    widths = [wide - group, group + 128]
    outs = [(dim, width) for width in widths]
    scratch = [pltpu.VMEM((seq, 128), F32)] * 2
    scratch += [pltpu.VMEM((seq, group), BF16), pltpu.VMEM((seq, wide), BF16)]
    if part:
        widths[1] += others[2].shape[1]
        outs = [(dim // 2, width) for width in widths for _ in range(2)]
        scratch += [pltpu.VMEM((dim, group), BF16), pltpu.VMEM((dim, widths[1]), BF16)]
    return pl.pallas_call(
        functools.partial(attend_back_kernel, carry is not None, bool(final), part),
        grid_spec=pltpu.PrefetchScalarGridSpec(
            num_scalar_prefetch=1 if part else 0,
            grid=(pairs,),
            in_specs=[column(group), column(128), column(128)]
            + [pl.BlockSpec((1, 2, seq), lambda i, *_: (i, 0, 0)), whole(seq, dim)]
            + [whole(dim, wide)]
            + more,
            out_specs=[whole(*shape) for shape in outs]
            + [whole(seq, dim)]
            + ([whole(8, dim)] if final else []),
            scratch_shapes=scratch,
        ),
        out_shape=[shaped(shape, BF16) for shape in outs]
        + [shaped((seq, dim), BF16)]
        + ([shaped((8, dim), F32)] if final else []),
        compiler_params=params(58),
        cost_estimate=cost(0.01),
    )(
        *((where,) if part else ()),
        mixed,
        grad,
        attended,
        logs,
        low,
        weight,
        *(() if carry is None else (carry,)),
        *final,
        *others,
    )


def ffn_kernel(final, paired, *refs):
    low_ref, cot_ref, up_ref, down_ref, out_in = refs[:5]
    back_in = refs[5] if final else None
    out_ref, back_ref, gu_ref, gd_ref, out_sum, back_sum, act, hid = refs[5 + final :]

    def chunk(first):
        up, down = up_ref[...], down_ref[...]
        for start in range(0, low_ref.shape[0], BLOCK):
            here = pl.ds(start, BLOCK)
            hidden = dot_nn(low_ref[here, :], up)
            grad_active = dot_nt(cot_ref[start // BLOCK, 0], down)
            square = hidden * hidden
            bend = jnp.tanh(hidden * (GELU_A + (GELU_A * GELU_B) * square))
            gate = 0.5 + 0.5 * bend
            active = (hidden * gate).astype(BF16)
            slope = gate + hidden * (0.5 - 0.5 * bend * bend) * (
                GELU_A + (3 * GELU_A * GELU_B) * square
            )
            grad_hidden = (grad_active * slope).astype(BF16)
            act[here, :] = active
            hid[here, :] = grad_hidden
            add_out, add_back = dot_nn(active, down), dot_nt(grad_hidden, up)
            if first:
                out_sum[here, :] = add_out
                back_sum[here, :] = add_back
            else:
                total = out_sum[here, :] + add_out + out_in[here, :].astype(F32)
                out_ref[here, :] = total.astype(out_ref.dtype)
                total = back_sum[here, :] + add_back
                if final:
                    total = total + back_in[here, :].astype(F32)
                back_ref[here, :] = total.astype(BF16)
        gu_ref[...] = dot_tn(low_ref[...], hid[...]).astype(BF16)
        cot = cot_ref[...].reshape(act.shape[0], -1)
        grad_down = dot_tn(act[...], cot).astype(BF16)
        if paired:
            dim = grad_down.shape[1]
            grad_down = grad_down.reshape(-1, 2 * paired, dim)
            for side in range(2):
                gd_ref[:, side * dim : (side + 1) * dim] = grad_down[
                    :, side * paired : (side + 1) * paired
                ].reshape(-1, dim)
        else:
            gd_ref[...] = grad_down

    for place in range(2):

        @pl.when(pl.program_id(0) == place)
        def _(place=place):
            chunk(place == 0)


def feed_forward(low, pair, up, down, out_in, part, back_in=None):
    tok, dim = low.shape
    final = back_in is not None
    wide = down.shape[0]
    chunk = wide // 2
    paired = part if part % 16 == 0 else 0
    tall, long = (chunk // 2, 2 * dim) if paired else (chunk, dim)
    outs = pl.pallas_call(
        functools.partial(ffn_kernel, int(final), paired),
        grid=(2,),
        in_specs=[whole(tok, dim), part_of(pair, 1), columns(dim, chunk), rows(chunk, dim)]
        + [whole(tok, dim)] * (2 if final else 1),
        out_specs=[whole(tok, dim), whole(tok, dim), columns(dim, chunk), rows(tall, long)],
        out_shape=[shaped((tok, dim), BF16 if final else F32), shaped((tok, dim), BF16)]
        + [shaped((dim, wide), BF16), shaped((2 * tall, long), BF16)],
        scratch_shapes=[pltpu.VMEM((tok, dim), F32)] * 2 + [pltpu.VMEM((tok, chunk), BF16)] * 2,
        compiler_params=params(58),
        cost_estimate=cost(0.01),
    )(low, pair, up, down, out_in, *((back_in,) if final else ()))
    if paired:
        return outs
    grad_down = outs[3].reshape(-1, 2, part, dim).transpose(0, 2, 1, 3).reshape(-1, 2 * dim)
    return list(outs[:3]) + [grad_down]


def by_place(where_ref, refs):
    x, c = where_ref[0], where_ref[1]
    own, other_x, other_c, other_both = (ref[...].astype(F32) for ref in refs)
    low_x = [jnp.where(x == 0, own, other_x), jnp.where(x == 0, other_c, other_both)]
    high_x = [jnp.where(x == 0, other_x, own), jnp.where(x == 0, other_both, other_c)]
    return [
        [jnp.where(c == 0, side[0], side[1]) for side in (low_x, high_x)],
        [jnp.where(c == 0, side[1], side[0]) for side in (low_x, high_x)],
    ]


def finish_ffn(fan, where_ref, all_ref, up_ref, down_ref):
    part, dim = all_ref.shape[2], down_ref.shape[1]
    count = up_ref.shape[1] // fan // 2
    for core in range(2):
        for side in range(2):
            here = slice(side * part, (side + 1) * part)
            for block in range(count):
                place = (2 * block + core) * fan
                up_ref[here, place : place + fan] = all_ref[
                    core, side, :, block * fan : (block + 1) * fan
                ].astype(F32)
            start = count * fan
            for half in range(2):
                place = core * fan + side * fan // 2 + half * part
                down_ref[place : place + part, :] = all_ref[
                    core, side, :, start + half * dim : start + (half + 1) * dim
                ].astype(F32)


def finish_qkv(pairs, where_ref, *refs):
    pieces, (qkv_ref, proj_ref, *norm_refs) = by_place(where_ref, refs[:4]), refs[4:]
    part, dim = refs[0].shape[0], qkv_ref.shape[1] // 3
    sums = []
    for side in range(2):
        here = slice(side * part, (side + 1) * part)
        for core in range(2):
            piece = pieces[core][side]
            for pair in range(pairs):
                for which in range(3):
                    place = which * dim + core * dim // 2 + pair * 128
                    start = (pair * 3 + which) * 128
                    qkv_ref[here, place : place + 128] = piece[:, start : start + 128]
            start = pairs * 384 + 128
            proj_ref[here, core * dim // 2 : (core + 1) * dim // 2] = piece[:, start:]
        norms = slice(pairs * 384, pairs * 384 + 128)
        sums.append(pieces[0][side][:, norms] + pieces[1][side][:, norms])
    sums = jnp.concatenate(sums, axis=0).T
    for place, norm_ref in enumerate(norm_refs):
        norm_ref[...] = sums[place : place + 1].reshape(norm_ref.shape)


def settle_kernel(in_ref, out_ref):
    out_ref[...] = in_ref[...]


def settle(value):
    spec = pl.BlockSpec((1,) + value.shape[1:], lambda i: (i, 0, 0))
    return pl.pallas_call(
        settle_kernel,
        grid=value.shape[:1],
        in_specs=[spec],
        out_specs=spec,
        out_shape=shaped(value.shape, value.dtype),
        cost_estimate=cost(0.01),
    )(value)


def finish(kernel, where, pieces, *shapes):
    return pl.pallas_call(
        kernel,
        grid_spec=pltpu.PrefetchScalarGridSpec(
            num_scalar_prefetch=1,
            grid=(1,),
            in_specs=[whole(*piece.shape) for piece in pieces],
            out_specs=[whole(*shape) for shape in shapes],
        ),
        out_shape=[shaped(shape, F32) for shape in shapes],
        compiler_params=params(58),
        cost_estimate=cost(0.01),
    )(where, *pieces)


class Grid:
    def __init__(self):
        self.z_count = lax.axis_size("dp") // 2
        self.dp, self.head = lax.axis_index("dp"), lax.axis_index("head")
        self.z, self.y, self.x, self.c = self.dp // 2, self.dp % 2, self.head // 2, self.head % 2
        assert lax.axis_size("head") == 4 and lax.axis_size("dp") % 2 == 0

    def send(self, value, z=0, y=0, x=0, c=0):
        pairs = []
        for source in range(self.z_count * 8):
            zi, yi, xi, ci = source // 8, source // 4 % 2, source // 2 % 2, source % 2
            zt, yt, xt, ct = (zi + z) % self.z_count, yi ^ y, xi ^ x, ci ^ c
            pairs.append((source, ((zt * 2 + yt) * 2 + xt) * 2 + ct))
        return lax.ppermute(value, BOTH, pairs)

    def pick(self, value, axis, index):
        return lax.dynamic_index_in_dim(value, index, axis, keepdims=False)

    def join(self, mine, other, index, axis):
        shape = mine.shape[:axis] + (2,) + mine.shape[axis:]
        here = lax.broadcasted_iota(jnp.int32, shape, axis) == index
        mine, other = (jnp.broadcast_to(jnp.expand_dims(v, axis), shape) for v in (mine, other))
        return jnp.where(here, mine, other)

    def to_z(self, piece):
        return [piece] + [self.send(piece, z=step) for step in range(1, self.z_count)]

    def by_z(self, got):
        shape = (self.z_count,) + got[0].shape
        steps = (self.z - lax.broadcasted_iota(jnp.int32, shape, 0)) % self.z_count
        out = jnp.broadcast_to(got[0], shape)
        for step in range(1, self.z_count):
            out = jnp.where(steps == step, jnp.broadcast_to(got[step], shape), out)
        return out

    def over_z(self, piece):
        copies = jnp.broadcast_to(piece, (self.z_count,) + piece.shape)
        groups = [list(range(y, self.z_count * 2, 2)) for y in range(2)]
        return lax.all_to_all(
            copies, "dp", split_axis=0, concat_axis=0, tiled=True, axis_index_groups=groups
        )

    def over_y(self, value, got):
        return self.join(value, got, self.y, 1)

    def over_x(self, value, got, axis):
        return self.join(value, got, self.x, axis)

    def halves(self, name, values):
        axis, index = (1, self.y) if name == "y" else (values[0].ndim - 3, self.x)
        low, high = (
            sum(lax.index_in_dim(v, place, axis, False).astype(F32) for v in values).astype(BF16)
            for place in range(2)
        )
        return jnp.where(index == 0, high, low), jnp.where(index == 0, low, high)

    def by_block(self, *values):
        totals = [keep.astype(F32) + got.astype(F32) for keep, got in values]
        return [
            jnp.concatenate(
                [self.pick(total, 0, (self.z + step) % self.z_count) for total in totals], axis=-1
            ).astype(BF16)
            for step in range(self.z_count)
        ]

    def end(self, parts):
        return self.total(
            [parts[0]] + [self.send(part, z=step) for step, part in enumerate(parts) if step]
        )

    def total(self, parts):
        return sum(value.astype(F32) for value in parts).astype(BF16)

    def share(self, piece):
        return [piece, self.send(piece, x=1), self.send(piece, c=1), self.send(piece, x=1, c=1)]

    def share_all(self, piece):
        both = self.join(piece, self.send(piece, x=1), self.x, 0)
        return self.join(both, self.send(both, c=1), self.c, 0)


def exchange(value):
    return lax.all_to_all(value, "head", split_axis=0, concat_axis=0, tiled=True)


def after(value, *done):
    return lax.optimization_barrier((value, done))[0]


def flat(value):
    return value.reshape(-1, value.shape[-1])


def local(
    tokens,
    qkv_weight,
    proj_weight,
    up_weight,
    down_weight,
    attn_gain,
    attn_bias,
    ffn_gain,
    ffn_bias,
    cotangent,
):
    grid = Grid()
    dim = tokens.shape[-1]
    share = qkv_weight.shape[0]
    part = share // 2
    half = dim // 2
    pairs = half // 128
    hidden = up_weight.shape[1]
    dp_count = lax.axis_size("dp")
    fan = hidden // dp_count // 2
    core = grid.c.reshape(1).astype(jnp.int32)
    assert tokens.shape[0] == 4 and tokens.shape[1] * 4 == SEQ
    assert fan == 4 * part

    def row_half(value):
        return lax.dynamic_slice_in_dim(value, grid.x * part, part, 0)

    qkv = grid.pick(qkv_weight.reshape(share, 3, 2, pairs, 128), 2, grid.c)
    qkv = qkv.transpose(0, 2, 1, 3).reshape(share, -1)
    table = jnp.stack([attn_gain, attn_bias, ffn_gain, ffn_bias], axis=1)
    table = jnp.pad(table, ((0, 0), (0, 124)))
    piece = jnp.concatenate([qkv, table], axis=1).astype(BF16)
    up = grid.pick(row_half(up_weight).reshape(part, dp_count, 2, fan), 2, grid.c)
    proj = grid.pick(row_half(proj_weight).reshape(part, 2, half), 1, grid.c)
    up_piece = jnp.concatenate([up.reshape(part, -1), proj], axis=1).astype(BF16)
    down_piece = grid.pick(down_weight.reshape(2, fan, dim), 0, grid.c).astype(BF16)
    where = jnp.stack([grid.x, grid.y]).astype(jnp.int32)
    where_head = jnp.stack([grid.x, grid.c]).astype(jnp.int32)

    both = exchange(after(jnp.stack([tokens, cotangent], axis=1), piece))
    first_z = grid.by_z(after(grid.to_z(piece), up_piece, down_piece))
    up_got = grid.to_z(after(up_piece, first_z))
    w_mine = flat(grid.over_y(first_z, after(grid.send(first_z, y=1), up_got)))
    w_theirs = grid.send(w_mine, c=1)
    up_z = grid.by_z(after(up_got, w_mine))
    up_y = grid.send(up_z, y=1)
    up_x = grid.send(up_z, x=1)
    down_both = grid.join(
        down_piece, grid.send(after(down_piece, up_got), y=1), grid.y, 0
    )
    down_mine = grid.over_z(after(down_both, both))
    low, mixed_mine, att_mine, log_mine, table = attend(
        after(both, up_z), w_mine, pairs, True
    )
    mixed_theirs, att_theirs, log_theirs = attend(low, w_theirs, pairs, False)
    up_y, up_x = after((up_y, up_x), att_mine, att_theirs)
    up_xy = grid.send(up_y, x=1)
    up_y = grid.over_y(up_z, up_y)
    up_x = grid.over_y(up_x, up_xy)
    up_mine = flat(grid.over_x(up_y, up_x, 2))
    up_theirs = grid.send(up_mine, c=1)
    down_mine = flat(after(down_mine, up_xy))
    down_theirs = grid.send(down_mine, c=1)
    middle, low_two = project(core, both, att_mine, att_theirs, up_mine, up_theirs, table)
    out, back, gu_theirs, gd_theirs = feed_forward(
        low_two, both, up_theirs, after(down_theirs, low_two), middle, part
    )
    gd_core, gu_core = grid.send(gd_theirs, c=1), grid.send(gu_theirs, c=1)
    out, back, gu_mine, gd_mine = feed_forward(low_two, both, up_mine, down_mine, out, part, back)
    gd_core, gu_core = after((gd_core, gu_core), back)

    def blocks(value):
        return value.reshape(grid.z_count, 2, 2, -1, value.shape[-1])

    gd_out, gd_keep = grid.halves("y", [blocks(gd_mine), blocks(gd_core)])
    gd_got = grid.send(gd_out, y=1)
    gu_out, gu_keep = grid.halves("x", [blocks(gu_mine), blocks(after(gu_core, gd_out))])
    gu_got = grid.send(gu_out, x=1)
    grad_middle, ga_mine, ga_theirs, gp_mine, gp_theirs, norm_two = middle_back(
        core, middle, after(back, gd_out, gu_out), both, table, up_mine, up_theirs, att_mine,
        att_theirs,
    )
    gp_core = grid.send(gp_theirs, c=1)
    gq_theirs, gq_rest, grad_low = attend_back(
        mixed_theirs, ga_theirs, att_theirs, log_theirs, low, w_theirs, pairs
    )
    gq_core = [grid.send(value, c=1) for value in (gq_theirs, gq_rest)]
    gd_got, gu_got, gp_core = after((gd_got, gu_got, gp_core), grad_low)
    gd_out, gd_keep = grid.halves("x", [gd_keep, gd_got])
    gd_got = grid.send(gd_out, x=1)
    gu_out, gu_keep = grid.halves("y", [gu_keep, gu_got])
    gu_got = grid.send(gu_out, y=1)
    out_home = exchange(after(out.reshape(4, SEQ // 4, dim), gd_out, gu_out))
    mine = (mixed_mine, after(ga_mine, gd_out, gu_out), att_mine, log_mine, low, w_mine, pairs)
    final = (both, grad_middle, table, norm_two)
    if part % 16 == 0:
        *cuts, grad_x, _ = attend_back(
            *mine, grad_low, final, where, (*gq_core, gp_mine, gp_core), part
        )
        left_out, left_keep, right_out, right_keep = cuts
    else:
        gq_mine, gq_more, grad_x, _ = attend_back(*mine, grad_low, final)
        left_out, left_keep = grid.halves("x", [blocks(gq_mine), blocks(gq_core[0])])
        right_out, right_keep = grid.halves(
            "y",
            [
                jnp.concatenate([blocks(gq_more), blocks(gp_mine)], axis=-1),
                jnp.concatenate([blocks(gq_core[1]), blocks(gp_core)], axis=-1),
            ],
        )
    left_got, right_got = grid.send(left_out, x=1), grid.send(right_out, y=1)
    left_keep, left_got, right_keep, right_got = (
        value.reshape(grid.z_count, 2, part, -1)
        for value in (left_keep, left_got, right_keep, right_got)
    )
    gd_got, gu_got, out_home = after((gd_got, gu_got, out_home), left_out, right_out)
    out_home = settle(out_home)
    ffn_parts = grid.by_block((gu_keep, gu_got), (gd_keep, gd_got))
    left_got, right_got = after((left_got, right_got), ffn_parts, out_home)
    ffn_got = [grid.send(part, z=step) for step, part in enumerate(ffn_parts) if step]
    left_out, left_keep = grid.halves("y", [left_keep, left_got])
    left_got = grid.send(left_out, y=1)
    right_out, right_keep = grid.halves("x", [right_keep, right_got])
    right_got = grid.send(right_out, x=1)
    grad_home = exchange(after(grad_x.reshape(4, SEQ // 4, dim), left_got))
    left_got, right_got = after((left_got, right_got), ffn_got)
    qkv_parts = grid.by_block((left_keep, left_got), (right_keep, right_got))
    sum_ffn = after(grid.total([ffn_parts[0], *ffn_got]), qkv_parts)
    ffn_x = grid.send(sum_ffn, x=1)
    qkv_got = [grid.send(part, z=step) for step, part in enumerate(qkv_parts) if step]
    qkv_got, grad_home = after((qkv_got, grad_home), grad_home)
    sum_qkv = grid.total([qkv_parts[0], *qkv_got])
    ffn_x = grid.join(sum_ffn, ffn_x, grid.x, 0)
    all_ffn = grid.join(ffn_x, grid.send(ffn_x, c=1), grid.c, 0)
    shares = grid.share(sum_qkv)
    grad_home = after(grad_home, sum_qkv).astype(F32)
    shard_up, shard_down = finish(
        functools.partial(finish_ffn, fan), where_head, [after(all_ffn, sum_qkv)],
        (share, hidden), (2 * fan, dim),
    )
    shard_qkv, shard_proj, *norms = finish(
        functools.partial(finish_qkv, pairs), where_head, after(shares, shard_up),
        (share, 3 * dim), (share, dim), *[(share,)] * 4,
    )
    return (
        out_home,
        grad_home,
        shard_qkv,
        shard_proj,
        shard_up,
        shard_down,
        norms[0],
        norms[1],
        norms[2],
        norms[3],
    )


def solution(mesh):
    spread = P("dp", "head", None)
    placed = (spread,) + (P("dp", None),) * 4 + (P("dp"),) * 4 + (spread,)
    return jax.shard_map(
        local,
        mesh=mesh,
        in_specs=placed,
        out_specs=(spread, spread) + (P("dp", None),) * 4 + (P("dp"),) * 4,
        check_vma=False,
    )
```

```python
import functools

import jax
import jax.numpy as jnp
from jax import lax
from jax.experimental import pallas as pl
from jax.experimental.pallas import tpu as pltpu
from jax.sharding import PartitionSpec as P

HEADS = 12
HEAD_DIM = 64
SEQ = 1024
EPSILON = 1e-05
BOTH = ("dp", "head")
BLOCK = 256
GELU_A = 0.7978845608028654
GELU_B = 0.044715
F32 = jnp.float32
BF16 = jnp.bfloat16


def params(mebi):
    return pltpu.CompilerParams(vmem_limit_bytes=mebi * 2**20)


def dot_nn(left, right):
    return lax.dot_general(left, right, (((1,), (0,)), ((), ())), preferred_element_type=F32)


def dot_nt(left, right):
    return lax.dot_general(left, right, (((1,), (1,)), ((), ())), preferred_element_type=F32)


def dot_tn(left, right):
    return lax.dot_general(left, right, (((0,), (0,)), ((), ())), preferred_element_type=F32)


def cost(micros):
    return pl.CostEstimate(
        flops=int(micros * 1.1e9), bytes_accessed=int(micros * 3e6), transcendentals=0
    )


def whole(*shape):
    return pl.BlockSpec(shape, lambda *_: (0,) * len(shape))


def part_of(pair, which):
    parts, _, count, dim = pair.shape
    return pl.BlockSpec((parts, 1, count, dim), lambda *_: (0, which, 0, 0))


def part_rows(pair, which):
    _, _, count, dim = pair.shape
    return pl.BlockSpec((1, 1, count, dim), lambda i, *_: (i, which, 0, 0))


def rows(count, width):
    return pl.BlockSpec((count, width), lambda i, *_: (i, 0))


def shaped(shape, dtype):
    return jax.ShapeDtypeStruct(shape, dtype)


def normalise(vector):
    centred = vector - jnp.mean(vector, axis=-1, keepdims=True)
    inverse = lax.rsqrt(jnp.mean(centred * centred, axis=-1, keepdims=True) + EPSILON)
    return centred * inverse, inverse


def norm_back(unit, inverse, gain, grad):
    scaled = grad * gain
    return inverse * (
        scaled
        - jnp.mean(scaled, axis=-1, keepdims=True)
        - unit * jnp.mean(scaled * unit, axis=-1, keepdims=True)
    )


def proj_kernel(core_ref, x_ref, am_ref, at_ref, pm_ref, pt_ref, table_ref, mid_ref, low_ref, total):
    half = am_ref.shape[1]
    mine = pl.multiple_of(core_ref[0] * half, half)
    theirs = pl.multiple_of((1 - core_ref[0]) * half, half)
    a_mine, a_theirs = am_ref[...], at_ref[...]
    for place, weight in ((mine, pm_ref), (theirs, pt_ref)):
        total[:, pl.ds(place, half)] = (
            x_ref[0, 0, :, pl.ds(place, half)].astype(F32)
            + dot_nn(a_mine, weight[pl.ds(mine, half), :])
            + dot_nn(a_theirs, weight[pl.ds(theirs, half), :])
        )
    mid_ref[...] = total[...].astype(BF16)
    unit, _ = normalise(total[...])
    low_ref[...] = (unit * table_ref[2:3] + table_ref[3:4]).astype(BF16)


def proj_spec(dim):
    half = dim // 2
    return pl.BlockSpec((dim, half), lambda i, *_: (0, 4))


def project(core, x, a_mine, a_theirs, w_mine, w_theirs, table):
    tok, dim = SEQ, x.shape[-1]
    half = dim // 2
    return pl.pallas_call(
        proj_kernel,
        grid_spec=pltpu.PrefetchScalarGridSpec(
            num_scalar_prefetch=1,
            grid=(tok // BLOCK,),
            in_specs=[part_rows(x, 0), rows(BLOCK, half), rows(BLOCK, half)]
            + [proj_spec(dim), proj_spec(dim), whole(8, dim)],
            out_specs=[rows(BLOCK, dim), rows(BLOCK, dim)],
            scratch_shapes=[pltpu.VMEM((BLOCK, dim), F32)],
        ),
        out_shape=[shaped((tok, dim), BF16), shaped((tok, dim), BF16)],
        compiler_params=params(58),
        cost_estimate=cost(0.01),
    )(core, x, a_mine, a_theirs, w_mine, w_theirs, table)


def middle_kernel(
    core_ref, mid_ref, back_ref, cot_ref, table_ref, pm_ref, pt_ref, am_ref, at_ref,
    grad_ref, gm_ref, gt_ref, wm_ref, wt_ref, norm_ref, heads, branch,
):
    half = am_ref.shape[1]
    step = pl.program_id(0)
    mine = pl.multiple_of(core_ref[0] * half, half)
    theirs = pl.multiple_of((1 - core_ref[0]) * half, half)
    here = pl.ds(pl.multiple_of(step * BLOCK, BLOCK), BLOCK)

    @pl.when(step == 0)
    def _():
        norm_ref[...] = jnp.zeros_like(norm_ref)

    unit, inverse = normalise(mid_ref[...].astype(F32))
    grad = back_ref[...].astype(F32)
    norm_ref[0:1] += jnp.sum(grad * unit, axis=0, keepdims=True)
    norm_ref[1:2] += jnp.sum(grad, axis=0, keepdims=True)
    back = norm_back(unit, inverse, table_ref[2:3], grad)
    grad_ref[...] = (cot_ref[0, 0].astype(F32) + back).astype(BF16)
    branch[here, :half] = grad_ref[:, pl.ds(mine, half)]
    branch[here, half:] = grad_ref[:, pl.ds(theirs, half)]
    heads[here, :half] = am_ref[...]
    heads[here, half:] = at_ref[...]
    for place, out in ((mine, gm_ref), (theirs, gt_ref)):
        out[...] = (
            dot_nt(branch[here, :half], pm_ref[pl.ds(place, half), :])
            + dot_nt(branch[here, half:], pt_ref[pl.ds(place, half), :])
        ).astype(BF16)

    @pl.when(step == pl.num_programs(0) - 1)
    def _():
        for place, start in ((mine, 0), (theirs, half)):
            total = dot_tn(heads[:, start : start + half], branch[...]).astype(BF16)
            wm_ref[pl.ds(place, half), :] = total[:, :half]
            wt_ref[pl.ds(place, half), :] = total[:, half:]


def middle_back(core, middle, back, cot, table, w_mine, w_theirs, a_mine, a_theirs):
    tok, dim = middle.shape
    half = dim // 2
    return pl.pallas_call(
        middle_kernel,
        grid_spec=pltpu.PrefetchScalarGridSpec(
            num_scalar_prefetch=1,
            grid=(tok // BLOCK,),
            in_specs=[rows(BLOCK, dim), rows(BLOCK, dim), part_rows(cot, 1)]
            + [whole(8, dim), proj_spec(dim), proj_spec(dim)]
            + [rows(BLOCK, half)] * 2,
            out_specs=[rows(BLOCK, dim), rows(BLOCK, half), rows(BLOCK, half)]
            + [whole(dim, half), whole(dim, half), whole(8, dim)],
            scratch_shapes=[pltpu.VMEM((tok, dim), BF16)] * 2,
        ),
        out_shape=[shaped((tok, dim), BF16)]
        + [shaped((tok, half), BF16)] * 2
        + [shaped((dim, half), BF16)] * 2
        + [shaped((8, dim), F32)],
        compiler_params=params(58),
        cost_estimate=cost(0.01),
    )(core, middle, back, cot, table, w_mine, w_theirs, a_mine, a_theirs)


def lane_low(count):
    return lax.broadcasted_iota(jnp.int32, (count, 128), 1) < HEAD_DIM


def upper():
    return lax.broadcasted_iota(jnp.int32, (BLOCK, BLOCK), 0) <= lax.broadcasted_iota(
        jnp.int32, (BLOCK, BLOCK), 1
    )


def keep_head(low_lanes, head, value):
    zero = jnp.zeros((), value.dtype)
    return jnp.where(low_lanes, value, zero) if head == 0 else jnp.where(low_lanes, zero, value)


def attend_kernel(first, *refs):
    if first:
        x_ref, w_ref, tail_ref, low_ref, mixed_ref, o_ref, l_ref, table_ref = refs
    else:
        low_ref, w_ref, mixed_ref, o_ref, l_ref = refs
    seq = mixed_ref.shape[0]

    if first:

        @pl.when(pl.program_id(0) == 0)
        def _():
            table_ref[...] = tail_ref[...].astype(F32).T[:8]
            for start in range(0, seq, BLOCK):
                here = pl.ds(start, BLOCK)
                unit, _ = normalise(x_ref[start // BLOCK, 0].astype(F32))
                low_ref[here, :] = (unit * table_ref[0:1] + table_ref[1:2]).astype(BF16)

    mixed_ref[...] = dot_nn(low_ref[...], w_ref[...]).astype(BF16)
    q_ref, k_ref, v_ref = (mixed_ref.at[:, 128 * i : 128 * (i + 1)] for i in range(3))
    low_lanes = lane_low(BLOCK)
    allowed = upper()
    scaling = jnp.asarray(HEAD_DIM**-0.5, BF16)
    tiles = [(block, head) for block in range(seq // BLOCK) for head in range(2)]
    with_ones = jnp.concatenate([v_ref[...], jnp.ones((seq, 128), BF16)], axis=1)

    def score(block, head):
        end = (block + 1) * BLOCK
        queries = keep_head(low_lanes, head, q_ref[block * BLOCK : end, :] * scaling)
        raw = dot_nt(k_ref[:end, :], queries)
        last = jnp.where(allowed, raw[end - BLOCK :, :], -1e30)
        return jnp.concatenate([raw[: end - BLOCK, :], last], axis=0) if block else last

    ahead = 3
    waiting = [score(*tile) for tile in tiles[:ahead]]
    parts = []
    for step, (block, head) in enumerate(tiles):
        end = (block + 1) * BLOCK
        if step + ahead < len(tiles):
            waiting.append(score(*tiles[step + ahead]))
        scores = waiting.pop(0)
        row_max = jnp.max(scores, axis=0, keepdims=True)
        weights = jnp.exp(scores - row_max).astype(BF16)
        summed = dot_tn(weights, with_ones[:end])
        totals = summed[:, 128:]
        parts.append(summed[:, :128] / totals)
        l_ref[0, head : head + 1, block * BLOCK : end] = row_max + jnp.log(totals.T[0:1, :])
        if head == 1:
            o_ref[block * BLOCK : end, :] = jnp.where(low_lanes, parts[-2], parts[-1]).astype(BF16)


def columns(count, width):
    return pl.BlockSpec((count, width), lambda i, *_: (0, i))


def attend(value, weight, pairs, first):
    seq, dim = SEQ, value.shape[-1]
    group = 3 * 128
    tail = pl.BlockSpec((dim, 128), lambda i: (0, 3 * pairs))
    return pl.pallas_call(
        functools.partial(attend_kernel, first),
        grid=(pairs,),
        in_specs=[part_of(value, 0) if first else whole(seq, dim), columns(dim, group)]
        + ([tail] if first else []),
        out_specs=([whole(seq, dim)] if first else [])
        + [columns(seq, group), columns(seq, 128), pl.BlockSpec((1, 2, seq), lambda i: (i, 0, 0))]
        + ([whole(8, dim)] if first else []),
        out_shape=([shaped((seq, dim), BF16)] if first else [])
        + [shaped((seq, pairs * group), BF16), shaped((seq, pairs * 128), BF16)]
        + [shaped((pairs, 2, seq), F32)]
        + ([shaped((8, dim), F32)] if first else []),
        compiler_params=params(58),
        cost_estimate=cost(0.01),
    )(value, weight, *((weight,) if first else ()))


def attend_back_kernel(carry, final, part, *refs):
    if part:
        where_ref, *refs = refs
    mixed_ref, do_ref, o_ref, l_ref, low_ref, w_ref, *refs = refs
    if carry:
        grad_in, *refs = refs
    if final:
        x_ref, mid_ref, table_ref, norm_two, *refs = refs
    if part:
        core_ref, core_more, gp_ref, gp_core, *refs = refs
        left_out, left_keep, right_out, right_keep, *refs = refs
    else:
        gq_ref, more_ref, *refs = refs
    if final:
        out_ref, norm_ref, *refs = refs
    else:
        grad_ref, *refs = refs
    sum_k, sum_v, both, every, *sums = refs
    q_ref, k_ref, v_ref = (mixed_ref.at[:, 128 * i : 128 * (i + 1)] for i in range(3))
    dq_ref, dk_ref, dv_ref = (both.at[:, 128 * i : 128 * (i + 1)] for i in range(3))
    seq = mixed_ref.shape[0]
    step = pl.program_id(0)
    low_lanes = lane_low(BLOCK)
    low_all = lane_low(seq)
    allowed = upper()
    scaling = jnp.asarray(HEAD_DIM**-0.5, BF16)
    head_keys = [keep_head(low_all, head, k_ref[...]) for head in range(2)]
    tiles = [(block, head) for block in reversed(range(seq // BLOCK)) for head in range(2)]

    def scored(block, head):
        start, end = block * BLOCK, (block + 1) * BLOCK
        q_head = keep_head(low_lanes, head, q_ref[start:end, :] * scaling)
        g_head = keep_head(low_lanes, head, do_ref[start:end, :])
        return q_head, g_head, dot_nt(k_ref[:end, :], q_head), dot_nt(v_ref[:end, :], g_head)

    ahead = 2
    waiting = [scored(*tile) for tile in tiles[:ahead]]
    for number, (block, head) in enumerate(tiles):
        start, end = block * BLOCK, (block + 1) * BLOCK
        if number + ahead < len(tiles):
            waiting.append(scored(*tiles[number + ahead]))
        q_head, g_head, scores, grad_probs = waiting.pop(0)
        if head == 0:
            dots = (do_ref[start:end, :].astype(F32) * o_ref[start:end, :].astype(F32)).T
        centre = jnp.sum(dots[HEAD_DIM * head : HEAD_DIM * (head + 1)], axis=0, keepdims=True)
        probs = jnp.exp(scores - l_ref[0, head : head + 1, start:end])
        last = jnp.where(allowed, probs[start:, :], 0.0)
        probs = jnp.concatenate([probs[:start, :], last], axis=0) if block else last
        grad_scores = (probs * (grad_probs - centre)).astype(BF16)
        terms = (
            dot_tn(grad_scores, head_keys[head][:end]),
            dot_nn(grad_scores, q_head),
            dot_nn(probs.astype(BF16), g_head),
        )
        if head == 0:
            add_q, add_k, add_v = terms
            continue
        add_q, add_k, add_v = add_q + terms[0], add_k + terms[1], add_v + terms[2]
        dq_ref[start:end, :] = (add_q * HEAD_DIM**-0.5).astype(BF16)
        if end == seq:
            sum_k[...] = add_k
            sum_v[...] = add_v
        else:
            sum_k[:end, :] += add_k
            sum_v[:end, :] += add_v
    dk_ref[...] = sum_k[...].astype(BF16)
    dv_ref[...] = sum_v[...].astype(BF16)

    here = pl.ds(pl.multiple_of(step * 384, 384), 384)
    grad_qkv = dot_tn(low_ref[...], both[...]).astype(BF16)
    every[:, here] = both[...]

    def cut(out, keep, columns, source, size, index):
        for block in range(source.shape[0] // (2 * size)):
            to = pl.ds(block * size, size)
            for ref, side in ((out, 1 - index), (keep, index)):
                start = pl.multiple_of(block * 2 * size + side * size, 16)
                ref[to, columns] = source[pl.ds(start, size), :]

    @pl.when(step < pl.num_programs(0) - 1)
    def _():
        if part:
            sums[0][...] = (grad_qkv.astype(F32) + core_ref[:, here].astype(F32)).astype(BF16)
            cut(left_out, left_keep, here, sums[0], part, where_ref[0])
        else:
            gq_ref[:, here] = grad_qkv

    @pl.when(step == pl.num_programs(0) - 1)
    def _():
        if part:
            sums[1][:, :384] = (
                grad_qkv.astype(F32) + core_more[:, :384].astype(F32)
            ).astype(BF16)
        else:
            more_ref[:, :384] = grad_qkv


    @pl.when(step == pl.num_programs(0) - 1)
    def _():
        if final:
            norm_ref[...] = jnp.zeros_like(norm_ref)
        for start in range(0, seq, BLOCK):
            here = pl.ds(start, BLOCK)
            grad = dot_nt(every[here, :], w_ref[...])
            if carry:
                grad = grad + grad_in[here, :].astype(F32)
            if not final:
                grad_ref[here, :] = grad.astype(BF16)
                continue
            unit, inverse = normalise(x_ref[start // BLOCK, 0].astype(F32))
            norm_ref[0:1] += jnp.sum(grad * unit, axis=0, keepdims=True)
            norm_ref[1:2] += jnp.sum(grad, axis=0, keepdims=True)
            back = norm_back(unit, inverse, table_ref[0:1], grad)
            out_ref[here, :] = (mid_ref[here, :].astype(F32) + back).astype(BF16)
        tail = jnp.zeros((128, low_ref.shape[1]), F32)
        if final:
            tail = jnp.concatenate([norm_ref[:2], norm_two[:2], tail[4:]], axis=0)
        if part:
            sums[1][:, 384:512] = (tail.T + core_more[:, 384:].astype(F32)).astype(BF16)
            sums[1][:, 512:] = (gp_ref[...].astype(F32) + gp_core[...].astype(F32)).astype(BF16)
            cut(right_out, right_keep, slice(None), sums[1], 2 * part, where_ref[1])
        else:
            more_ref[:, 384:] = tail.T.astype(BF16)


def attend_back(
    mixed, grad, attended, logs, low, weight, pairs, carry=None, final=(), where=None, others=(), part=0
):
    seq, dim = low.shape
    group = 3 * 128
    wide = pairs * group

    def column(width):
        return pl.BlockSpec((seq, width), lambda i, *_: (0, i))

    more = [whole(seq, dim)] if carry is not None else []
    more += [part_of(final[0], 0), whole(seq, dim), whole(8, dim), whole(8, dim)] if final else []
    more += [whole(*other.shape) for other in others]
    widths = [wide - group, group + 128]
    outs = [(dim, width) for width in widths]
    scratch = [pltpu.VMEM((seq, 128), F32)] * 2
    scratch += [pltpu.VMEM((seq, group), BF16), pltpu.VMEM((seq, wide), BF16)]
    if part:
        widths[1] += others[2].shape[1]
        outs = [(dim // 2, width) for width in widths for _ in range(2)]
        scratch += [pltpu.VMEM((dim, group), BF16), pltpu.VMEM((dim, widths[1]), BF16)]
    return pl.pallas_call(
        functools.partial(attend_back_kernel, carry is not None, bool(final), part),
        grid_spec=pltpu.PrefetchScalarGridSpec(
            num_scalar_prefetch=1 if part else 0,
            grid=(pairs,),
            in_specs=[column(group), column(128), column(128)]
            + [pl.BlockSpec((1, 2, seq), lambda i, *_: (i, 0, 0)), whole(seq, dim)]
            + [whole(dim, wide)]
            + more,
            out_specs=[whole(*shape) for shape in outs]
            + [whole(seq, dim)]
            + ([whole(8, dim)] if final else []),
            scratch_shapes=scratch,
        ),
        out_shape=[shaped(shape, BF16) for shape in outs]
        + [shaped((seq, dim), BF16)]
        + ([shaped((8, dim), F32)] if final else []),
        compiler_params=params(58),
        cost_estimate=cost(0.01),
    )(
        *((where,) if part else ()),
        mixed,
        grad,
        attended,
        logs,
        low,
        weight,
        *(() if carry is None else (carry,)),
        *final,
        *others,
    )


def ffn_kernel(final, paired, *refs):
    low_ref, cot_ref, up_ref, down_ref, out_in = refs[:5]
    back_in = refs[5] if final else None
    out_ref, back_ref, gu_ref, gd_ref, out_sum, back_sum, act, hid = refs[5 + final :]

    def chunk(first):
        up, down = up_ref[...], down_ref[...]
        for start in range(0, low_ref.shape[0], BLOCK):
            here = pl.ds(start, BLOCK)
            hidden = dot_nn(low_ref[here, :], up)
            grad_active = dot_nt(cot_ref[start // BLOCK, 0], down)
            square = hidden * hidden
            bend = jnp.tanh(hidden * (GELU_A + (GELU_A * GELU_B) * square))
            gate = 0.5 + 0.5 * bend
            active = (hidden * gate).astype(BF16)
            slope = gate + hidden * (0.5 - 0.5 * bend * bend) * (
                GELU_A + (3 * GELU_A * GELU_B) * square
            )
            grad_hidden = (grad_active * slope).astype(BF16)
            act[here, :] = active
            hid[here, :] = grad_hidden
            add_out, add_back = dot_nn(active, down), dot_nt(grad_hidden, up)
            if first:
                out_sum[here, :] = add_out
                back_sum[here, :] = add_back
            else:
                total = out_sum[here, :] + add_out + out_in[here, :].astype(F32)
                out_ref[here, :] = total.astype(out_ref.dtype)
                total = back_sum[here, :] + add_back
                if final:
                    total = total + back_in[here, :].astype(F32)
                back_ref[here, :] = total.astype(BF16)
        gu_ref[...] = dot_tn(low_ref[...], hid[...]).astype(BF16)
        cot = cot_ref[...].reshape(act.shape[0], -1)
        grad_down = dot_tn(act[...], cot).astype(BF16)
        if paired:
            dim = grad_down.shape[1]
            grad_down = grad_down.reshape(-1, 2 * paired, dim)
            for side in range(2):
                gd_ref[:, side * dim : (side + 1) * dim] = grad_down[
                    :, side * paired : (side + 1) * paired
                ].reshape(-1, dim)
        else:
            gd_ref[...] = grad_down

    for place in range(2):

        @pl.when(pl.program_id(0) == place)
        def _(place=place):
            chunk(place == 0)


def feed_forward(low, pair, up, down, out_in, part, back_in=None):
    tok, dim = low.shape
    final = back_in is not None
    wide = down.shape[0]
    chunk = wide // 2
    paired = part if part % 16 == 0 else 0
    tall, long = (chunk // 2, 2 * dim) if paired else (chunk, dim)
    outs = pl.pallas_call(
        functools.partial(ffn_kernel, int(final), paired),
        grid=(2,),
        in_specs=[whole(tok, dim), part_of(pair, 1), columns(dim, chunk), rows(chunk, dim)]
        + [whole(tok, dim)] * (2 if final else 1),
        out_specs=[whole(tok, dim), whole(tok, dim), columns(dim, chunk), rows(tall, long)],
        out_shape=[shaped((tok, dim), BF16 if final else F32), shaped((tok, dim), BF16)]
        + [shaped((dim, wide), BF16), shaped((2 * tall, long), BF16)],
        scratch_shapes=[pltpu.VMEM((tok, dim), F32)] * 2 + [pltpu.VMEM((tok, chunk), BF16)] * 2,
        compiler_params=params(58),
        cost_estimate=cost(0.01),
    )(low, pair, up, down, out_in, *((back_in,) if final else ()))
    if paired:
        return outs
    grad_down = outs[3].reshape(-1, 2, part, dim).transpose(0, 2, 1, 3).reshape(-1, 2 * dim)
    return list(outs[:3]) + [grad_down]


def spread_kernel(widths, where_ref, *refs):
    del where_ref
    count = len(refs) // (2 * len(widths) + 1)
    ins, outs = refs[: 2 * len(widths) * count], refs[2 * len(widths) * count :]
    position = 0
    for out in outs:
        start = 0
        for width in widths:
            total = ins[position][0].astype(F32) + ins[position + 1][0].astype(F32)
            out[:, start : start + width] = total.astype(BF16)
            start += width
            position += 2


def spread(where, *items):
    z_count, part = items[0][0].shape[:2]
    widths = [item[0].shape[-1] for item in items]
    arrays, in_specs = [], []
    for step in range(z_count):
        for item in items:
            spec = pl.BlockSpec(
                (1, part, item[0].shape[-1]),
                lambda i, where_ref, step=step: ((where_ref[0] + step) % z_count, 0, 0),
            )
            arrays += item
            in_specs += [spec, spec]
    return pl.pallas_call(
        functools.partial(spread_kernel, widths),
        grid_spec=pltpu.PrefetchScalarGridSpec(
            num_scalar_prefetch=1,
            grid=(1,),
            in_specs=in_specs,
            out_specs=[pl.BlockSpec((part, sum(widths)), lambda i, _: (0, 0))] * z_count,
        ),
        out_shape=[shaped((part, sum(widths)), BF16)] * z_count,
        compiler_params=params(58),
        cost_estimate=cost(0.01),
    )(where, *arrays)


def by_place(where_ref, refs):
    x, c = where_ref[0], where_ref[1]
    own, other_x, other_c, other_both = (ref[...] for ref in refs)
    low_x = [jnp.where(x == 0, own, other_x), jnp.where(x == 0, other_c, other_both)]
    high_x = [jnp.where(x == 0, other_x, own), jnp.where(x == 0, other_both, other_c)]
    return [
        [jnp.where(c == 0, side[0], side[1]) for side in (low_x, high_x)],
        [jnp.where(c == 0, side[1], side[0]) for side in (low_x, high_x)],
    ]


def finish_ffn(fan, where_ref, all_ref, up_ref, down_ref):
    part, dim = all_ref.shape[2], down_ref.shape[1]
    count = up_ref.shape[1] // fan // 2
    for core in range(2):
        for side in range(2):
            here = slice(side * part, (side + 1) * part)
            for block in range(count):
                place = (2 * block + core) * fan
                up_ref[here, place : place + fan] = all_ref[
                    core, side, :, block * fan : (block + 1) * fan
                ].astype(F32)
            start = count * fan
            for half in range(2):
                place = core * fan + side * fan // 2 + half * part
                down_ref[place : place + part, :] = all_ref[
                    core, side, :, start + half * dim : start + (half + 1) * dim
                ].astype(F32)


def finish_qkv(pairs, where_ref, *refs):
    pieces, (qkv_ref, proj_ref, *norm_refs) = by_place(where_ref, refs[:4]), refs[4:]
    part, dim = refs[0].shape[0], qkv_ref.shape[1] // 3
    sums = []
    for side in range(2):
        here = slice(side * part, (side + 1) * part)
        for core in range(2):
            piece = pieces[core][side]
            for pair in range(pairs):
                for which in range(3):
                    place = which * dim + core * dim // 2 + pair * 128
                    start = (pair * 3 + which) * 128
                    qkv_ref[here, place : place + 128] = piece[:, start : start + 128].astype(F32)
            start = pairs * 384 + 128
            proj_ref[here, core * dim // 2 : (core + 1) * dim // 2] = piece[:, start:].astype(F32)
        norms = slice(pairs * 384, pairs * 384 + 128)
        sums.append(
            pieces[0][side][:, norms].astype(F32) + pieces[1][side][:, norms].astype(F32)
        )
    sums = jnp.concatenate(sums, axis=0).T
    for place, norm_ref in enumerate(norm_refs):
        norm_ref[...] = sums[place : place + 1].reshape(norm_ref.shape)


def settle_kernel(in_ref, out_ref):
    out_ref[...] = in_ref[...]


def settle(value):
    spec = pl.BlockSpec((1,) + value.shape[1:], lambda i: (i, 0, 0))
    return pl.pallas_call(
        settle_kernel,
        grid=value.shape[:1],
        in_specs=[spec],
        out_specs=spec,
        out_shape=shaped(value.shape, value.dtype),
        cost_estimate=cost(0.01),
    )(value)


def finish(kernel, where, pieces, *shapes):
    return pl.pallas_call(
        kernel,
        grid_spec=pltpu.PrefetchScalarGridSpec(
            num_scalar_prefetch=1,
            grid=(1,),
            in_specs=[whole(*piece.shape) for piece in pieces],
            out_specs=[whole(*shape) for shape in shapes],
        ),
        out_shape=[shaped(shape, F32) for shape in shapes],
        compiler_params=params(58),
        cost_estimate=cost(0.01),
    )(where, *pieces)


class Grid:
    def __init__(self):
        self.z_count = lax.axis_size("dp") // 2
        self.dp, self.head = lax.axis_index("dp"), lax.axis_index("head")
        self.z, self.y, self.x, self.c = self.dp // 2, self.dp % 2, self.head // 2, self.head % 2
        assert lax.axis_size("head") == 4 and lax.axis_size("dp") % 2 == 0

    def send(self, value, z=0, y=0, x=0, c=0):
        pairs = []
        for source in range(self.z_count * 8):
            zi, yi, xi, ci = source // 8, source // 4 % 2, source // 2 % 2, source % 2
            zt, yt, xt, ct = (zi + z) % self.z_count, yi ^ y, xi ^ x, ci ^ c
            pairs.append((source, ((zt * 2 + yt) * 2 + xt) * 2 + ct))
        return lax.ppermute(value, BOTH, pairs)

    def pick(self, value, axis, index):
        return lax.dynamic_index_in_dim(value, index, axis, keepdims=False)

    def join(self, mine, other, index, axis):
        shape = mine.shape[:axis] + (2,) + mine.shape[axis:]
        here = lax.broadcasted_iota(jnp.int32, shape, axis) == index
        mine, other = (jnp.broadcast_to(jnp.expand_dims(v, axis), shape) for v in (mine, other))
        return jnp.where(here, mine, other)

    def to_z(self, piece):
        return [piece] + [self.send(piece, z=step) for step in range(1, self.z_count)]

    def by_z(self, got):
        shape = (self.z_count,) + got[0].shape
        steps = (self.z - lax.broadcasted_iota(jnp.int32, shape, 0)) % self.z_count
        out = jnp.broadcast_to(got[0], shape)
        for step in range(1, self.z_count):
            out = jnp.where(steps == step, jnp.broadcast_to(got[step], shape), out)
        return out

    def over_z(self, piece):
        copies = jnp.broadcast_to(piece, (self.z_count,) + piece.shape)
        groups = [list(range(y, self.z_count * 2, 2)) for y in range(2)]
        return lax.all_to_all(
            copies, "dp", split_axis=0, concat_axis=0, tiled=True, axis_index_groups=groups
        )

    def over_y(self, value, got):
        return self.join(value, got, self.y, 1)

    def over_x(self, value, got, axis):
        return self.join(value, got, self.x, axis)

    def halves(self, name, values):
        axis, index = (1, self.y) if name == "y" else (values[0].ndim - 3, self.x)
        low, high = (
            sum(lax.index_in_dim(v, place, axis, False).astype(F32) for v in values).astype(BF16)
            for place in range(2)
        )
        return jnp.where(index == 0, high, low), jnp.where(index == 0, low, high)

    def by_block(self, *values):
        totals = [keep.astype(F32) + got.astype(F32) for keep, got in values]
        return [
            jnp.concatenate(
                [self.pick(total, 0, (self.z + step) % self.z_count) for total in totals], axis=-1
            ).astype(BF16)
            for step in range(self.z_count)
        ]

    def end(self, parts):
        return self.total(
            [parts[0]] + [self.send(part, z=step) for step, part in enumerate(parts) if step]
        )

    def total(self, parts):
        return sum(value.astype(F32) for value in parts).astype(BF16)

    def share(self, piece):
        return [piece, self.send(piece, x=1), self.send(piece, c=1), self.send(piece, x=1, c=1)]

    def share_all(self, piece):
        both = self.join(piece, self.send(piece, x=1), self.x, 0)
        return self.join(both, self.send(both, c=1), self.c, 0)


def exchange(value):
    return lax.all_to_all(value, "head", split_axis=0, concat_axis=0, tiled=True)


def after(value, *done):
    return lax.optimization_barrier((value, done))[0]


def flat(value):
    return value.reshape(-1, value.shape[-1])


def local(
    tokens,
    qkv_weight,
    proj_weight,
    up_weight,
    down_weight,
    attn_gain,
    attn_bias,
    ffn_gain,
    ffn_bias,
    cotangent,
):
    grid = Grid()
    dim = tokens.shape[-1]
    share = qkv_weight.shape[0]
    part = share // 2
    half = dim // 2
    pairs = half // 128
    hidden = up_weight.shape[1]
    dp_count = lax.axis_size("dp")
    fan = hidden // dp_count // 2
    core = grid.c.reshape(1).astype(jnp.int32)
    assert tokens.shape[0] == 4 and tokens.shape[1] * 4 == SEQ
    assert fan == 4 * part

    def row_half(value):
        return lax.dynamic_slice_in_dim(value, grid.x * part, part, 0)

    qkv = grid.pick(qkv_weight.reshape(share, 3, 2, pairs, 128), 2, grid.c)
    qkv = qkv.transpose(0, 2, 1, 3).reshape(share, -1)
    table = jnp.stack([attn_gain, attn_bias, ffn_gain, ffn_bias], axis=1)
    table = jnp.pad(table, ((0, 0), (0, 124)))
    piece = jnp.concatenate([qkv, table], axis=1).astype(BF16)
    up = grid.pick(row_half(up_weight).reshape(part, dp_count, 2, fan), 2, grid.c)
    proj = grid.pick(row_half(proj_weight).reshape(part, 2, half), 1, grid.c)
    up_piece = jnp.concatenate([up.reshape(part, -1), proj], axis=1).astype(BF16)
    down_piece = grid.pick(down_weight.reshape(2, fan, dim), 0, grid.c).astype(BF16)
    where = jnp.stack([grid.x, grid.y]).astype(jnp.int32)
    where_head = jnp.stack([grid.x, grid.c]).astype(jnp.int32)

    both = exchange(after(jnp.stack([tokens, cotangent], axis=1), piece))
    first_z = grid.by_z(after(grid.to_z(piece), up_piece, down_piece))
    up_got = grid.to_z(after(up_piece, first_z))
    w_mine = flat(grid.over_y(first_z, after(grid.send(first_z, y=1), up_got)))
    w_theirs = grid.send(w_mine, c=1)
    up_z = grid.by_z(after(up_got, w_mine))
    up_y = grid.send(up_z, y=1)
    up_x = grid.send(up_z, x=1)
    down_both = grid.join(
        down_piece, grid.send(after(down_piece, up_got), y=1), grid.y, 0
    )
    down_mine = grid.over_z(after(down_both, both))
    low, mixed_mine, att_mine, log_mine, table = attend(
        after(both, up_z), w_mine, pairs, True
    )
    mixed_theirs, att_theirs, log_theirs = attend(low, w_theirs, pairs, False)
    up_y, up_x = after((up_y, up_x), att_mine, att_theirs)
    up_xy = grid.send(up_y, x=1)
    up_y = grid.over_y(up_z, up_y)
    up_x = grid.over_y(up_x, up_xy)
    up_mine = flat(grid.over_x(up_y, up_x, 2))
    up_theirs = grid.send(up_mine, c=1)
    down_mine = flat(after(down_mine, up_xy))
    down_theirs = grid.send(down_mine, c=1)
    middle, low_two = project(core, both, att_mine, att_theirs, up_mine, up_theirs, table)
    out, back, gu_theirs, gd_theirs = feed_forward(
        low_two, both, up_theirs, after(down_theirs, low_two), middle, part
    )
    gd_core, gu_core = grid.send(gd_theirs, c=1), grid.send(gu_theirs, c=1)
    out, back, gu_mine, gd_mine = feed_forward(low_two, both, up_mine, down_mine, out, part, back)
    gd_core, gu_core = after((gd_core, gu_core), back)

    def blocks(value):
        return value.reshape(grid.z_count, 2, 2, -1, value.shape[-1])

    gd_out, gd_keep = grid.halves("y", [blocks(gd_mine), blocks(gd_core)])
    gd_got = grid.send(gd_out, y=1)
    gu_out, gu_keep = grid.halves("x", [blocks(gu_mine), blocks(after(gu_core, gd_out))])
    gu_got = grid.send(gu_out, x=1)
    grad_middle, ga_mine, ga_theirs, gp_mine, gp_theirs, norm_two = middle_back(
        core, middle, after(back, gd_out, gu_out), both, table, up_mine, up_theirs, att_mine,
        att_theirs,
    )
    gp_core = grid.send(gp_theirs, c=1)
    gq_theirs, gq_rest, grad_low = attend_back(
        mixed_theirs, ga_theirs, att_theirs, log_theirs, low, w_theirs, pairs
    )
    gq_core = [grid.send(value, c=1) for value in (gq_theirs, gq_rest)]
    gd_got, gu_got, gp_core = after((gd_got, gu_got, gp_core), grad_low)
    gd_out, gd_keep = grid.halves("x", [gd_keep, gd_got])
    gd_got = grid.send(gd_out, x=1)
    gu_out, gu_keep = grid.halves("y", [gu_keep, gu_got])
    gu_got = grid.send(gu_out, y=1)
    out_home = exchange(after(out.reshape(4, SEQ // 4, dim), gd_out, gu_out))
    mine = (mixed_mine, after(ga_mine, gd_out, gu_out), att_mine, log_mine, low, w_mine, pairs)
    final = (both, grad_middle, table, norm_two)
    if part % 16 == 0:
        *cuts, grad_x, _ = attend_back(
            *mine, grad_low, final, where, (*gq_core, gp_mine, gp_core), part
        )
        left_out, left_keep, right_out, right_keep = cuts
    else:
        gq_mine, gq_more, grad_x, _ = attend_back(*mine, grad_low, final)
        left_out, left_keep = grid.halves("x", [blocks(gq_mine), blocks(gq_core[0])])
        right_out, right_keep = grid.halves(
            "y",
            [
                jnp.concatenate([blocks(gq_more), blocks(gp_mine)], axis=-1),
                jnp.concatenate([blocks(gq_core[1]), blocks(gp_core)], axis=-1),
            ],
        )
    left_got, right_got = grid.send(left_out, x=1), grid.send(right_out, y=1)
    left_keep, left_got, right_keep, right_got = (
        value.reshape(grid.z_count, 2, part, -1)
        for value in (left_keep, left_got, right_keep, right_got)
    )
    gd_got, gu_got, out_home = after((gd_got, gu_got, out_home), left_out, right_out)
    out_home = settle(out_home)
    ffn_parts = grid.by_block((gu_keep, gu_got), (gd_keep, gd_got))
    left_got, right_got = after((left_got, right_got), ffn_parts, out_home)
    ffn_got = [grid.send(part, z=step) for step, part in enumerate(ffn_parts) if step]
    left_out, left_keep = grid.halves("y", [left_keep, left_got])
    left_got = grid.send(left_out, y=1)
    right_out, right_keep = grid.halves("x", [right_keep, right_got])
    right_got = grid.send(right_out, x=1)
    grad_home = exchange(after(grad_x.reshape(4, SEQ // 4, dim), left_got))
    left_got, right_got = after((left_got, right_got), ffn_got)
    qkv_parts = spread(
        grid.z.reshape(1).astype(jnp.int32), (left_keep, left_got), (right_keep, right_got)
    )
    sum_ffn = after(grid.total([ffn_parts[0], *ffn_got]), qkv_parts)
    ffn_x = grid.send(sum_ffn, x=1)
    qkv_got = [grid.send(part, z=step) for step, part in enumerate(qkv_parts) if step]
    qkv_got, grad_home = after((qkv_got, grad_home), grad_home)
    sum_qkv = grid.total([qkv_parts[0], *qkv_got])
    ffn_x = grid.join(sum_ffn, ffn_x, grid.x, 0)
    all_ffn = grid.join(ffn_x, grid.send(ffn_x, c=1), grid.c, 0)
    shares = grid.share(sum_qkv)
    grad_home = after(grad_home, sum_qkv).astype(F32)
    shard_up, shard_down = finish(
        functools.partial(finish_ffn, fan), where_head, [after(all_ffn, sum_qkv)],
        (share, hidden), (2 * fan, dim),
    )
    shard_qkv, shard_proj, *norms = finish(
        functools.partial(finish_qkv, pairs), where_head, after(shares, shard_up),
        (share, 3 * dim), (share, dim), *[(share,)] * 4,
    )
    return (
        out_home,
        grad_home,
        shard_qkv,
        shard_proj,
        shard_up,
        shard_down,
        norms[0],
        norms[1],
        norms[2],
        norms[3],
    )


def solution(mesh):
    spread = P("dp", "head", None)
    placed = (spread,) + (P("dp", None),) * 4 + (P("dp"),) * 4 + (spread,)
    return jax.shard_map(
        local,
        mesh=mesh,
        in_specs=placed,
        out_specs=(spread, spread) + (P("dp", None),) * 4 + (P("dp"),) * 4,
        check_vma=False,
    )
```

```python
import functools

import jax
import jax.numpy as jnp
from jax import lax
from jax.experimental import pallas as pl
from jax.experimental.pallas import tpu as pltpu
from jax.sharding import PartitionSpec as P

HEADS = 12
HEAD_DIM = 64
SEQ = 1024
EPSILON = 1e-05
BOTH = ("dp", "head")
BLOCK = 256
GELU_A = 0.7978845608028654
GELU_B = 0.044715
F32 = jnp.float32
BF16 = jnp.bfloat16


def params(mebi):
    return pltpu.CompilerParams(vmem_limit_bytes=mebi * 2**20)


def dot_nn(left, right):
    return lax.dot_general(left, right, (((1,), (0,)), ((), ())), preferred_element_type=F32)


def dot_nt(left, right):
    return lax.dot_general(left, right, (((1,), (1,)), ((), ())), preferred_element_type=F32)


def dot_tn(left, right):
    return lax.dot_general(left, right, (((0,), (0,)), ((), ())), preferred_element_type=F32)


def cost(micros):
    return pl.CostEstimate(
        flops=int(micros * 1.1e9), bytes_accessed=int(micros * 3e6), transcendentals=0
    )


def whole(*shape):
    return pl.BlockSpec(shape, lambda *_: (0,) * len(shape))


def part_of(pair, which):
    parts, _, count, dim = pair.shape
    return pl.BlockSpec((parts, 1, count, dim), lambda *_: (0, which, 0, 0))


def part_rows(pair, which):
    _, _, count, dim = pair.shape
    return pl.BlockSpec((1, 1, count, dim), lambda i, *_: (i, which, 0, 0))


def rows(count, width):
    return pl.BlockSpec((count, width), lambda i, *_: (i, 0))


def shaped(shape, dtype):
    return jax.ShapeDtypeStruct(shape, dtype)


def normalise(vector):
    centred = vector - jnp.mean(vector, axis=-1, keepdims=True)
    inverse = lax.rsqrt(jnp.mean(centred * centred, axis=-1, keepdims=True) + EPSILON)
    return centred * inverse, inverse


def norm_back(unit, inverse, gain, grad):
    scaled = grad * gain
    return inverse * (
        scaled
        - jnp.mean(scaled, axis=-1, keepdims=True)
        - unit * jnp.mean(scaled * unit, axis=-1, keepdims=True)
    )


def proj_kernel(core_ref, x_ref, am_ref, at_ref, pm_ref, pt_ref, table_ref, mid_ref, low_ref, total):
    half = am_ref.shape[1]
    mine = pl.multiple_of(core_ref[0] * half, half)
    theirs = pl.multiple_of((1 - core_ref[0]) * half, half)
    a_mine, a_theirs = am_ref[...], at_ref[...]
    for place, weight in ((mine, pm_ref), (theirs, pt_ref)):
        total[:, pl.ds(place, half)] = (
            x_ref[0, 0, :, pl.ds(place, half)].astype(F32)
            + dot_nn(a_mine, weight[pl.ds(mine, half), :])
            + dot_nn(a_theirs, weight[pl.ds(theirs, half), :])
        )
    mid_ref[...] = total[...].astype(BF16)
    unit, _ = normalise(total[...])
    low_ref[...] = (unit * table_ref[2:3] + table_ref[3:4]).astype(BF16)


def proj_spec(dim):
    half = dim // 2
    return pl.BlockSpec((dim, half), lambda i, *_: (0, 4))


def project(core, x, a_mine, a_theirs, w_mine, w_theirs, table):
    tok, dim = SEQ, x.shape[-1]
    half = dim // 2
    return pl.pallas_call(
        proj_kernel,
        grid_spec=pltpu.PrefetchScalarGridSpec(
            num_scalar_prefetch=1,
            grid=(tok // BLOCK,),
            in_specs=[part_rows(x, 0), rows(BLOCK, half), rows(BLOCK, half)]
            + [proj_spec(dim), proj_spec(dim), whole(8, dim)],
            out_specs=[rows(BLOCK, dim), rows(BLOCK, dim)],
            scratch_shapes=[pltpu.VMEM((BLOCK, dim), F32)],
        ),
        out_shape=[shaped((tok, dim), BF16), shaped((tok, dim), BF16)],
        compiler_params=params(58),
        cost_estimate=cost(0.01),
    )(core, x, a_mine, a_theirs, w_mine, w_theirs, table)


def middle_kernel(
    core_ref, mid_ref, back_ref, cot_ref, table_ref, pm_ref, pt_ref, am_ref, at_ref,
    grad_ref, gm_ref, gt_ref, wm_ref, wt_ref, norm_ref, heads, branch,
):
    half = am_ref.shape[1]
    step = pl.program_id(0)
    mine = pl.multiple_of(core_ref[0] * half, half)
    theirs = pl.multiple_of((1 - core_ref[0]) * half, half)
    here = pl.ds(pl.multiple_of(step * BLOCK, BLOCK), BLOCK)

    @pl.when(step == 0)
    def _():
        norm_ref[...] = jnp.zeros_like(norm_ref)

    unit, inverse = normalise(mid_ref[...].astype(F32))
    grad = back_ref[...].astype(F32)
    norm_ref[0:1] += jnp.sum(grad * unit, axis=0, keepdims=True)
    norm_ref[1:2] += jnp.sum(grad, axis=0, keepdims=True)
    back = norm_back(unit, inverse, table_ref[2:3], grad)
    grad_ref[...] = (cot_ref[0, 0].astype(F32) + back).astype(BF16)
    branch[here, :half] = grad_ref[:, pl.ds(mine, half)]
    branch[here, half:] = grad_ref[:, pl.ds(theirs, half)]
    heads[here, :half] = am_ref[...]
    heads[here, half:] = at_ref[...]
    for place, out in ((mine, gm_ref), (theirs, gt_ref)):
        out[...] = (
            dot_nt(branch[here, :half], pm_ref[pl.ds(place, half), :])
            + dot_nt(branch[here, half:], pt_ref[pl.ds(place, half), :])
        ).astype(BF16)

    @pl.when(step == pl.num_programs(0) - 1)
    def _():
        for place, start in ((mine, 0), (theirs, half)):
            total = dot_tn(heads[:, start : start + half], branch[...]).astype(BF16)
            wm_ref[pl.ds(place, half), :] = total[:, :half]
            wt_ref[pl.ds(place, half), :] = total[:, half:]


def middle_back(core, middle, back, cot, table, w_mine, w_theirs, a_mine, a_theirs):
    tok, dim = middle.shape
    half = dim // 2
    return pl.pallas_call(
        middle_kernel,
        grid_spec=pltpu.PrefetchScalarGridSpec(
            num_scalar_prefetch=1,
            grid=(tok // BLOCK,),
            in_specs=[rows(BLOCK, dim), rows(BLOCK, dim), part_rows(cot, 1)]
            + [whole(8, dim), proj_spec(dim), proj_spec(dim)]
            + [rows(BLOCK, half)] * 2,
            out_specs=[rows(BLOCK, dim), rows(BLOCK, half), rows(BLOCK, half)]
            + [whole(dim, half), whole(dim, half), whole(8, dim)],
            scratch_shapes=[pltpu.VMEM((tok, dim), BF16)] * 2,
        ),
        out_shape=[shaped((tok, dim), BF16)]
        + [shaped((tok, half), BF16)] * 2
        + [shaped((dim, half), BF16)] * 2
        + [shaped((8, dim), F32)],
        compiler_params=params(58),
        cost_estimate=cost(0.01),
    )(core, middle, back, cot, table, w_mine, w_theirs, a_mine, a_theirs)


def lane_low(count):
    return lax.broadcasted_iota(jnp.int32, (count, 128), 1) < HEAD_DIM


def upper():
    return lax.broadcasted_iota(jnp.int32, (BLOCK, BLOCK), 0) <= lax.broadcasted_iota(
        jnp.int32, (BLOCK, BLOCK), 1
    )


def keep_head(low_lanes, head, value):
    zero = jnp.zeros((), value.dtype)
    return jnp.where(low_lanes, value, zero) if head == 0 else jnp.where(low_lanes, zero, value)


def attend_kernel(first, *refs):
    if first:
        x_ref, w_ref, tail_ref, low_ref, mixed_ref, o_ref, l_ref, table_ref = refs
    else:
        low_ref, w_ref, mixed_ref, o_ref, l_ref = refs
    seq = mixed_ref.shape[0]

    if first:

        @pl.when(pl.program_id(0) == 0)
        def _():
            table_ref[...] = tail_ref[...].astype(F32).T[:8]
            for start in range(0, seq, BLOCK):
                here = pl.ds(start, BLOCK)
                unit, _ = normalise(x_ref[start // BLOCK, 0].astype(F32))
                low_ref[here, :] = (unit * table_ref[0:1] + table_ref[1:2]).astype(BF16)

    mixed_ref[...] = dot_nn(low_ref[...], w_ref[...]).astype(BF16)
    q_ref, k_ref, v_ref = (mixed_ref.at[:, 128 * i : 128 * (i + 1)] for i in range(3))
    low_lanes = lane_low(BLOCK)
    allowed = upper()
    scaling = jnp.asarray(HEAD_DIM**-0.5, BF16)
    tiles = [(block, head) for block in range(seq // BLOCK) for head in range(2)]
    with_ones = jnp.concatenate([v_ref[...], jnp.ones((seq, 128), BF16)], axis=1)

    def score(block, head):
        end = (block + 1) * BLOCK
        queries = keep_head(low_lanes, head, q_ref[block * BLOCK : end, :] * scaling)
        raw = dot_nt(k_ref[:end, :], queries)
        last = jnp.where(allowed, raw[end - BLOCK :, :], -1e30)
        return jnp.concatenate([raw[: end - BLOCK, :], last], axis=0) if block else last

    ahead = 3
    waiting = [score(*tile) for tile in tiles[:ahead]]
    parts = []
    for step, (block, head) in enumerate(tiles):
        end = (block + 1) * BLOCK
        if step + ahead < len(tiles):
            waiting.append(score(*tiles[step + ahead]))
        scores = waiting.pop(0)
        row_max = jnp.max(scores, axis=0, keepdims=True)
        weights = jnp.exp(scores - row_max).astype(BF16)
        summed = dot_tn(weights, with_ones[:end])
        totals = summed[:, 128:]
        parts.append(summed[:, :128] / totals)
        l_ref[0, head : head + 1, block * BLOCK : end] = row_max + jnp.log(totals.T[0:1, :])
        if head == 1:
            o_ref[block * BLOCK : end, :] = jnp.where(low_lanes, parts[-2], parts[-1]).astype(BF16)


def columns(count, width):
    return pl.BlockSpec((count, width), lambda i, *_: (0, i))


def attend(value, weight, pairs, first):
    seq, dim = SEQ, value.shape[-1]
    group = 3 * 128
    tail = pl.BlockSpec((dim, 128), lambda i: (0, 3 * pairs))
    return pl.pallas_call(
        functools.partial(attend_kernel, first),
        grid=(pairs,),
        in_specs=[part_of(value, 0) if first else whole(seq, dim), columns(dim, group)]
        + ([tail] if first else []),
        out_specs=([whole(seq, dim)] if first else [])
        + [columns(seq, group), columns(seq, 128), pl.BlockSpec((1, 2, seq), lambda i: (i, 0, 0))]
        + ([whole(8, dim)] if first else []),
        out_shape=([shaped((seq, dim), BF16)] if first else [])
        + [shaped((seq, pairs * group), BF16), shaped((seq, pairs * 128), BF16)]
        + [shaped((pairs, 2, seq), F32)]
        + ([shaped((8, dim), F32)] if first else []),
        compiler_params=params(58),
        cost_estimate=cost(0.01),
    )(value, weight, *((weight,) if first else ()))


def attend_back_kernel(carry, final, part, *refs):
    if part:
        where_ref, *refs = refs
    mixed_ref, do_ref, o_ref, l_ref, low_ref, w_ref, *refs = refs
    if carry:
        grad_in, *refs = refs
    if final:
        x_ref, mid_ref, table_ref, norm_two, *refs = refs
    if part:
        core_ref, core_more, gp_ref, gp_core, *refs = refs
        left_out, left_keep, right_out, right_keep, *refs = refs
    else:
        gq_ref, more_ref, *refs = refs
    if final:
        out_ref, norm_ref, *refs = refs
    else:
        grad_ref, *refs = refs
    sum_k, sum_v, both, every, *sums = refs
    q_ref, k_ref, v_ref = (mixed_ref.at[:, 128 * i : 128 * (i + 1)] for i in range(3))
    dq_ref, dk_ref, dv_ref = (both.at[:, 128 * i : 128 * (i + 1)] for i in range(3))
    seq = mixed_ref.shape[0]
    step = pl.program_id(0)
    low_lanes = lane_low(BLOCK)
    low_all = lane_low(seq)
    allowed = upper()
    scaling = jnp.asarray(HEAD_DIM**-0.5, BF16)
    head_keys = [keep_head(low_all, head, k_ref[...]) for head in range(2)]
    tiles = [(block, head) for block in reversed(range(seq // BLOCK)) for head in range(2)]

    def scored(block, head):
        start, end = block * BLOCK, (block + 1) * BLOCK
        q_head = keep_head(low_lanes, head, q_ref[start:end, :] * scaling)
        g_head = keep_head(low_lanes, head, do_ref[start:end, :])
        return q_head, g_head, dot_nt(k_ref[:end, :], q_head), dot_nt(v_ref[:end, :], g_head)

    ahead = 2
    waiting = [scored(*tile) for tile in tiles[:ahead]]
    for number, (block, head) in enumerate(tiles):
        start, end = block * BLOCK, (block + 1) * BLOCK
        if number + ahead < len(tiles):
            waiting.append(scored(*tiles[number + ahead]))
        q_head, g_head, scores, grad_probs = waiting.pop(0)
        if head == 0:
            dots = (do_ref[start:end, :].astype(F32) * o_ref[start:end, :].astype(F32)).T
        centre = jnp.sum(dots[HEAD_DIM * head : HEAD_DIM * (head + 1)], axis=0, keepdims=True)
        probs = jnp.exp(scores - l_ref[0, head : head + 1, start:end])
        last = jnp.where(allowed, probs[start:, :], 0.0)
        probs = jnp.concatenate([probs[:start, :], last], axis=0) if block else last
        grad_scores = (probs * (grad_probs - centre)).astype(BF16)
        terms = (
            dot_tn(grad_scores, head_keys[head][:end]),
            dot_nn(grad_scores, q_head),
            dot_nn(probs.astype(BF16), g_head),
        )
        if head == 0:
            add_q, add_k, add_v = terms
            continue
        add_q, add_k, add_v = add_q + terms[0], add_k + terms[1], add_v + terms[2]
        dq_ref[start:end, :] = (add_q * HEAD_DIM**-0.5).astype(BF16)
        if end == seq:
            sum_k[...] = add_k
            sum_v[...] = add_v
        else:
            sum_k[:end, :] += add_k
            sum_v[:end, :] += add_v
    dk_ref[...] = sum_k[...].astype(BF16)
    dv_ref[...] = sum_v[...].astype(BF16)

    here = pl.ds(pl.multiple_of(step * 384, 384), 384)
    grad_qkv = dot_tn(low_ref[...], both[...]).astype(BF16)
    every[:, here] = both[...]

    def cut(out, keep, columns, source, size, index):
        for block in range(source.shape[0] // (2 * size)):
            to = pl.ds(block * size, size)
            for ref, side in ((out, 1 - index), (keep, index)):
                start = pl.multiple_of(block * 2 * size + side * size, 16)
                ref[to, columns] = source[pl.ds(start, size), :]

    @pl.when(step < pl.num_programs(0) - 1)
    def _():
        if part:
            sums[0][...] = (grad_qkv.astype(F32) + core_ref[:, here].astype(F32)).astype(BF16)
            cut(left_out, left_keep, here, sums[0], part, where_ref[0])
        else:
            gq_ref[:, here] = grad_qkv

    @pl.when(step == pl.num_programs(0) - 1)
    def _():
        if part:
            sums[1][:, :384] = (
                grad_qkv.astype(F32) + core_more[:, :384].astype(F32)
            ).astype(BF16)
        else:
            more_ref[:, :384] = grad_qkv


    @pl.when(step == pl.num_programs(0) - 1)
    def _():
        if final:
            norm_ref[...] = jnp.zeros_like(norm_ref)
        for start in range(0, seq, BLOCK):
            here = pl.ds(start, BLOCK)
            grad = dot_nt(every[here, :], w_ref[...])
            if carry:
                grad = grad + grad_in[here, :].astype(F32)
            if not final:
                grad_ref[here, :] = grad.astype(BF16)
                continue
            unit, inverse = normalise(x_ref[start // BLOCK, 0].astype(F32))
            norm_ref[0:1] += jnp.sum(grad * unit, axis=0, keepdims=True)
            norm_ref[1:2] += jnp.sum(grad, axis=0, keepdims=True)
            back = norm_back(unit, inverse, table_ref[0:1], grad)
            out_ref[here, :] = (mid_ref[here, :].astype(F32) + back).astype(BF16)
        tail = jnp.zeros((128, low_ref.shape[1]), F32)
        if final:
            tail = jnp.concatenate([norm_ref[:2], norm_two[:2], tail[4:]], axis=0)
        if part:
            sums[1][:, 384:512] = (tail.T + core_more[:, 384:].astype(F32)).astype(BF16)
            sums[1][:, 512:] = (gp_ref[...].astype(F32) + gp_core[...].astype(F32)).astype(BF16)
            cut(right_out, right_keep, slice(None), sums[1], 2 * part, where_ref[1])
        else:
            more_ref[:, 384:] = tail.T.astype(BF16)


def attend_back(
    mixed, grad, attended, logs, low, weight, pairs, carry=None, final=(), where=None, others=(), part=0
):
    seq, dim = low.shape
    group = 3 * 128
    wide = pairs * group

    def column(width):
        return pl.BlockSpec((seq, width), lambda i, *_: (0, i))

    more = [whole(seq, dim)] if carry is not None else []
    more += [part_of(final[0], 0), whole(seq, dim), whole(8, dim), whole(8, dim)] if final else []
    more += [whole(*other.shape) for other in others]
    widths = [wide - group, group + 128]
    outs = [(dim, width) for width in widths]
    scratch = [pltpu.VMEM((seq, 128), F32)] * 2
    scratch += [pltpu.VMEM((seq, group), BF16), pltpu.VMEM((seq, wide), BF16)]
    if part:
        widths[1] += others[2].shape[1]
        outs = [(dim // 2, width) for width in widths for _ in range(2)]
        scratch += [pltpu.VMEM((dim, group), BF16), pltpu.VMEM((dim, widths[1]), BF16)]
    return pl.pallas_call(
        functools.partial(attend_back_kernel, carry is not None, bool(final), part),
        grid_spec=pltpu.PrefetchScalarGridSpec(
            num_scalar_prefetch=1 if part else 0,
            grid=(pairs,),
            in_specs=[column(group), column(128), column(128)]
            + [pl.BlockSpec((1, 2, seq), lambda i, *_: (i, 0, 0)), whole(seq, dim)]
            + [whole(dim, wide)]
            + more,
            out_specs=[whole(*shape) for shape in outs]
            + [whole(seq, dim)]
            + ([whole(8, dim)] if final else []),
            scratch_shapes=scratch,
        ),
        out_shape=[shaped(shape, BF16) for shape in outs]
        + [shaped((seq, dim), BF16)]
        + ([shaped((8, dim), F32)] if final else []),
        compiler_params=params(58),
        cost_estimate=cost(0.01),
    )(
        *((where,) if part else ()),
        mixed,
        grad,
        attended,
        logs,
        low,
        weight,
        *(() if carry is None else (carry,)),
        *final,
        *others,
    )


def ffn_kernel(final, paired, *refs):
    low_ref, cot_ref, up_ref, down_ref, out_in = refs[:5]
    back_in = refs[5] if final else None
    out_ref, back_ref, gu_ref, gd_ref, out_sum, back_sum, act, hid = refs[5 + final :]

    def chunk(first):
        up, down = up_ref[...], down_ref[...]
        for start in range(0, low_ref.shape[0], BLOCK):
            here = pl.ds(start, BLOCK)
            hidden = dot_nn(low_ref[here, :], up)
            grad_active = dot_nt(cot_ref[start // BLOCK, 0], down)
            square = hidden * hidden
            bend = jnp.tanh(hidden * (GELU_A + (GELU_A * GELU_B) * square))
            gate = 0.5 + 0.5 * bend
            active = (hidden * gate).astype(BF16)
            slope = gate + hidden * (0.5 - 0.5 * bend * bend) * (
                GELU_A + (3 * GELU_A * GELU_B) * square
            )
            grad_hidden = (grad_active * slope).astype(BF16)
            act[here, :] = active
            hid[here, :] = grad_hidden
            add_out, add_back = dot_nn(active, down), dot_nt(grad_hidden, up)
            if first:
                out_sum[here, :] = add_out
                back_sum[here, :] = add_back
            else:
                total = out_sum[here, :] + add_out + out_in[here, :].astype(F32)
                out_ref[here, :] = total.astype(out_ref.dtype)
                total = back_sum[here, :] + add_back
                if final:
                    total = total + back_in[here, :].astype(F32)
                back_ref[here, :] = total.astype(BF16)
        gu_ref[...] = dot_tn(low_ref[...], hid[...]).astype(BF16)
        cot = cot_ref[...].reshape(act.shape[0], -1)
        grad_down = dot_tn(act[...], cot).astype(BF16)
        if paired:
            dim = grad_down.shape[1]
            grad_down = grad_down.reshape(-1, 2 * paired, dim)
            for side in range(2):
                gd_ref[:, side * dim : (side + 1) * dim] = grad_down[
                    :, side * paired : (side + 1) * paired
                ].reshape(-1, dim)
        else:
            gd_ref[...] = grad_down

    for place in range(2):

        @pl.when(pl.program_id(0) == place)
        def _(place=place):
            chunk(place == 0)


def feed_forward(low, pair, up, down, out_in, part, back_in=None):
    tok, dim = low.shape
    final = back_in is not None
    wide = down.shape[0]
    chunk = wide // 2
    paired = part if part % 16 == 0 else 0
    tall, long = (chunk // 2, 2 * dim) if paired else (chunk, dim)
    outs = pl.pallas_call(
        functools.partial(ffn_kernel, int(final), paired),
        grid=(2,),
        in_specs=[whole(tok, dim), part_of(pair, 1), columns(dim, chunk), rows(chunk, dim)]
        + [whole(tok, dim)] * (2 if final else 1),
        out_specs=[whole(tok, dim), whole(tok, dim), columns(dim, chunk), rows(tall, long)],
        out_shape=[shaped((tok, dim), BF16 if final else F32), shaped((tok, dim), BF16)]
        + [shaped((dim, wide), BF16), shaped((2 * tall, long), BF16)],
        scratch_shapes=[pltpu.VMEM((tok, dim), F32)] * 2 + [pltpu.VMEM((tok, chunk), BF16)] * 2,
        compiler_params=params(58),
        cost_estimate=cost(0.01),
    )(low, pair, up, down, out_in, *((back_in,) if final else ()))
    if paired:
        return outs
    grad_down = outs[3].reshape(-1, 2, part, dim).transpose(0, 2, 1, 3).reshape(-1, 2 * dim)
    return list(outs[:3]) + [grad_down]


def spread_kernel(widths, where_ref, *refs):
    del where_ref
    count = len(refs) // (2 * len(widths) + 1)
    ins, outs = refs[: 2 * len(widths) * count], refs[2 * len(widths) * count :]
    position = 0
    for out in outs:
        start = 0
        for width in widths:
            total = ins[position][0].astype(F32) + ins[position + 1][0].astype(F32)
            out[:, start : start + width] = total.astype(BF16)
            start += width
            position += 2


def spread(where, *items):
    z_count, part = items[0][0].shape[:2]
    widths = [item[0].shape[-1] for item in items]
    arrays, in_specs = [], []
    for step in range(z_count):
        for item in items:
            spec = pl.BlockSpec(
                (1, part, item[0].shape[-1]),
                lambda i, where_ref, step=step: ((where_ref[0] + step) % z_count, 0, 0),
            )
            arrays += item
            in_specs += [spec, spec]
    return pl.pallas_call(
        functools.partial(spread_kernel, widths),
        grid_spec=pltpu.PrefetchScalarGridSpec(
            num_scalar_prefetch=1,
            grid=(1,),
            in_specs=in_specs,
            out_specs=[pl.BlockSpec((part, sum(widths)), lambda i, _: (0, 0))] * z_count,
        ),
        out_shape=[shaped((part, sum(widths)), BF16)] * z_count,
        compiler_params=params(58),
        cost_estimate=cost(0.01),
    )(where, *arrays)


def by_place(where_ref, refs):
    x, c = where_ref[0], where_ref[1]
    own, other_x, other_c, other_both = (ref[...] for ref in refs)
    low_x = [jnp.where(x == 0, own, other_x), jnp.where(x == 0, other_c, other_both)]
    high_x = [jnp.where(x == 0, other_x, own), jnp.where(x == 0, other_both, other_c)]
    return [
        [jnp.where(c == 0, side[0], side[1]) for side in (low_x, high_x)],
        [jnp.where(c == 0, side[1], side[0]) for side in (low_x, high_x)],
    ]


def finish_ffn(fan, where_ref, all_ref, up_ref, down_ref):
    part, dim = all_ref.shape[2], down_ref.shape[1]
    count = up_ref.shape[1] // fan // 2
    for core in range(2):
        for side in range(2):
            here = slice(side * part, (side + 1) * part)
            for block in range(count):
                place = (2 * block + core) * fan
                up_ref[here, place : place + fan] = all_ref[
                    core, side, :, block * fan : (block + 1) * fan
                ].astype(F32)
            start = count * fan
            for half in range(2):
                place = core * fan + side * fan // 2 + half * part
                down_ref[place : place + part, :] = all_ref[
                    core, side, :, start + half * dim : start + (half + 1) * dim
                ].astype(F32)


def finish_qkv(pairs, where_ref, *refs):
    pieces, (qkv_ref, proj_ref, *norm_refs) = by_place(where_ref, refs[:4]), refs[4:]
    part, dim = refs[0].shape[0], qkv_ref.shape[1] // 3
    sums = []
    for side in range(2):
        here = slice(side * part, (side + 1) * part)
        for core in range(2):
            piece = pieces[core][side]
            for pair in range(pairs):
                for which in range(3):
                    place = which * dim + core * dim // 2 + pair * 128
                    start = (pair * 3 + which) * 128
                    qkv_ref[here, place : place + 128] = piece[:, start : start + 128].astype(F32)
            start = pairs * 384 + 128
            proj_ref[here, core * dim // 2 : (core + 1) * dim // 2] = piece[:, start:].astype(F32)
        norms = slice(pairs * 384, pairs * 384 + 128)
        sums.append(
            pieces[0][side][:, norms].astype(F32) + pieces[1][side][:, norms].astype(F32)
        )
    sums = jnp.concatenate(sums, axis=0).T
    for place, norm_ref in enumerate(norm_refs):
        norm_ref[...] = sums[place : place + 1].reshape(norm_ref.shape)


def settle_kernel(in_ref, out_ref):
    out_ref[...] = in_ref[...]


def settle(value):
    spec = pl.BlockSpec((1,) + value.shape[1:], lambda i: (i, 0, 0))
    return pl.pallas_call(
        settle_kernel,
        grid=value.shape[:1],
        in_specs=[spec],
        out_specs=spec,
        out_shape=shaped(value.shape, value.dtype),
        cost_estimate=cost(0.01),
    )(value)


def finish(kernel, where, pieces, *shapes):
    return pl.pallas_call(
        kernel,
        grid_spec=pltpu.PrefetchScalarGridSpec(
            num_scalar_prefetch=1,
            grid=(1,),
            in_specs=[whole(*piece.shape) for piece in pieces],
            out_specs=[whole(*shape) for shape in shapes],
        ),
        out_shape=[shaped(shape, F32) for shape in shapes],
        compiler_params=params(58),
        cost_estimate=cost(0.01),
    )(where, *pieces)


class Grid:
    def __init__(self):
        self.z_count = lax.axis_size("dp") // 2
        self.dp, self.head = lax.axis_index("dp"), lax.axis_index("head")
        self.z, self.y, self.x, self.c = self.dp // 2, self.dp % 2, self.head // 2, self.head % 2
        assert lax.axis_size("head") == 4 and lax.axis_size("dp") % 2 == 0

    def send(self, value, z=0, y=0, x=0, c=0):
        pairs = []
        for source in range(self.z_count * 8):
            zi, yi, xi, ci = source // 8, source // 4 % 2, source // 2 % 2, source % 2
            zt, yt, xt, ct = (zi + z) % self.z_count, yi ^ y, xi ^ x, ci ^ c
            pairs.append((source, ((zt * 2 + yt) * 2 + xt) * 2 + ct))
        return lax.ppermute(value, BOTH, pairs)

    def pick(self, value, axis, index):
        return lax.dynamic_index_in_dim(value, index, axis, keepdims=False)

    def join(self, mine, other, index, axis):
        shape = mine.shape[:axis] + (2,) + mine.shape[axis:]
        here = lax.broadcasted_iota(jnp.int32, shape, axis) == index
        mine, other = (jnp.broadcast_to(jnp.expand_dims(v, axis), shape) for v in (mine, other))
        return jnp.where(here, mine, other)

    def to_z(self, piece):
        return [piece] + [self.send(piece, z=step) for step in range(1, self.z_count)]

    def by_z(self, got):
        shape = (self.z_count,) + got[0].shape
        steps = (self.z - lax.broadcasted_iota(jnp.int32, shape, 0)) % self.z_count
        out = jnp.broadcast_to(got[0], shape)
        for step in range(1, self.z_count):
            out = jnp.where(steps == step, jnp.broadcast_to(got[step], shape), out)
        return out

    def over_z(self, piece):
        copies = jnp.broadcast_to(piece, (self.z_count,) + piece.shape)
        groups = [list(range(y, self.z_count * 2, 2)) for y in range(2)]
        return lax.all_to_all(
            copies, "dp", split_axis=0, concat_axis=0, tiled=True, axis_index_groups=groups
        )

    def over_y(self, value, got):
        return self.join(value, got, self.y, 1)

    def over_x(self, value, got, axis):
        return self.join(value, got, self.x, axis)

    def halves(self, name, values):
        axis, index = (1, self.y) if name == "y" else (values[0].ndim - 3, self.x)
        low, high = (
            sum(lax.index_in_dim(v, place, axis, False).astype(F32) for v in values).astype(BF16)
            for place in range(2)
        )
        return jnp.where(index == 0, high, low), jnp.where(index == 0, low, high)

    def by_block(self, *values):
        totals = [keep.astype(F32) + got.astype(F32) for keep, got in values]
        return [
            jnp.concatenate(
                [self.pick(total, 0, (self.z + step) % self.z_count) for total in totals], axis=-1
            ).astype(BF16)
            for step in range(self.z_count)
        ]

    def end(self, parts):
        return self.total(
            [parts[0]] + [self.send(part, z=step) for step, part in enumerate(parts) if step]
        )

    def total(self, parts):
        return sum(value.astype(F32) for value in parts).astype(BF16)

    def share(self, piece):
        return [piece, self.send(piece, x=1), self.send(piece, c=1), self.send(piece, x=1, c=1)]

    def share_all(self, piece):
        both = self.join(piece, self.send(piece, x=1), self.x, 0)
        return self.join(both, self.send(both, c=1), self.c, 0)


def exchange(value):
    return lax.all_to_all(value, "head", split_axis=0, concat_axis=0, tiled=True)


def after(value, *done):
    return lax.optimization_barrier((value, done))[0]


def flat(value):
    return value.reshape(-1, value.shape[-1])


def local(
    tokens,
    qkv_weight,
    proj_weight,
    up_weight,
    down_weight,
    attn_gain,
    attn_bias,
    ffn_gain,
    ffn_bias,
    cotangent,
):
    grid = Grid()
    dim = tokens.shape[-1]
    share = qkv_weight.shape[0]
    part = share // 2
    half = dim // 2
    pairs = half // 128
    hidden = up_weight.shape[1]
    dp_count = lax.axis_size("dp")
    fan = hidden // dp_count // 2
    core = grid.c.reshape(1).astype(jnp.int32)
    assert tokens.shape[0] == 4 and tokens.shape[1] * 4 == SEQ
    assert fan == 4 * part

    def row_half(value):
        return lax.dynamic_slice_in_dim(value, grid.x * part, part, 0)

    qkv = grid.pick(qkv_weight.reshape(share, 3, 2, pairs, 128), 2, grid.c)
    qkv = qkv.transpose(0, 2, 1, 3).reshape(share, -1)
    table = jnp.stack([attn_gain, attn_bias, ffn_gain, ffn_bias], axis=1)
    table = jnp.pad(table, ((0, 0), (0, 124)))
    piece = jnp.concatenate([qkv, table], axis=1).astype(BF16)
    up = grid.pick(row_half(up_weight).reshape(part, dp_count, 2, fan), 2, grid.c)
    proj = grid.pick(row_half(proj_weight).reshape(part, 2, half), 1, grid.c)
    up_piece = jnp.concatenate([up.reshape(part, -1), proj], axis=1).astype(BF16)
    down_piece = grid.pick(down_weight.reshape(2, fan, dim), 0, grid.c).astype(BF16)
    where = jnp.stack([grid.x, grid.y]).astype(jnp.int32)
    where_head = jnp.stack([grid.x, grid.c]).astype(jnp.int32)

    both = exchange(after(jnp.stack([tokens, cotangent], axis=1), piece))
    first_z = grid.by_z(after(grid.to_z(piece), up_piece, down_piece))
    up_got = grid.to_z(after(up_piece, first_z))
    w_mine = flat(grid.over_y(first_z, after(grid.send(first_z, y=1), up_got)))
    w_theirs = grid.send(w_mine, c=1)
    up_z = grid.by_z(after(up_got, w_mine))
    up_y = grid.send(up_z, y=1)
    up_x = grid.send(up_z, x=1)
    down_both = grid.join(
        down_piece, grid.send(after(down_piece, up_got), y=1), grid.y, 0
    )
    down_mine = grid.over_z(after(down_both, both))
    low, mixed_mine, att_mine, log_mine, table = attend(
        after(both, up_z), w_mine, pairs, True
    )
    mixed_theirs, att_theirs, log_theirs = attend(low, w_theirs, pairs, False)
    up_y, up_x = after((up_y, up_x), att_mine, att_theirs)
    up_xy = grid.send(up_y, x=1)
    up_y = grid.over_y(up_z, up_y)
    up_x = grid.over_y(up_x, up_xy)
    up_mine = flat(grid.over_x(up_y, up_x, 2))
    up_theirs = grid.send(up_mine, c=1)
    down_mine = flat(after(down_mine, up_xy))
    down_theirs = grid.send(down_mine, c=1)
    middle, low_two = project(core, both, att_mine, att_theirs, up_mine, up_theirs, table)
    out, back, gu_theirs, gd_theirs = feed_forward(
        low_two, both, up_theirs, after(down_theirs, low_two), middle, part
    )
    gd_core, gu_core = grid.send(gd_theirs, c=1), grid.send(gu_theirs, c=1)
    out, back, gu_mine, gd_mine = feed_forward(low_two, both, up_mine, down_mine, out, part, back)
    gd_core, gu_core = after((gd_core, gu_core), back)

    def blocks(value):
        return value.reshape(grid.z_count, 2, 2, -1, value.shape[-1])

    gd_out, gd_keep = grid.halves("y", [blocks(gd_mine), blocks(gd_core)])
    gd_got = grid.send(gd_out, y=1)
    gu_out, gu_keep = grid.halves("x", [blocks(gu_mine), blocks(after(gu_core, gd_out))])
    gu_got = grid.send(gu_out, x=1)
    grad_middle, ga_mine, ga_theirs, gp_mine, gp_theirs, norm_two = middle_back(
        core, middle, after(back, gd_out, gu_out), both, table, up_mine, up_theirs, att_mine,
        att_theirs,
    )
    gp_core = grid.send(gp_theirs, c=1)
    gq_theirs, gq_rest, grad_low = attend_back(
        mixed_theirs, ga_theirs, att_theirs, log_theirs, low, w_theirs, pairs
    )
    gq_core = [grid.send(value, c=1) for value in (gq_theirs, gq_rest)]
    gd_got, gu_got, gp_core = after((gd_got, gu_got, gp_core), grad_low)
    gd_out, gd_keep = grid.halves("x", [gd_keep, gd_got])
    gd_got = grid.send(gd_out, x=1)
    gu_out, gu_keep = grid.halves("y", [gu_keep, gu_got])
    gu_got = grid.send(gu_out, y=1)
    out_home = exchange(after(out.reshape(4, SEQ // 4, dim), gd_out, gu_out))
    mine = (mixed_mine, after(ga_mine, gd_out, gu_out), att_mine, log_mine, low, w_mine, pairs)
    final = (both, grad_middle, table, norm_two)
    if part % 16 == 0:
        *cuts, grad_x, _ = attend_back(
            *mine, grad_low, final, where, (*gq_core, gp_mine, gp_core), part
        )
        left_out, left_keep, right_out, right_keep = cuts
    else:
        gq_mine, gq_more, grad_x, _ = attend_back(*mine, grad_low, final)
        left_out, left_keep = grid.halves("x", [blocks(gq_mine), blocks(gq_core[0])])
        right_out, right_keep = grid.halves(
            "y",
            [
                jnp.concatenate([blocks(gq_more), blocks(gp_mine)], axis=-1),
                jnp.concatenate([blocks(gq_core[1]), blocks(gp_core)], axis=-1),
            ],
        )
    left_got, right_got = grid.send(left_out, x=1), grid.send(right_out, y=1)
    left_keep, left_got, right_keep, right_got = (
        value.reshape(grid.z_count, 2, part, -1)
        for value in (left_keep, left_got, right_keep, right_got)
    )
    gd_got, gu_got, out_home = after((gd_got, gu_got, out_home), left_out, right_out)
    out_home = settle(out_home)
    ffn_parts = grid.by_block((gu_keep, gu_got), (gd_keep, gd_got))
    left_got, right_got = after((left_got, right_got), ffn_parts, out_home)
    ffn_got = [grid.send(part, z=step) for step, part in enumerate(ffn_parts) if step]
    left_out, left_keep = grid.halves("y", [left_keep, left_got])
    left_got = grid.send(left_out, y=1)
    right_out, right_keep = grid.halves("x", [right_keep, right_got])
    right_got = grid.send(right_out, x=1)
    grad_home = exchange(after(grad_x.reshape(4, SEQ // 4, dim), left_got))
    left_got, right_got = after((left_got, right_got), ffn_got)
    qkv_parts = spread(
        grid.z.reshape(1).astype(jnp.int32), (left_keep, left_got), (right_keep, right_got)
    )
    sum_ffn = after(grid.total([ffn_parts[0], *ffn_got]), qkv_parts)
    ffn_x = grid.send(sum_ffn, x=1)
    qkv_got = [grid.send(part, z=step) for step, part in enumerate(qkv_parts) if step]
    qkv_got, grad_home = after((qkv_got, grad_home), grad_home)
    ffn_x = grid.join(sum_ffn, ffn_x, grid.x, 0)
    all_ffn = grid.join(ffn_x, grid.send(ffn_x, c=1), grid.c, 0)
    shard_up, shard_down = finish(
        functools.partial(finish_ffn, fan), where_head, [all_ffn], (share, hidden), (2 * fan, dim)
    )
    sum_qkv = grid.total([qkv_parts[0], *after(qkv_got, shard_up)])
    shares = grid.share(sum_qkv)
    grad_home = after(grad_home, sum_qkv).astype(F32)
    shard_qkv, shard_proj, *norms = finish(
        functools.partial(finish_qkv, pairs), where_head, after(shares, shard_up),
        (share, 3 * dim), (share, dim), *[(share,)] * 4,
    )
    return (
        out_home,
        grad_home,
        shard_qkv,
        shard_proj,
        shard_up,
        shard_down,
        norms[0],
        norms[1],
        norms[2],
        norms[3],
    )


def solution(mesh):
    spread = P("dp", "head", None)
    placed = (spread,) + (P("dp", None),) * 4 + (P("dp"),) * 4 + (spread,)
    return jax.shard_map(
        local,
        mesh=mesh,
        in_specs=placed,
        out_specs=(spread, spread) + (P("dp", None),) * 4 + (P("dp"),) * 4,
        check_vma=False,
    )
```
